128 devices in a mesh: dp: 8 (over z, core), table: 16 (over x, y).
Axes of the slice: x: 4, y: 4, z: 4, core: 2. Of those that a mesh axis runs over, the one named last changes fastest.
Arguments:
- table: bfloat16 [524288, 512], P(('dp', 'table')), may hold values from -10.2 to 10.2
- last_update: int32 [524288], P(('dp', 'table')), may hold values from 0 to 63
- item_owner: int32 [65536, 1], P(('dp', 'table')), may hold values from 0 to 127; in each aligned block of 512 rows (0 to 511, 512 to 1023, ...) at most 8 rows name the same one
- item_slot: int32 [65536], P(('dp', 'table')), may hold values from 0 to 4095
- neg_owner: int32 [16384, 1], P(('dp', 'table')), may hold values from 0 to 127; in each aligned block of 128 rows (0 to 127, 128 to 255, ...) at most 2 rows name the same one
- neg_slot: int32 [16384], P(('dp', 'table')), may hold values from 0 to 4095
- seq_lengths: int32 [128, 4], P(('dp', 'table')), may hold values from 1 to 256, 512 in all within a row
- w_in: bfloat16 [512, 2048], replicated, may hold values from -0.25 to 0.25
- w_out: bfloat16 [512, 512], replicated, may hold values from -0.25 to 0.25
Outputs:
- token_loss: float32 [65536], P(('dp', 'table'))
- table_grad: float32 [524288, 512], P(('dp', 'table'))
- grad_in: float32 [512, 2048], replicated
- grad_out: float32 [512, 512], replicated
The draws below stay inside these ranges and needn't reach their ends.
Inputs may be any that keep to these rules, and one draw needn't show every extreme that they name: `item_owner`: in each aligned block of 512 rows no owner is named more than 8 times; some owner is named exactly that often. `neg_owner`: in each aligned block of 128 rows no owner is named more than 2 times; some owner is named exactly that often.
All inputs are finite; a program needn't handle non-finite values.
Results may differ from the reference program's by a relative error of at most 0.02.
Values may be sent and summed in bfloat16 or wider, within the bound.
A program may use at most 128 MiB of HBM per device.

```python
import math
from functools import partial
import jax
import jax.numpy as jnp
import numpy as np
from jax import lax

D = 512
H = 4
DH = 128
TOK_DEV = 512
SEQ_DEV = 4
LMAX = 256
NNEG = 128
ROWS_DEV = 4096
NOW = 64
CAP_TOK = 8
CAP_NEG = 2
ROWS = 524288
TOKENS = 65536
NEGS = 16384
N_DP = 8
N_TABLE = 16
DEVICES = 128


def draw_table(key, part):
    key = jax.random.fold_in(key, 7)
    first = jax.random.fold_in(key, 0)
    return jnp.clip(jax.random.normal(first, (ROWS, D), jnp.float32), -4.0, 4.0).astype(jnp.bfloat16)


def plant(entries, stream_key, least, high):
    longest = entries.shape.index(max(entries.shape))
    spots = []
    for shift in (0, 1):
        where = [jax.random.randint(jax.random.fold_in(stream_key, axis), (), 0, length) for axis, length in enumerate(entries.shape)]
        where[longest] = (where[longest] + shift) % entries.shape[longest]
        spots.append(tuple(where))
    return entries.at[spots[0]].set(least).at[spots[1]].set(high)


def length_profile(amount, total, reach, slope):
    weights = [(1 << 20) // math.isqrt(grade ** slope) + 1 for grade in range(2, amount + 1)]
    spare, counts = total - reach - (amount - 1), [1] * (amount - 1)
    while spare > 0:
        movable = [i for i in range(amount - 1) if counts[i] < reach]
        mass, left = sum([weights[i] for i in movable]), spare
        for i in movable:
            more = min(reach - counts[i], max(1, left * weights[i] // mass), spare)
            counts[i] = counts[i] + more
            spare = spare - more
    return np.array([reach] + counts)


def uneven_parts(rng, count, total, bound, slope):
    if count == 2:
        one = jax.random.randint(rng, (), max(1, total - bound), min(bound, total - 1) + 1)
        return jnp.stack([one, total - one])
    sizes = jnp.asarray(length_profile(count, total, bound, slope), jnp.int32)
    twos = (count - 1) // 2
    source_of, receiver = sizes[1:1 + 2 * twos:2], sizes[2:2 + 2 * twos:2]
    margin = jnp.minimum(source_of - 1, bound - receiver)
    moved = jax.random.randint(jax.random.fold_in(rng, 1), (twos,), 0, 1 << 20) % (margin + 1)
    sizes = sizes.at[1:1 + 2 * twos:2].set(source_of - moved).at[2:2 + 2 * twos:2].set(receiver + moved)
    return sizes[jax.random.permutation(jax.random.fold_in(rng, 2), count)]


def deal_out(rng, own, number, rows, number_of, top, bound, lean):
    order = jax.random.permutation(rng, number_of)
    heavy_load, ordinary = portions_of(number_of, rows * top, bound, lean, True), portions_of(number_of, rows * top, bound, lean, False)
    places = jnp.arange(number_of)

    def named(sizes, rotation):
        used = int((sizes > 0).sum())
        fixed = max(1, used // 4)
        shifted = fixed + (places - fixed + rotation * (used - fixed)) % max(1, number_of - fixed)
        return jnp.zeros((number_of,), jnp.int32).at[order[jnp.where(places < fixed, places, shifted)]].set(jnp.asarray(sizes, jnp.int32))

    sizes = jnp.where(number % 4 == 0, named(heavy_load, number // 4), named(ordinary, number - number // 4 - 1))
    mixed = jax.random.permutation(jax.random.fold_in(own, 3), number_of)
    donor, taker = mixed[0:number_of // 2 * 2:2], mixed[1:number_of // 2 * 2:2]
    margin = jnp.minimum(sizes[donor] - 1, bound - sizes[taker]) // 2
    margin = jnp.where((donor == order[0]) | (taker == order[0]) | (sizes[taker] == 0), 0, jnp.maximum(margin, 0))
    shifted = jax.random.randint(jax.random.fold_in(own, 4), (number_of // 2,), 0, 1 << 20) % (margin + 1)
    sizes = sizes.at[donor].add(-shifted).at[taker].add(shifted)
    labels = jnp.searchsorted(jnp.cumsum(sizes), jnp.arange(rows * top), side="right").astype(jnp.int32)
    listing = labels.reshape(top, rows).T
    listing = listing[jax.random.permutation(jax.random.fold_in(own, 1), rows)]
    rotation = jax.random.randint(jax.random.fold_in(own, 2), (rows, 1), 0, top)
    return jnp.take_along_axis(listing, (jnp.arange(top)[None, :] + rotation) % top, axis=1)


def portions_of(number_of, total, most, slope, full):
    weights = [(1 << 20) // math.isqrt(standing ** slope) + 1 for standing in range(1, number_of + 1)]
    largest = most if full else min(most, max(-(-total // number_of), total * weights[0] // sum(weights)))
    least = 1 if total - largest >= number_of - 1 else 0
    holding, rest = [largest] + [least] * (number_of - 1), total - largest - least * (number_of - 1)
    while rest > 0:
        free = [i for i in range(1, number_of) if holding[i] < largest] or [i for i in range(1, number_of) if holding[i] < most]
        mass, remaining = sum([weights[i] for i in free]), rest
        for i in free:
            more = min(most - holding[i], max(1, remaining * weights[i] // mass), rest)
            holding[i] = holding[i] + more
            rest = rest - more
    return np.array(holding)


def centred(rng, extent, spread, most, kind=jnp.bfloat16):
    values = spread * jax.random.normal(rng, extent, jnp.float32)
    return jnp.clip(values, min=-most, max=most).astype(kind)


def setup_inputs(seed: int = 0) -> dict:
    arg_keys = jax.random.split(jax.random.key(seed), 10)
    table = draw_table(jax.random.fold_in(arg_keys[9], 71), 0)
    last_update = plant(jax.random.randint(arg_keys[1], (ROWS,), 0, NOW), jax.random.fold_in(arg_keys[1], 1), 0, NOW - 1).astype(jnp.int32)
    item_owner_keys = jax.random.split(jax.random.fold_in(arg_keys[2], 1), TOKENS // TOK_DEV)
    item_owner_turns = jax.random.permutation(jax.random.fold_in(arg_keys[2], 3), TOKENS // TOK_DEV)
    item_owner = jax.vmap(lambda own, number: deal_out(jax.random.fold_in(arg_keys[2], 2), own, number, TOK_DEV, DEVICES, 1, CAP_TOK, 2))(item_owner_keys, item_owner_turns).reshape((TOKENS, 1))
    item_slot = plant(jax.random.randint(arg_keys[3], (TOKENS,), 0, ROWS_DEV), jax.random.fold_in(arg_keys[3], 1), 0, ROWS_DEV - 1).astype(jnp.int32)
    neg_owner_keys = jax.random.split(jax.random.fold_in(arg_keys[4], 1), NEGS // NNEG)
    neg_owner_turns = jax.random.permutation(jax.random.fold_in(arg_keys[4], 3), NEGS // NNEG)
    neg_owner = jax.vmap(lambda own, number: deal_out(jax.random.fold_in(arg_keys[4], 2), own, number, NNEG, DEVICES, 1, CAP_NEG, 1))(neg_owner_keys, neg_owner_turns).reshape((NEGS, 1))
    neg_slot = plant(jax.random.randint(arg_keys[5], (NEGS,), 0, ROWS_DEV), jax.random.fold_in(arg_keys[5], 1), 0, ROWS_DEV - 1).astype(jnp.int32)
    seq_lengths = jax.vmap(lambda own: uneven_parts(own, SEQ_DEV, TOK_DEV, LMAX, 2))(jax.random.split(arg_keys[6], DEVICES)).reshape((DEVICES, SEQ_DEV)).astype(jnp.int32)
    w_in = centred(arg_keys[7], (D, 4 * D), D ** -0.5, 0.25)
    w_out = centred(arg_keys[8], (D, D), D ** -0.5, 0.25)
    return {"table": table, "last_update": last_update, "item_owner": item_owner, "item_slot": item_slot, "neg_owner": neg_owner, "neg_slot": neg_slot, "seq_lengths": seq_lengths, "w_in": w_in, "w_out": w_out}


RHO = 0.97
TAU = 0.125
EPS = 1e-05

def normalize(values):
    center = values - lax.optimization_barrier(jnp.mean(values, -1, keepdims=True))
    return center * lax.rsqrt(lax.optimization_barrier(jnp.mean(center * center, -1, keepdims=True)) + EPS)

def layer_loss(rows32, w_in32, w_out32, lengths):
    width = rows32.shape[1]
    x32 = rows32[:TOK_DEV]
    negatives = rows32[TOK_DEV:].astype(jnp.bfloat16)
    ends = jnp.cumsum(lengths)
    where = jnp.arange(TOK_DEV, dtype=jnp.int32)
    segment = lax.optimization_barrier(jnp.sum((where[:, None] >= ends[None, :]).astype(jnp.int32), 1))
    normed = normalize(x32).astype(jnp.bfloat16)
    mixed = jax.nn.silu(jnp.dot(normed, w_in32.astype(jnp.bfloat16), preferred_element_type=jnp.float32)).astype(jnp.bfloat16)
    gate_part, value, query, key_part = jnp.split(mixed, 4, axis=1)
    query = query.reshape(TOK_DEV, H, DH)
    key_part = key_part.reshape(TOK_DEV, H, DH)
    value = value.reshape(TOK_DEV, H, DH)
    scores = jnp.einsum('qhd,khd->hqk', query, key_part, preferred_element_type=jnp.float32)
    visible = (segment[:, None] == segment[None, :]) & (where[None, :] <= where[:, None])
    weights = (jax.nn.silu(scores) * (1.0 / LMAX) * visible[None].astype(jnp.float32)).astype(jnp.bfloat16)
    attended = jnp.einsum('hqk,khd->qhd', weights, value, preferred_element_type=jnp.float32).reshape(TOK_DEV, width)
    gated = (normalize(attended) * gate_part.astype(jnp.float32)).astype(jnp.bfloat16)
    out = (x32 + jnp.dot(gated, w_out32.astype(jnp.bfloat16), preferred_element_type=jnp.float32)).astype(jnp.bfloat16)
    following = jnp.concatenate([x32[1:], jnp.zeros((1, width), jnp.float32)], 0)
    valid = jnp.concatenate([segment[1:] == segment[:-1], jnp.zeros((1,), bool)]).astype(jnp.float32)
    positive = lax.optimization_barrier(jnp.sum(out.astype(jnp.float32) * following, 1)) * TAU
    negative = jnp.dot(out, negatives.T, preferred_element_type=jnp.float32) * TAU
    top = lax.stop_gradient(jnp.maximum(positive, lax.optimization_barrier(jnp.max(negative, 1))))
    total = jnp.exp(positive - top) + lax.optimization_barrier(jnp.sum(jnp.exp(negative - top[:, None]), 1))
    losses = (jnp.log(total) + top - positive) * valid
    return (jnp.sum(losses), losses)

def reference(table, last_update, item_owner, item_slot, neg_owner, neg_slot, seq_lengths, w_in, w_out):
    devices = N_DP * N_TABLE
    rows_dev = table.shape[0] // devices
    width = table.shape[1]
    fade = jnp.power(jnp.float32(RHO), (NOW - last_update).astype(jnp.float32))
    tok_ids = (item_owner[:, 0] * rows_dev + item_slot).astype(jnp.int32).reshape(devices, TOK_DEV)
    neg_ids = (neg_owner[:, 0] * rows_dev + neg_slot).astype(jnp.int32).reshape(devices, NNEG)
    all_ids = jnp.concatenate([tok_ids, neg_ids], 1)
    w_in32 = w_in.astype(jnp.float32)
    w_out32 = w_out.astype(jnp.float32)

    def step(carry, inputs):
        index, lengths = inputs
        scale = fade[index][:, None]
        rows = (table[index].astype(jnp.float32) * scale).astype(jnp.bfloat16)
        rows32 = lax.optimization_barrier(rows).astype(jnp.float32)
        fn = partial(lambda r, a, b, s: layer_loss(r, a, b, s), s=lengths)
        total, pull, losses = jax.vjp(fn, rows32, w_in32, w_out32, has_aux=True)
        grad_rows, grad_a, grad_b = pull(jnp.float32(1.0))
        return ((carry[0] + grad_a, carry[1] + grad_b), (losses, grad_rows * scale))
    start = (jnp.zeros(w_in.shape, jnp.float32), jnp.zeros(w_out.shape, jnp.float32))
    (grad_in, grad_out), (losses, grads) = lax.scan(step, start, (all_ids, seq_lengths))
    table_grad = jnp.zeros((table.shape[0], width), jnp.float32).at[all_ids.reshape(-1)].add(grads.reshape(-1, width))
    return (losses.reshape(-1), table_grad, grad_in, grad_out)
```

```python
import functools

import jax
import jax.numpy as jnp
from jax import lax
from jax.experimental import pallas as pl
from jax.experimental.pallas import tpu as pltpu
from jax.sharding import PartitionSpec as P

D = 512
H = 4
DH = 128
TOK = 512
NEG = 128
ALL = TOK + NEG
DEV = 128
CAP = 10
MSG = 48
LMAX = 256
NOW = 64
ROWS = 4096
WIDE = 5 * D
LOG_RHO = -0.030459207484708574
TAU = 0.125
EPS = 1e-05
MESH = pl.DeviceIdType.MESH
VMEM = pl.BlockSpec(memory_space=pltpu.VMEM)
ANY = pl.BlockSpec(memory_space=pl.ANY)
F32 = jnp.float32
BF16 = jnp.bfloat16
PARTS = ((0, 896), (896, 896), (1792, 768))


def nt(a, b):
    return lax.dot_general(a, b, (((1,), (1,)), ((), ())), preferred_element_type=F32)


def nn(a, b):
    return jnp.dot(a, b, preferred_element_type=F32)


def tn(a, b):
    return lax.dot_general(a, b, (((0,), (0,)), ((), ())), preferred_element_type=F32)


def iota(shape, dim):
    return lax.broadcasted_iota(jnp.int32, shape, dim)


class Place:
    def __init__(self):
        self.dp = lax.axis_index("dp")
        self.tb = lax.axis_index("table")
        self.me = self.dp * 16 + self.tb
        self.z = self.dp // 2
        self.core = lax.rem(self.dp, 2)
        self.x = self.tb // 4
        self.y = lax.rem(self.tb, 4)

    def along(self, axis, shift):
        z, x, y = self.z, self.x, self.y
        if axis == "z":
            z = lax.rem(z + shift, 4)
        if axis == "x":
            x = lax.rem(x + shift, 4)
        if axis == "y":
            y = lax.rem(y + shift, 4)
        return (z * 2 + self.core, x * 4 + y)

    def sibling(self):
        return (self.z * 2 + 1 - self.core, self.tb)


def announce(place):
    barrier = pltpu.get_barrier_semaphore()

    def greet(k, carry):
        other = lax.rem(place.me + k, DEV)
        pl.semaphore_signal(
            barrier, inc=1, device_id=(other // 16, lax.rem(other, 16)), device_id_type=MESH
        )
        return carry

    lax.fori_loop(1, DEV, greet, 0)
    return barrier


def peers(place, c):
    zs = [lax.rem(place.z + j, 4) * 2 for j in range(4)]
    xs = [lax.rem(place.x + j, 4) * 4 for j in range(4)]
    ys = [lax.rem(place.y + c + j, 4) for j in range(4)]
    cores = [place.core, 1 - place.core]
    return [
        (zs[a] + cores[k], xs[(a + b) % 4] + ys[a])
        for b in range(4)
        for a in range(4)
        for k in range(2)
    ]


def fetch_kernel(
    item_owner,
    neg_owner,
    item_slot,
    neg_slot,
    table_ref,
    update_ref,
    rows_ref,
    ids_ref,
    pos_ref,
    table_vmem,
    faded,
    asked,
    stage,
    outbox,
    local_sem,
    id_send,
    id_recv,
    row_send,
    row_recv,
):
    place = Place()
    load = pltpu.make_async_copy(table_ref, table_vmem, local_sem)
    load.start()
    barrier = announce(place)
    owner = jnp.concatenate([item_owner[...], neg_owner[...]], 1)
    slot = jnp.concatenate([item_slot[...], neg_slot[...]], 1)
    onehot = (iota((DEV, ALL), 0) == owner).astype(F32)
    upto = (iota((ALL, ALL), 0) <= iota((ALL, ALL), 1)).astype(F32).astype(BF16)
    count = nn(onehot.astype(BF16), upto)
    rank = jnp.sum(onehot * count, 0, keepdims=True).astype(jnp.int32) - 1
    ranked = (iota((DEV, ALL), 0) == rank).astype(F32).astype(BF16)
    high = (onehot * (slot // 64).astype(F32)).astype(BF16)
    low = (onehot * (slot % 64).astype(F32)).astype(BF16)
    asked[...] = (64.0 * nt(high, ranked) + nt(low, ranked)).astype(jnp.int32)
    pos_ref[...] = rank * DEV + owner
    pl.semaphore_wait(barrier, DEV - 1)

    def ask(c, carry):
        for k, (d, t) in enumerate(peers(place, c)):

            def send(d=d, t=t):
                pltpu.make_async_remote_copy(
                    src_ref=asked.at[pl.ds(d * 16 + t, 1)],
                    dst_ref=ids_ref.at[pl.ds(place.me, 1)],
                    send_sem=id_send,
                    recv_sem=id_recv,
                    device_id=(d, t),
                    device_id_type=MESH,
                ).start()

            if k == 0:
                pl.when(c > 0)(send)
            else:
                send()
        return carry

    lax.fori_loop(0, 4, ask, 0)
    ids_ref[pl.ds(place.me, 1), :] = asked[pl.ds(place.me, 1), :]
    fade = jnp.exp((NOW - update_ref[...]).astype(F32) * LOG_RHO)
    fade = jnp.transpose(jnp.concatenate([fade, jnp.zeros((96, 128), F32)], 0))
    load.wait()
    for c in range(32):
        block = table_vmem[c * 128 : (c + 1) * 128, :].astype(F32) * fade[:, c : c + 1]
        faded[c * 128 : (c + 1) * 128, :] = block.astype(BF16)
    most = asked.at[pl.ds(0, DEV - 1)]
    pltpu.make_async_copy(most, most, id_send).wait()
    pltpu.make_async_copy(most, most, id_recv).wait()

    def serve(c, carry):
        group = peers(place, c)
        wanted = jnp.concatenate([ids_ref[pl.ds(d * 16 + t, 1), :] for d, t in group], 0)
        chosen = [
            (iota((32, ROWS), 1) == wanted[:, r : r + 1]).astype(F32).astype(BF16)
            for r in range(CAP)
        ]
        found = nn(jnp.concatenate(chosen, 0), faded[...])
        for r in range(CAP):
            for b in range(4):
                stage[pl.ds(4 * r + b, 32, stride=MSG), :] = found[
                    r * 32 : (r + 1) * 32, b * 128 : (b + 1) * 128
                ]
        base = c * 32
        outbox[pl.ds(base, 32)] = stage[...].astype(BF16).reshape(32, MSG, 128)
        for k, (d, t) in enumerate(group):

            def send(k=k, d=d, t=t):
                pltpu.make_async_remote_copy(
                    src_ref=outbox.at[base + k],
                    dst_ref=rows_ref.at[place.me],
                    send_sem=row_send,
                    recv_sem=row_recv,
                    device_id=(d, t),
                    device_id_type=MESH,
                ).start()

            if k == 0:
                pl.when(c > 0)(send)
            else:
                send()
        return carry

    for r in range(CAP * 4, MSG):
        stage[pl.ds(r, 32, stride=MSG), :] = jnp.zeros((32, 128), F32)
    lax.fori_loop(0, 4, serve, 0)
    rows_ref[place.me] = outbox[0]
    most = outbox.at[pl.ds(0, DEV - 1)]
    pltpu.make_async_copy(most, most, row_send).wait()
    pltpu.make_async_copy(most, most, row_recv).wait()


def fetch(item_owner, neg_owner, item_slot, neg_slot, table, update):
    return pl.pallas_call(
        fetch_kernel,
        out_shape=(
            jax.ShapeDtypeStruct((DEV, MSG, 128), BF16),
            jax.ShapeDtypeStruct((DEV, 128), jnp.int32),
            jax.ShapeDtypeStruct((1, ALL), jnp.int32),
        ),
        in_specs=[VMEM, VMEM, VMEM, VMEM, ANY, VMEM],
        out_specs=(VMEM, VMEM, VMEM),
        scratch_shapes=[
            pltpu.VMEM((ROWS, D), BF16),
            pltpu.VMEM((ROWS, D), BF16),
            pltpu.VMEM((DEV, 128), jnp.int32),
            pltpu.VMEM((32 * MSG, 128), F32),
            pltpu.VMEM((DEV, MSG, 128), BF16),
            pltpu.SemaphoreType.DMA,
            pltpu.SemaphoreType.DMA,
            pltpu.SemaphoreType.DMA,
            pltpu.SemaphoreType.DMA,
            pltpu.SemaphoreType.DMA,
        ],
        compiler_params=pltpu.CompilerParams(
            collective_id=0, has_side_effects=True, vmem_limit_bytes=50 << 20
        ),
        name="fetch",
    )(
        item_owner.reshape(1, TOK),
        neg_owner.reshape(1, NEG),
        item_slot.reshape(1, TOK),
        neg_slot.reshape(1, NEG),
        table,
        update,
    )


def reduce_kernel(
    box_ref,
    grad_ref,
    arrived_ref,
    total_ref,
    half,
    acc0,
    acc1,
    acc2,
    in1,
    in2,
    in3,
    row_send,
    row_recv,
    core_send,
    core_recv,
    step_send,
    step_recv,
):
    place = Place()
    barrier = announce(place)
    arrived_ref[place.me] = box_ref[place.me]
    pl.semaphore_wait(barrier, DEV - 1)
    mine = pl.multiple_of(place.core * 256, 256)
    other = pl.multiple_of((1 - place.core) * 256, 256)
    swap = pltpu.make_async_remote_copy(
        src_ref=grad_ref.at[pl.ds(other, 256)],
        dst_ref=half,
        send_sem=core_send.at[0],
        recv_sem=core_recv.at[0],
        device_id=place.sibling(),
        device_id_type=MESH,
    )
    swap.start()

    def post(c):
        for k, (d, t) in enumerate(peers(place, c)):
            if c == 0 and k == 0:
                continue
            pltpu.make_async_remote_copy(
                src_ref=box_ref.at[d * 16 + t],
                dst_ref=arrived_ref.at[place.me],
                send_sem=row_send,
                recv_sem=row_recv,
                device_id=(d, t),
                device_id_type=MESH,
            ).start()

    coordinate = {"x": place.x, "y": place.y, "z": place.z}
    axes = (("x", "y", "z"), ("y", "z", "x"), ("z", "x", "y"))

    def send(p, step, shift, src, dst):
        copy = pltpu.make_async_remote_copy(
            src_ref=src,
            dst_ref=dst,
            send_sem=step_send.at[p, step, shift - 1],
            recv_sem=step_recv.at[p, step, shift - 1],
            device_id=place.along(axes[p][(0, 1, 2, 1, 0)[step]], shift),
            device_id_type=MESH,
        )
        copy.start()
        return copy

    post(0)
    swap.wait()
    acc0[...] = (grad_ref[pl.ds(mine, 256), :].astype(F32) + half[...].astype(F32)).astype(BF16)
    first = []
    for p, (start, width) in enumerate(PARTS):
        at = coordinate[axes[p][0]]
        cols = pl.ds(start, width)
        for shift in (1, 2, 3):
            to = pl.multiple_of(lax.rem(at + shift, 4) * 64, 64)
            first.append(
                send(p, 0, shift, acc0.at[pl.ds(to, 64), cols], in1.at[shift - 1, :, cols])
            )
    post(1)
    second = []
    for p, (start, width) in enumerate(PARTS):
        at = coordinate[axes[p][0]]
        cols = pl.ds(start, width)
        for copy in first[3 * p : 3 * p + 3]:
            copy.wait()
        total = acc0[pl.ds(pl.multiple_of(at * 64, 64), 64), cols].astype(F32)
        for k in range(3):
            total += in1[k, :, cols].astype(F32)
        acc1[:, cols] = total.astype(BF16)
        at = coordinate[axes[p][1]]
        for shift in (1, 2, 3):
            to = pl.multiple_of(lax.rem(at + shift, 4) * 16, 16)
            second.append(
                send(p, 1, shift, acc1.at[pl.ds(to, 16), cols], in2.at[shift - 1, :, cols])
            )
    post(2)
    third = []
    for p, (start, width) in enumerate(PARTS):
        at = coordinate[axes[p][1]]
        cols = pl.ds(start, width)
        for copy in second[3 * p : 3 * p + 3]:
            copy.wait()
        total = acc1[pl.ds(pl.multiple_of(at * 16, 16), 16), cols].astype(F32)
        for k in range(3):
            total += in2[k, :, cols].astype(F32)
        acc2[:, cols] = total.astype(BF16)
        at = coordinate[axes[p][2]]
        in3[at, :, cols] = acc2[:, cols]
        for shift in (1, 2, 3):
            third.append(send(p, 2, shift, acc2.at[:, cols], in3.at[at, :, cols]))
    post(3)
    fourth = []
    places = []
    for p, (start, width) in enumerate(PARTS):
        cols = pl.ds(start, width)
        for copy in third[3 * p : 3 * p + 3]:
            copy.wait()
        total = in3[0, :, cols].astype(F32)
        for k in range(1, 4):
            total += in3[k, :, cols].astype(F32)
        wide = pl.multiple_of(mine + coordinate[axes[p][0]] * 64, 64)
        narrow = pl.multiple_of(wide + coordinate[axes[p][1]] * 16, 16)
        places.append(wide)
        total_ref[pl.ds(narrow, 16), cols] = total.astype(BF16)
        piece = total_ref.at[pl.ds(narrow, 16), cols]
        for shift in (1, 2, 3):
            fourth.append(send(p, 3, shift, piece, piece))
    fifth = []
    for p, (start, width) in enumerate(PARTS):
        for copy in fourth[3 * p : 3 * p + 3]:
            copy.wait()
        piece = total_ref.at[pl.ds(places[p], 64), pl.ds(start, width)]
        for shift in (1, 2, 3):
            fifth.append(send(p, 4, shift, piece, piece))
    last = []
    for p, (start, width) in enumerate(PARTS):
        for copy in fifth[3 * p : 3 * p + 3]:
            copy.wait()
        piece = total_ref.at[pl.ds(mine, 256), pl.ds(start, width)]
        copy = pltpu.make_async_remote_copy(
            src_ref=piece,
            dst_ref=piece,
            send_sem=core_send.at[p + 1],
            recv_sem=core_recv.at[p + 1],
            device_id=place.sibling(),
            device_id_type=MESH,
        )
        copy.start()
        last.append(copy)
    for copy in last:
        copy.wait()
    most = box_ref.at[pl.ds(0, DEV - 1)]
    pltpu.make_async_copy(most, most, row_send).wait()
    pltpu.make_async_copy(most, most, row_recv).wait()


def reduce(box, grad):
    return pl.pallas_call(
        reduce_kernel,
        out_shape=(
            jax.ShapeDtypeStruct((DEV, MSG, 128), BF16),
            jax.ShapeDtypeStruct((D, WIDE), BF16),
        ),
        in_specs=[VMEM, VMEM],
        out_specs=(VMEM, VMEM),
        scratch_shapes=[
            pltpu.VMEM((256, WIDE), BF16),
            pltpu.VMEM((256, WIDE), BF16),
            pltpu.VMEM((64, WIDE), BF16),
            pltpu.VMEM((16, WIDE), BF16),
            pltpu.VMEM((3, 64, WIDE), BF16),
            pltpu.VMEM((3, 16, WIDE), BF16),
            pltpu.VMEM((4, 16, WIDE), BF16),
            pltpu.SemaphoreType.DMA,
            pltpu.SemaphoreType.DMA,
            pltpu.SemaphoreType.DMA((4,)),
            pltpu.SemaphoreType.DMA((4,)),
            pltpu.SemaphoreType.DMA((3, 5, 3)),
            pltpu.SemaphoreType.DMA((3, 5, 3)),
        ],
        compiler_params=pltpu.CompilerParams(
            collective_id=1, has_side_effects=True, vmem_limit_bytes=48 << 20
        ),
        name="reduce",
    )(box, grad)


def scatter_kernel(arrived_ref, ids_ref, update_ref, out_ref, wide, rows, slots):
    step = pl.program_id(0)

    @pl.when(step == 0)
    def _():
        for s in range(8):
            block = arrived_ref[s * 16 : (s + 1) * 16].astype(F32)
            wide[s * 16 * MSG : (s + 1) * 16 * MSG, :] = block.reshape(16 * MSG, 128)
        for c in range(CAP):
            for b in range(4):
                piece = wide[pl.ds(4 * c + b, DEV, stride=MSG), :]
                rows[c * 128 : (c + 1) * 128, b * 128 : (b + 1) * 128] = piece.astype(BF16)
        slots[...] = jnp.transpose(ids_ref[...])[:16, :]

    fade = jnp.exp((NOW - update_ref[...]).astype(F32) * LOG_RHO)
    fade = jnp.transpose(jnp.concatenate([fade, jnp.zeros((120, 128), F32)], 0))
    for s in range(8):
        first = step * 1024 + s * 128
        chosen = [
            (iota((128, 128), 0) + first == slots[c : c + 1, :]).astype(F32).astype(BF16)
            for c in range(CAP)
        ]
        summed = nn(jnp.concatenate(chosen, 1), rows[...])
        out_ref[s * 128 : (s + 1) * 128, :] = summed * fade[:, s : s + 1]


def scatter(arrived, ids, update):
    return pl.pallas_call(
        scatter_kernel,
        grid=(4,),
        out_shape=jax.ShapeDtypeStruct((ROWS, D), F32),
        in_specs=[
            pl.BlockSpec((DEV, MSG, 128), lambda i: (0, 0, 0)),
            pl.BlockSpec((DEV, 128), lambda i: (0, 0)),
            pl.BlockSpec((8, 128), lambda i: (i, 0)),
        ],
        out_specs=pl.BlockSpec((1024, D), lambda i: (i, 0)),
        scratch_shapes=[
            pltpu.VMEM((DEV * MSG, 128), F32),
            pltpu.VMEM((CAP * 128, D), BF16),
            pltpu.VMEM((16, 128), jnp.int32),
        ],
        compiler_params=pltpu.CompilerParams(vmem_limit_bytes=48 << 20),
        name="scatter",
    )(arrived, ids, update)


def normalize(values):
    center = values - jnp.mean(values, -1, keepdims=True)
    return center * lax.rsqrt(jnp.mean(center * center, -1, keepdims=True) + EPS)


def layer_loss(rows32, w_in32, w_out32, lengths):
    width = rows32.shape[1]
    x32 = rows32[:TOK]
    negatives = rows32[TOK:].astype(jnp.bfloat16)
    ends = jnp.cumsum(lengths)
    where = jnp.arange(TOK, dtype=jnp.int32)
    segment = jnp.sum((where[:, None] >= ends[None, :]).astype(jnp.int32), 1)
    normed = normalize(x32).astype(jnp.bfloat16)
    mixed = jax.nn.silu(
        jnp.dot(normed, w_in32.astype(jnp.bfloat16), preferred_element_type=jnp.float32)
    ).astype(jnp.bfloat16)
    gate_part, value, query, key_part = jnp.split(mixed, 4, axis=1)
    query = query.reshape(TOK, H, DH)
    key_part = key_part.reshape(TOK, H, DH)
    value = value.reshape(TOK, H, DH)
    scores = jnp.einsum("qhd,khd->hqk", query, key_part, preferred_element_type=jnp.float32)
    visible = (segment[:, None] == segment[None, :]) & (where[None, :] <= where[:, None])
    weights = (jax.nn.silu(scores) * (1.0 / LMAX) * visible[None].astype(jnp.float32)).astype(
        jnp.bfloat16
    )
    attended = jnp.einsum(
        "hqk,khd->qhd", weights, value, preferred_element_type=jnp.float32
    ).reshape(TOK, width)
    gated = (normalize(attended) * gate_part.astype(jnp.float32)).astype(jnp.bfloat16)
    out = (
        x32 + jnp.dot(gated, w_out32.astype(jnp.bfloat16), preferred_element_type=jnp.float32)
    ).astype(jnp.bfloat16)
    following = jnp.concatenate([x32[1:], jnp.zeros((1, width), jnp.float32)], 0)
    valid = jnp.concatenate([segment[1:] == segment[:-1], jnp.zeros((1,), bool)]).astype(
        jnp.float32
    )
    positive = jnp.sum(out.astype(jnp.float32) * following, 1) * TAU
    negative = jnp.dot(out, negatives.T, preferred_element_type=jnp.float32) * TAU
    top = lax.stop_gradient(jnp.maximum(positive, jnp.max(negative, 1)))
    total = jnp.exp(positive - top) + jnp.sum(jnp.exp(negative - top[:, None]), 1)
    losses = (jnp.log(total) + top - positive) * valid
    return (jnp.sum(losses), losses)


def layer(rows, pos, w_in, w_out, lengths):
    flat = rows[:, : 4 * CAP].reshape(DEV, CAP, D)
    owner, rank = pos[0] % DEV, pos[0] // DEV
    rows32 = flat[owner, rank].astype(F32)
    fn = lambda r, a, b: layer_loss(r, a, b, lengths)
    total, pull, losses = jax.vjp(fn, rows32, w_in.astype(F32), w_out.astype(F32), has_aux=True)
    grad_rows, grad_a, grad_b = pull(jnp.float32(1.0))
    chosen = (jnp.arange(CAP * DEV)[:, None] == pos).astype(BF16)
    sent = jnp.dot(chosen, grad_rows.astype(BF16), preferred_element_type=F32).astype(BF16)
    sent = sent.reshape(CAP, DEV, 4, 128).transpose(1, 0, 2, 3).reshape(DEV, 4 * CAP, 128)
    box = jnp.pad(sent, ((0, 0), (0, MSG - 4 * CAP), (0, 0)))
    grad = jnp.concatenate([grad_a, grad_b], 1).astype(BF16)
    return losses, box, grad


def on_device(
    table, last_update, item_owner, item_slot, neg_owner, neg_slot, seq_lengths, w_in, w_out
):
    update = last_update.reshape(ROWS // 128, 128)
    rows, ids, pos = fetch(item_owner, neg_owner, item_slot, neg_slot, table, update)
    losses, box, grad = layer(rows, pos, w_in, w_out, seq_lengths[0])
    arrived, total = reduce(box, grad)
    table_grad = scatter(arrived, ids, update)
    grad_in = total[:, : 4 * D].astype(F32)
    grad_out = total[:, 4 * D :].astype(F32)
    return (losses, table_grad, grad_in, grad_out)


def solution(mesh):
    placed = (
        P(("dp", "table"), None),
        P(("dp", "table")),
        P(("dp", "table"), None),
        P(("dp", "table")),
        P(("dp", "table"), None),
        P(("dp", "table")),
        P(("dp", "table"), None),
        P(),
        P(),
    )
    return jax.shard_map(
        on_device,
        mesh=mesh,
        in_specs=placed,
        out_specs=(P(("dp", "table")), P(("dp", "table"), None), P(), P()),
        check_vma=False,
    )
```

```python
import functools

import jax
import jax.numpy as jnp
from jax import lax
from jax.experimental import pallas as pl
from jax.experimental.pallas import tpu as pltpu
from jax.sharding import PartitionSpec as P

D = 512
H = 4
DH = 128
TOK = 512
NEG = 128
ALL = TOK + NEG
DEV = 128
CAP = 10
MSG = 48
LMAX = 256
NOW = 64
ROWS = 4096
WIDE = 5 * D
LOG_RHO = -0.030459207484708574
TAU = 0.125
EPS = 1e-05
MESH = pl.DeviceIdType.MESH
VMEM = pl.BlockSpec(memory_space=pltpu.VMEM)
ANY = pl.BlockSpec(memory_space=pl.ANY)
F32 = jnp.float32
BF16 = jnp.bfloat16
PARTS = ((0, 896), (896, 896), (1792, 768))


def nt(a, b):
    return lax.dot_general(a, b, (((1,), (1,)), ((), ())), preferred_element_type=F32)


def nn(a, b):
    return jnp.dot(a, b, preferred_element_type=F32)


def tn(a, b):
    return lax.dot_general(a, b, (((0,), (0,)), ((), ())), preferred_element_type=F32)


def iota(shape, dim):
    return lax.broadcasted_iota(jnp.int32, shape, dim)


class Place:
    def __init__(self):
        self.dp = lax.axis_index("dp")
        self.tb = lax.axis_index("table")
        self.me = self.dp * 16 + self.tb
        self.z = self.dp // 2
        self.core = lax.rem(self.dp, 2)
        self.x = self.tb // 4
        self.y = lax.rem(self.tb, 4)

    def along(self, axis, shift):
        z, x, y = self.z, self.x, self.y
        if axis == "z":
            z = lax.rem(z + shift, 4)
        if axis == "x":
            x = lax.rem(x + shift, 4)
        if axis == "y":
            y = lax.rem(y + shift, 4)
        return (z * 2 + self.core, x * 4 + y)

    def sibling(self):
        return (self.z * 2 + 1 - self.core, self.tb)


def announce(place):
    barrier = pltpu.get_barrier_semaphore()

    def greet(k, carry):
        other = lax.rem(place.me + k, DEV)
        pl.semaphore_signal(
            barrier, inc=1, device_id=(other // 16, lax.rem(other, 16)), device_id_type=MESH
        )
        return carry

    lax.fori_loop(1, DEV, greet, 0)
    return barrier


def peers(place, c):
    zs = [lax.rem(place.z + j, 4) * 2 for j in range(4)]
    xs = [lax.rem(place.x + j, 4) * 4 for j in range(4)]
    ys = [lax.rem(place.y + c + j, 4) for j in range(4)]
    cores = [place.core, 1 - place.core]
    return [
        (zs[a] + cores[k], xs[(a + b) % 4] + ys[a])
        for b in range(4)
        for a in range(4)
        for k in range(2)
    ]


def fetch_kernel(
    item_owner,
    neg_owner,
    item_slot,
    neg_slot,
    table_ref,
    update_ref,
    rows_ref,
    ids_ref,
    pos_ref,
    table_vmem,
    faded,
    asked,
    stage,
    outbox,
    local_sem,
    id_send,
    id_recv,
    row_send,
    row_recv,
):
    place = Place()
    load = pltpu.make_async_copy(table_ref, table_vmem, local_sem)
    load.start()
    barrier = announce(place)
    owner = jnp.concatenate([item_owner[...], neg_owner[...]], 1)
    slot = jnp.concatenate([item_slot[...], neg_slot[...]], 1)
    onehot = (iota((DEV, ALL), 0) == owner).astype(F32)
    upto = (iota((ALL, ALL), 0) <= iota((ALL, ALL), 1)).astype(F32).astype(BF16)
    count = nn(onehot.astype(BF16), upto)
    rank = jnp.sum(onehot * count, 0, keepdims=True).astype(jnp.int32) - 1
    ranked = (iota((DEV, ALL), 0) == rank).astype(F32).astype(BF16)
    high = (onehot * (slot // 64).astype(F32)).astype(BF16)
    low = (onehot * (slot % 64).astype(F32)).astype(BF16)
    asked[...] = (64.0 * nt(high, ranked) + nt(low, ranked)).astype(jnp.int32)
    pos_ref[...] = rank * DEV + owner
    pl.semaphore_wait(barrier, DEV - 1)

    def ask(c, carry):
        for k, (d, t) in enumerate(peers(place, c)):

            def send(d=d, t=t):
                pltpu.make_async_remote_copy(
                    src_ref=asked.at[pl.ds(d * 16 + t, 1)],
                    dst_ref=ids_ref.at[pl.ds(place.me, 1)],
                    send_sem=id_send,
                    recv_sem=id_recv,
                    device_id=(d, t),
                    device_id_type=MESH,
                ).start()

            if k == 0:
                pl.when(c > 0)(send)
            else:
                send()
        return carry

    lax.fori_loop(0, 4, ask, 0)
    ids_ref[pl.ds(place.me, 1), :] = asked[pl.ds(place.me, 1), :]
    fade = jnp.exp((NOW - update_ref[...]).astype(F32) * LOG_RHO)
    fade = jnp.transpose(jnp.concatenate([fade, jnp.zeros((96, 128), F32)], 0))
    load.wait()
    for c in range(32):
        block = table_vmem[c * 128 : (c + 1) * 128, :].astype(F32) * fade[:, c : c + 1]
        faded[c * 128 : (c + 1) * 128, :] = block.astype(BF16)
    most = asked.at[pl.ds(0, DEV - 1)]
    pltpu.make_async_copy(most, most, id_send).wait()
    pltpu.make_async_copy(most, most, id_recv).wait()

    def serve(c, carry):
        group = peers(place, c)
        wanted = jnp.concatenate([ids_ref[pl.ds(d * 16 + t, 1), :] for d, t in group], 0)
        chosen = [
            (iota((32, ROWS), 1) == wanted[:, r : r + 1]).astype(F32).astype(BF16)
            for r in range(CAP)
        ]
        found = nn(jnp.concatenate(chosen, 0), faded[...])
        for r in range(CAP):
            for b in range(4):
                stage[pl.ds(4 * r + b, 32, stride=MSG), :] = found[
                    r * 32 : (r + 1) * 32, b * 128 : (b + 1) * 128
                ]
        base = c * 32
        outbox[pl.ds(base, 32)] = stage[...].astype(BF16).reshape(32, MSG, 128)
        for k, (d, t) in enumerate(group):

            def send(k=k, d=d, t=t):
                pltpu.make_async_remote_copy(
                    src_ref=outbox.at[base + k],
                    dst_ref=rows_ref.at[place.me],
                    send_sem=row_send,
                    recv_sem=row_recv,
                    device_id=(d, t),
                    device_id_type=MESH,
                ).start()

            if k == 0:
                pl.when(c > 0)(send)
            else:
                send()
        return carry

    for r in range(CAP * 4, MSG):
        stage[pl.ds(r, 32, stride=MSG), :] = jnp.zeros((32, 128), F32)
    lax.fori_loop(0, 4, serve, 0)
    rows_ref[place.me] = outbox[0]
    most = outbox.at[pl.ds(0, DEV - 1)]
    pltpu.make_async_copy(most, most, row_send).wait()
    pltpu.make_async_copy(most, most, row_recv).wait()


def fetch(item_owner, neg_owner, item_slot, neg_slot, table, update):
    return pl.pallas_call(
        fetch_kernel,
        out_shape=(
            jax.ShapeDtypeStruct((DEV, MSG, 128), BF16),
            jax.ShapeDtypeStruct((DEV, 128), jnp.int32),
            jax.ShapeDtypeStruct((1, ALL), jnp.int32),
        ),
        in_specs=[VMEM, VMEM, VMEM, VMEM, ANY, VMEM],
        out_specs=(VMEM, VMEM, VMEM),
        scratch_shapes=[
            pltpu.VMEM((ROWS, D), BF16),
            pltpu.VMEM((ROWS, D), BF16),
            pltpu.VMEM((DEV, 128), jnp.int32),
            pltpu.VMEM((32 * MSG, 128), F32),
            pltpu.VMEM((DEV, MSG, 128), BF16),
            pltpu.SemaphoreType.DMA,
            pltpu.SemaphoreType.DMA,
            pltpu.SemaphoreType.DMA,
            pltpu.SemaphoreType.DMA,
            pltpu.SemaphoreType.DMA,
        ],
        compiler_params=pltpu.CompilerParams(
            collective_id=0, has_side_effects=True, vmem_limit_bytes=50 << 20
        ),
        name="fetch",
    )(
        item_owner.reshape(1, TOK),
        neg_owner.reshape(1, NEG),
        item_slot.reshape(1, TOK),
        neg_slot.reshape(1, NEG),
        table,
        update,
    )


def reduce_kernel(
    box_ref,
    grad_ref,
    arrived_ref,
    total_ref,
    half,
    acc0,
    acc1,
    acc2,
    in1,
    in2,
    in3,
    row_send,
    row_recv,
    core_send,
    core_recv,
    step_send,
    step_recv,
):
    place = Place()
    barrier = announce(place)
    arrived_ref[place.me] = box_ref[place.me]
    pl.semaphore_wait(barrier, DEV - 1)
    mine = pl.multiple_of(place.core * 256, 256)
    other = pl.multiple_of((1 - place.core) * 256, 256)
    swap = pltpu.make_async_remote_copy(
        src_ref=grad_ref.at[pl.ds(other, 256)],
        dst_ref=half,
        send_sem=core_send.at[0],
        recv_sem=core_recv.at[0],
        device_id=place.sibling(),
        device_id_type=MESH,
    )
    swap.start()

    def post(c):
        for k, (d, t) in enumerate(peers(place, c)):
            if c == 0 and k == 0:
                continue
            pltpu.make_async_remote_copy(
                src_ref=box_ref.at[d * 16 + t],
                dst_ref=arrived_ref.at[place.me],
                send_sem=row_send,
                recv_sem=row_recv,
                device_id=(d, t),
                device_id_type=MESH,
            ).start()

    coordinate = {"x": place.x, "y": place.y, "z": place.z}
    axes = (("x", "y", "z"), ("y", "z", "x"), ("z", "x", "y"))

    def send(p, step, shift, src, dst):
        copy = pltpu.make_async_remote_copy(
            src_ref=src,
            dst_ref=dst,
            send_sem=step_send.at[p, step, shift - 1],
            recv_sem=step_recv.at[p, step, shift - 1],
            device_id=place.along(axes[p][(0, 1, 2, 1, 0)[step]], shift),
            device_id_type=MESH,
        )
        copy.start()
        return copy

    post(0)
    swap.wait()
    acc0[...] = (grad_ref[pl.ds(mine, 256), :].astype(F32) + half[...].astype(F32)).astype(BF16)
    first = []
    for p, (start, width) in enumerate(PARTS):
        at = coordinate[axes[p][0]]
        cols = pl.ds(start, width)
        for shift in (1, 2, 3):
            to = pl.multiple_of(lax.rem(at + shift, 4) * 64, 64)
            first.append(
                send(p, 0, shift, acc0.at[pl.ds(to, 64), cols], in1.at[shift - 1, :, cols])
            )
    post(1)
    second = []
    for p, (start, width) in enumerate(PARTS):
        at = coordinate[axes[p][0]]
        cols = pl.ds(start, width)
        for copy in first[3 * p : 3 * p + 3]:
            copy.wait()
        total = acc0[pl.ds(pl.multiple_of(at * 64, 64), 64), cols].astype(F32)
        for k in range(3):
            total += in1[k, :, cols].astype(F32)
        acc1[:, cols] = total.astype(BF16)
        at = coordinate[axes[p][1]]
        for shift in (1, 2, 3):
            to = pl.multiple_of(lax.rem(at + shift, 4) * 16, 16)
            second.append(
                send(p, 1, shift, acc1.at[pl.ds(to, 16), cols], in2.at[shift - 1, :, cols])
            )
    post(2)
    third = []
    for p, (start, width) in enumerate(PARTS):
        at = coordinate[axes[p][1]]
        cols = pl.ds(start, width)
        for copy in second[3 * p : 3 * p + 3]:
            copy.wait()
        total = acc1[pl.ds(pl.multiple_of(at * 16, 16), 16), cols].astype(F32)
        for k in range(3):
            total += in2[k, :, cols].astype(F32)
        acc2[:, cols] = total.astype(BF16)
        at = coordinate[axes[p][2]]
        in3[at, :, cols] = acc2[:, cols]
        for shift in (1, 2, 3):
            third.append(send(p, 2, shift, acc2.at[:, cols], in3.at[at, :, cols]))
    post(3)
    fourth = []
    places = []
    for p, (start, width) in enumerate(PARTS):
        cols = pl.ds(start, width)
        for copy in third[3 * p : 3 * p + 3]:
            copy.wait()
        total = in3[0, :, cols].astype(F32)
        for k in range(1, 4):
            total += in3[k, :, cols].astype(F32)
        wide = pl.multiple_of(mine + coordinate[axes[p][0]] * 64, 64)
        narrow = pl.multiple_of(wide + coordinate[axes[p][1]] * 16, 16)
        places.append(wide)
        total_ref[pl.ds(narrow, 16), cols] = total.astype(BF16)
        piece = total_ref.at[pl.ds(narrow, 16), cols]
        for shift in (1, 2, 3):
            fourth.append(send(p, 3, shift, piece, piece))
    fifth = []
    for p, (start, width) in enumerate(PARTS):
        for copy in fourth[3 * p : 3 * p + 3]:
            copy.wait()
        piece = total_ref.at[pl.ds(places[p], 64), pl.ds(start, width)]
        for shift in (1, 2, 3):
            fifth.append(send(p, 4, shift, piece, piece))
    last = []
    for p, (start, width) in enumerate(PARTS):
        for copy in fifth[3 * p : 3 * p + 3]:
            copy.wait()
        piece = total_ref.at[pl.ds(mine, 256), pl.ds(start, width)]
        copy = pltpu.make_async_remote_copy(
            src_ref=piece,
            dst_ref=piece,
            send_sem=core_send.at[p + 1],
            recv_sem=core_recv.at[p + 1],
            device_id=place.sibling(),
            device_id_type=MESH,
        )
        copy.start()
        last.append(copy)
    for copy in last:
        copy.wait()
    most = box_ref.at[pl.ds(0, DEV - 1)]
    pltpu.make_async_copy(most, most, row_send).wait()
    pltpu.make_async_copy(most, most, row_recv).wait()


def reduce(box, grad):
    return pl.pallas_call(
        reduce_kernel,
        out_shape=(
            jax.ShapeDtypeStruct((DEV, MSG, 128), BF16),
            jax.ShapeDtypeStruct((D, WIDE), BF16),
        ),
        in_specs=[VMEM, VMEM],
        out_specs=(VMEM, VMEM),
        scratch_shapes=[
            pltpu.VMEM((256, WIDE), BF16),
            pltpu.VMEM((256, WIDE), BF16),
            pltpu.VMEM((64, WIDE), BF16),
            pltpu.VMEM((16, WIDE), BF16),
            pltpu.VMEM((3, 64, WIDE), BF16),
            pltpu.VMEM((3, 16, WIDE), BF16),
            pltpu.VMEM((4, 16, WIDE), BF16),
            pltpu.SemaphoreType.DMA,
            pltpu.SemaphoreType.DMA,
            pltpu.SemaphoreType.DMA((4,)),
            pltpu.SemaphoreType.DMA((4,)),
            pltpu.SemaphoreType.DMA((3, 5, 3)),
            pltpu.SemaphoreType.DMA((3, 5, 3)),
        ],
        compiler_params=pltpu.CompilerParams(
            collective_id=1, has_side_effects=True, vmem_limit_bytes=48 << 20
        ),
        name="reduce",
    )(box, grad)


def scatter_kernel(arrived_ref, ids_ref, update_ref, out_ref, wide, rows, slots):
    step = pl.program_id(0)

    @pl.when(step == 0)
    def _():
        for s in range(8):
            block = arrived_ref[s * 16 : (s + 1) * 16].astype(F32)
            wide[s * 16 * MSG : (s + 1) * 16 * MSG, :] = block.reshape(16 * MSG, 128)
        for c in range(CAP):
            for b in range(4):
                piece = wide[pl.ds(4 * c + b, DEV, stride=MSG), :]
                rows[c * 128 : (c + 1) * 128, b * 128 : (b + 1) * 128] = piece.astype(BF16)
        slots[...] = jnp.transpose(ids_ref[...])[:16, :]

    fade = jnp.exp((NOW - update_ref[...]).astype(F32) * LOG_RHO)
    fade = jnp.transpose(jnp.concatenate([fade, jnp.zeros((120, 128), F32)], 0))
    for s in range(8):
        first = step * 1024 + s * 128
        chosen = [
            (iota((128, 128), 0) + first == slots[c : c + 1, :]).astype(F32).astype(BF16)
            for c in range(CAP)
        ]
        summed = nn(jnp.concatenate(chosen, 1), rows[...])
        out_ref[s * 128 : (s + 1) * 128, :] = summed * fade[:, s : s + 1]


def scatter(arrived, ids, update):
    return pl.pallas_call(
        scatter_kernel,
        grid=(4,),
        out_shape=jax.ShapeDtypeStruct((ROWS, D), F32),
        in_specs=[
            pl.BlockSpec((DEV, MSG, 128), lambda i: (0, 0, 0)),
            pl.BlockSpec((DEV, 128), lambda i: (0, 0)),
            pl.BlockSpec((8, 128), lambda i: (i, 0)),
        ],
        out_specs=pl.BlockSpec((1024, D), lambda i: (i, 0)),
        scratch_shapes=[
            pltpu.VMEM((DEV * MSG, 128), F32),
            pltpu.VMEM((CAP * 128, D), BF16),
            pltpu.VMEM((16, 128), jnp.int32),
        ],
        compiler_params=pltpu.CompilerParams(vmem_limit_bytes=48 << 20),
        name="scatter",
    )(arrived, ids, update)


def layer_kernel(
    lengths,
    rows_ref,
    pos_ref,
    w_in,
    w_out,
    loss_ref,
    box_ref,
    grad_ref,
    flat,
    held,
    where,
    x32,
    n32,
    nb,
    scale1,
    negatives,
    mixed,
    slope,
    weights,
    bend,
    attended,
    gated,
    d_out,
    d_next,
    d_att,
    d_score,
    d_pre,
    grads,
):
    for s in range(8):
        block = rows_ref[s * 16 : (s + 1) * 16].astype(F32)
        flat[s * 16 * MSG : (s + 1) * 16 * MSG, :] = block.reshape(16 * MSG, 128)
    for c in range(CAP):
        for b in range(4):
            piece = flat[pl.ds(4 * c + b, DEV, stride=MSG), :]
            held[c * 128 : (c + 1) * 128, b * 128 : (b + 1) * 128] = piece.astype(BF16)
    where[...] = jnp.transpose(jnp.broadcast_to(pos_ref[...], (128, ALL)))

    def take(i):
        at = where[i * 128 : (i + 1) * 128, :]
        chosen = [
            (iota((128, 128), 1) + c * 128 == at).astype(F32).astype(BF16) for c in range(CAP)
        ]
        return nn(jnp.concatenate(chosen, 1), held[...])

    for i in range(4):
        x = take(i)
        span = pl.ds(i * 128, 128)
        x32[span, :] = x
        center = x - jnp.mean(x, -1, keepdims=True)
        scale = lax.rsqrt(jnp.mean(center * center, -1, keepdims=True) + EPS)
        normed = center * scale
        n32[span, :] = normed
        nb[span, :] = normed.astype(BF16)
        scale1[span, :] = scale
    x = take(4)
    x32[pl.ds(512, 128), :] = x
    negatives[...] = x.astype(BF16)

    def project(cb, carry):
        cols = pl.ds(pl.multiple_of(cb * 256, 256), 256)
        pre = nn(nb[...], w_in[:, cols])
        sig = jax.nn.sigmoid(pre)
        mixed[:, cols] = (pre * sig).astype(BF16)
        slope[:, cols] = (sig * (1.0 + pre * (1.0 - sig))).astype(BF16)
        return carry

    lax.fori_loop(0, 8, project, 0)

    end1 = lengths[0, 0]
    end2 = end1 + lengths[0, 1]
    end3 = end2 + lengths[0, 2]

    def lanes(part, h):
        return pl.ds(pl.multiple_of(part * 512 + h * 128, 128), 128)

    def visible(i):
        row = iota((256, 256 * (i + 1)), 0) + 256 * i
        col = iota((256, 256 * (i + 1)), 1)
        start = jnp.where(
            row >= end3, end3, jnp.where(row >= end2, end2, jnp.where(row >= end1, end1, 0))
        )
        return jnp.where((col <= row) & (col >= start), 1.0 / LMAX, 0.0).astype(F32)

    def attend(h, carry):
        for i in range(2):
            span, past = pl.ds(256 * i, 256), pl.ds(0, 256 * (i + 1))
            score = nt(mixed[span, lanes(2, h)], mixed[past, lanes(3, h)])
            sig = jax.nn.sigmoid(score)
            seen = visible(i)
            weight = (score * sig * seen).astype(BF16)
            weights[h, span, past] = weight
            bend[h, span, past] = (sig * (1.0 + score * (1.0 - sig)) * seen).astype(BF16)
            attended[span, lanes(0, h)] = nn(weight, mixed[past, lanes(1, h)])
        return carry

    lax.fori_loop(0, H, attend, 0)

    d_next[pl.ds(0, 8), :] = jnp.zeros((8, D), F32)
    d_negatives = jnp.zeros((NEG, D), F32)
    for i in range(2):
        span = pl.ds(256 * i, 256)
        values = attended[span, :]
        center = values - jnp.mean(values, -1, keepdims=True)
        scale = lax.rsqrt(jnp.mean(center * center, -1, keepdims=True) + EPS)
        normed = center * scale
        gate = mixed[span, 0:512].astype(F32)
        gated_b = (normed * gate).astype(BF16)
        gated[span, :] = gated_b
        out_b = (x32[span, :] + nn(gated_b, w_out[...])).astype(BF16)
        out = out_b.astype(F32)
        following = x32[pl.ds(256 * i + 1, 256), :]
        positive = jnp.sum(out * following, -1, keepdims=True) * TAU
        negative = nt(out_b, negatives[...]) * TAU
        top = jnp.maximum(positive, jnp.max(negative, -1, keepdims=True))
        exp_p = jnp.exp(positive - top)
        exp_n = jnp.exp(negative - top)
        total = exp_p + jnp.sum(exp_n, -1, keepdims=True)
        row = iota((256, 1), 0) + (256 * i + 1)
        valid = (row != end1) & (row != end2) & (row != end3) & (row != TOK)
        valid = jnp.where(valid, 1.0, 0.0).astype(F32)
        loss = (jnp.log(total) + top - positive) * valid
        loss_ref[:, span] = jnp.transpose(jnp.broadcast_to(loss, (256, 128)))[:1, :]
        share = valid / total
        d_pos = (exp_p * share - valid) * TAU
        d_neg = (exp_n * (share * TAU)).astype(BF16)
        d_out_b = (d_pos * following + nn(d_neg, negatives[...])).astype(BF16)
        d_out[span, :] = d_out_b
        d_next[pl.ds(256 * i + 8, 256), :] = d_pos * out
        d_negatives += tn(d_neg, out_b)
        d_gated = nt(d_out_b, w_out[...])
        d_pre[span, 0:512] = (d_gated * normed * slope[span, 0:512].astype(F32)).astype(BF16)
        d_normed = d_gated * gate
        d_values = scale * (
            d_normed
            - jnp.mean(d_normed, -1, keepdims=True)
            - normed * jnp.mean(d_normed * normed, -1, keepdims=True)
        )
        d_att[span, :] = d_values.astype(BF16)
    grads[pl.ds(TOK, NEG), :] = d_negatives.astype(BF16)

    def back(h, carry):
        for i in range(2):
            span, past = pl.ds(256 * i, 256), pl.ds(0, 256 * (i + 1))
            d_weight = nt(d_att[span, lanes(0, h)], mixed[past, lanes(1, h)])
            d_s = (d_weight * bend[h, span, past].astype(F32)).astype(BF16)
            d_score[span, past] = d_s
            d_q = nn(d_s, mixed[past, lanes(3, h)])
            d_pre[span, lanes(2, h)] = (d_q * slope[span, lanes(2, h)].astype(F32)).astype(BF16)
        for i in range(2):
            span, future = pl.ds(256 * i, 256), pl.ds(256 * i, 512 - 256 * i)
            d_v = tn(weights[h, future, span], d_att[future, lanes(0, h)])
            d_pre[span, lanes(1, h)] = (d_v * slope[span, lanes(1, h)].astype(F32)).astype(BF16)
            d_k = tn(d_score[future, span], mixed[future, lanes(2, h)])
            d_pre[span, lanes(3, h)] = (d_k * slope[span, lanes(3, h)].astype(F32)).astype(BF16)
        return carry

    lax.fori_loop(0, H, back, 0)

    for i in range(2):
        span = pl.ds(256 * i, 256)
        d_normed = nt(d_pre[span, :], w_in[...])
        normed = n32[span, :]
        d_x = scale1[span, :] * (
            d_normed
            - jnp.mean(d_normed, -1, keepdims=True)
            - normed * jnp.mean(d_normed * normed, -1, keepdims=True)
        )
        d_x += d_out[span, :].astype(F32) + d_next[pl.ds(256 * i + 7, 256), :]
        grads[span, :] = d_x.astype(BF16)

    for j in range(CAP // 2):
        at = iota((256, ALL), 0) + j * 256
        sent = nn((at == pos_ref[...]).astype(F32).astype(BF16), grads[...])
        for c in range(2):
            for b in range(4):
                flat[pl.ds(4 * (2 * j + c) + b, DEV, stride=MSG), :] = sent[
                    c * 128 : (c + 1) * 128, b * 128 : (b + 1) * 128
                ]
    for s in range(8):
        block = flat[s * 16 * MSG : (s + 1) * 16 * MSG, :].astype(BF16)
        box_ref[s * 16 : (s + 1) * 16] = block.reshape(16, MSG, 128)

    def weigh(cb, carry):
        cols = pl.ds(pl.multiple_of(cb * 256, 256), 256)
        grad_ref[:, cols] = tn(nb[...], d_pre[:, cols]).astype(BF16)
        return carry

    lax.fori_loop(0, 8, weigh, 0)
    for cb in range(2):
        cols = pl.ds(cb * 256, 256)
        grad_ref[:, pl.ds(2048 + cb * 256, 256)] = tn(gated[...], d_out[:, cols]).astype(BF16)


def layer(rows, pos, w_in, w_out, lengths):
    losses, box, grad = pl.pallas_call(
        layer_kernel,
        out_shape=(
            jax.ShapeDtypeStruct((1, TOK), F32),
            jax.ShapeDtypeStruct((DEV, MSG, 128), BF16),
            jax.ShapeDtypeStruct((D, WIDE), BF16),
        ),
        in_specs=[pl.BlockSpec(memory_space=pltpu.SMEM), VMEM, VMEM, VMEM, VMEM],
        out_specs=(VMEM, VMEM, VMEM),
        scratch_shapes=[
            pltpu.VMEM((DEV * MSG, 128), F32),
            pltpu.VMEM((CAP * DEV, D), BF16),
            pltpu.VMEM((ALL, 128), jnp.int32),
            pltpu.VMEM((ALL, D), F32),
            pltpu.VMEM((TOK, D), F32),
            pltpu.VMEM((TOK, D), BF16),
            pltpu.VMEM((TOK, 1), F32),
            pltpu.VMEM((NEG, D), BF16),
            pltpu.VMEM((TOK, 4 * D), BF16),
            pltpu.VMEM((TOK, 4 * D), BF16),
            pltpu.VMEM((H, TOK, TOK), BF16),
            pltpu.VMEM((H, TOK, TOK), BF16),
            pltpu.VMEM((TOK, D), F32),
            pltpu.VMEM((TOK, D), BF16),
            pltpu.VMEM((TOK, D), BF16),
            pltpu.VMEM((TOK + 8, D), F32),
            pltpu.VMEM((TOK, D), BF16),
            pltpu.VMEM((TOK, TOK), BF16),
            pltpu.VMEM((TOK, 4 * D), BF16),
            pltpu.VMEM((ALL, D), BF16),
        ],
        compiler_params=pltpu.CompilerParams(vmem_limit_bytes=56 << 20),
        name="layer",
    )(lengths, rows, pos, w_in, w_out)
    return losses.reshape(TOK), box, grad


def on_device(
    table, last_update, item_owner, item_slot, neg_owner, neg_slot, seq_lengths, w_in, w_out
):
    update = last_update.reshape(ROWS // 128, 128)
    rows, ids, pos = fetch(item_owner, neg_owner, item_slot, neg_slot, table, update)
    losses, box, grad = layer(rows, pos, w_in, w_out, seq_lengths)
    arrived, total = reduce(box, grad)
    table_grad = scatter(arrived, ids, update)
    grad_in = total[:, : 4 * D].astype(F32)
    grad_out = total[:, 4 * D :].astype(F32)
    return (losses, table_grad, grad_in, grad_out)


def solution(mesh):
    placed = (
        P(("dp", "table"), None),
        P(("dp", "table")),
        P(("dp", "table"), None),
        P(("dp", "table")),
        P(("dp", "table"), None),
        P(("dp", "table")),
        P(("dp", "table"), None),
        P(),
        P(),
    )
    return jax.shard_map(
        on_device,
        mesh=mesh,
        in_specs=placed,
        out_specs=(P(("dp", "table")), P(("dp", "table"), None), P(), P()),
        check_vma=False,
    )
```

```python
import functools

import jax
import jax.numpy as jnp
from jax import lax
from jax.experimental import pallas as pl
from jax.experimental.pallas import tpu as pltpu
from jax.sharding import PartitionSpec as P

D = 512
H = 4
DH = 128
TOK = 512
NEG = 128
ALL = TOK + NEG
DEV = 128
CAP = 10
MSG = 48
LMAX = 256
NOW = 64
ROWS = 4096
WIDE = 5 * D
LOG_RHO = -0.030459207484708574
TAU = 0.125
EPS = 1e-05
MESH = pl.DeviceIdType.MESH
VMEM = pl.BlockSpec(memory_space=pltpu.VMEM)
ANY = pl.BlockSpec(memory_space=pl.ANY)
F32 = jnp.float32
BF16 = jnp.bfloat16


def nt(a, b):
    return lax.dot_general(a, b, (((1,), (1,)), ((), ())), preferred_element_type=F32)


def nn(a, b):
    return jnp.dot(a, b, preferred_element_type=F32)


def tn(a, b):
    return lax.dot_general(a, b, (((0,), (0,)), ((), ())), preferred_element_type=F32)


def iota(shape, dim):
    return lax.broadcasted_iota(jnp.int32, shape, dim)


class Place:
    def __init__(self):
        self.dp = lax.axis_index("dp")
        self.tb = lax.axis_index("table")
        self.me = self.dp * 16 + self.tb
        self.z = self.dp // 2
        self.core = lax.rem(self.dp, 2)
        self.x = self.tb // 4
        self.y = lax.rem(self.tb, 4)

    def along(self, axis, shift):
        z, x, y = self.z, self.x, self.y
        if axis == "z":
            z = lax.rem(z + shift, 4)
        if axis == "x":
            x = lax.rem(x + shift, 4)
        if axis == "y":
            y = lax.rem(y + shift, 4)
        return (z * 2 + self.core, x * 4 + y)

    def sibling(self):
        return (self.z * 2 + 1 - self.core, self.tb)


def announce(place):
    barrier = pltpu.get_barrier_semaphore()

    def greet(k, carry):
        other = lax.rem(place.me + k, DEV)
        pl.semaphore_signal(
            barrier, inc=1, device_id=(other // 16, lax.rem(other, 16)), device_id_type=MESH
        )
        return carry

    lax.fori_loop(1, DEV, greet, 0)
    return barrier


def peers(place, c):
    zs = [lax.rem(place.z + j, 4) * 2 for j in range(4)]
    xs = [lax.rem(place.x + j, 4) * 4 for j in range(4)]
    ys = [lax.rem(place.y + c + j, 4) for j in range(4)]
    cores = [place.core, 1 - place.core]
    return [
        (zs[a] + cores[k], xs[(a + b) % 4] + ys[a])
        for b in range(4)
        for a in range(4)
        for k in range(2)
    ]


def fetch_kernel(
    item_owner_ref,
    neg_owner_ref,
    item_slot_ref,
    neg_slot_ref,
    table_ref,
    update_ref,
    rows_ref,
    ids_ref,
    pos_ref,
    item_owner,
    neg_owner,
    item_slot,
    neg_slot,
    update,
    small_sem,
    table_vmem,
    faded,
    asked,
    stage,
    outbox,
    local_sem,
    id_send,
    id_recv,
    row_send,
    row_recv,
):
    place = Place()
    pairs = (
        (item_owner_ref, item_owner),
        (neg_owner_ref, neg_owner),
        (item_slot_ref, item_slot),
        (neg_slot_ref, neg_slot),
        (update_ref, update),
    )
    loads = [
        pltpu.make_async_copy(src, dst, small_sem.at[n]) for n, (src, dst) in enumerate(pairs)
    ]
    for copy in loads:
        copy.start()
    load = pltpu.make_async_copy(table_ref, table_vmem, local_sem)
    load.start()
    barrier = announce(place)
    for copy in loads:
        copy.wait()
    owner = jnp.concatenate([item_owner[...], neg_owner[...]], 1)
    slot = jnp.concatenate([item_slot[...], neg_slot[...]], 1)
    onehot = (iota((DEV, ALL), 0) == owner).astype(F32)
    upto = (iota((ALL, ALL), 0) <= iota((ALL, ALL), 1)).astype(F32).astype(BF16)
    count = nn(onehot.astype(BF16), upto)
    rank = jnp.sum(onehot * count, 0, keepdims=True).astype(jnp.int32) - 1
    ranked = (iota((DEV, ALL), 0) == rank).astype(F32).astype(BF16)
    high = (onehot * (slot // 64).astype(F32)).astype(BF16)
    low = (onehot * (slot % 64).astype(F32)).astype(BF16)
    asked[...] = (64.0 * nt(high, ranked) + nt(low, ranked)).astype(jnp.int32)
    pos_ref[...] = rank * DEV + owner
    pl.semaphore_wait(barrier, DEV - 1)

    def ask(c, carry):
        for k, (d, t) in enumerate(peers(place, c)):

            def send(d=d, t=t):
                pltpu.make_async_remote_copy(
                    src_ref=asked.at[pl.ds(d * 16 + t, 1)],
                    dst_ref=ids_ref.at[pl.ds(place.me, 1)],
                    send_sem=id_send,
                    recv_sem=id_recv,
                    device_id=(d, t),
                    device_id_type=MESH,
                ).start()

            if k == 0:
                pl.when(c > 0)(send)
            else:
                send()
        return carry

    lax.fori_loop(0, 4, ask, 0)
    ids_ref[pl.ds(place.me, 1), :] = asked[pl.ds(place.me, 1), :]
    fade = jnp.exp((NOW - update[...]).astype(F32) * LOG_RHO)
    fade = jnp.transpose(jnp.concatenate([fade, jnp.zeros((96, 128), F32)], 0))
    load.wait()
    for c in range(32):
        block = table_vmem[c * 128 : (c + 1) * 128, :].astype(F32) * fade[:, c : c + 1]
        faded[c * 128 : (c + 1) * 128, :] = block.astype(BF16)
    most = asked.at[pl.ds(0, DEV - 1)]
    pltpu.make_async_copy(most, most, id_send).wait()
    pltpu.make_async_copy(most, most, id_recv).wait()

    def serve(c, carry):
        group = peers(place, c)
        wanted = jnp.concatenate([ids_ref[pl.ds(d * 16 + t, 1), :] for d, t in group], 0)
        chosen = [
            (iota((32, ROWS), 1) == wanted[:, r : r + 1]).astype(F32).astype(BF16)
            for r in range(CAP)
        ]
        found = nn(jnp.concatenate(chosen, 0), faded[...])
        for r in range(CAP):
            for b in range(4):
                stage[pl.ds(4 * r + b, 32, stride=MSG), :] = found[
                    r * 32 : (r + 1) * 32, b * 128 : (b + 1) * 128
                ]
        base = c * 32
        outbox[pl.ds(base, 32)] = stage[...].astype(BF16).reshape(32, MSG, 128)
        for k, (d, t) in enumerate(group):

            def send(k=k, d=d, t=t):
                pltpu.make_async_remote_copy(
                    src_ref=outbox.at[base + k],
                    dst_ref=rows_ref.at[place.me],
                    send_sem=row_send,
                    recv_sem=row_recv,
                    device_id=(d, t),
                    device_id_type=MESH,
                ).start()

            if k == 0:
                pl.when(c > 0)(send)
            else:
                send()
        return carry

    for r in range(CAP * 4, MSG):
        stage[pl.ds(r, 32, stride=MSG), :] = jnp.zeros((32, 128), F32)
    lax.fori_loop(0, 4, serve, 0)
    rows_ref[place.me] = outbox[0]
    most = outbox.at[pl.ds(0, DEV - 1)]
    pltpu.make_async_copy(most, most, row_send).wait()
    pltpu.make_async_copy(most, most, row_recv).wait()


def fetch(item_owner, neg_owner, item_slot, neg_slot, table, update):
    return pl.pallas_call(
        fetch_kernel,
        out_shape=(
            jax.ShapeDtypeStruct((DEV, MSG, 128), BF16),
            jax.ShapeDtypeStruct((DEV, 128), jnp.int32),
            jax.ShapeDtypeStruct((1, ALL), jnp.int32),
        ),
        in_specs=[ANY] * 6,
        out_specs=(VMEM, VMEM, VMEM),
        scratch_shapes=[
            pltpu.VMEM((1, TOK), jnp.int32),
            pltpu.VMEM((1, NEG), jnp.int32),
            pltpu.VMEM((1, TOK), jnp.int32),
            pltpu.VMEM((1, NEG), jnp.int32),
            pltpu.VMEM((ROWS // 128, 128), jnp.int32),
            pltpu.SemaphoreType.DMA((5,)),
            pltpu.VMEM((ROWS, D), BF16),
            pltpu.VMEM((ROWS, D), BF16),
            pltpu.VMEM((DEV, 128), jnp.int32),
            pltpu.VMEM((32 * MSG, 128), F32),
            pltpu.VMEM((DEV, MSG, 128), BF16),
            pltpu.SemaphoreType.DMA,
            pltpu.SemaphoreType.DMA,
            pltpu.SemaphoreType.DMA,
            pltpu.SemaphoreType.DMA,
            pltpu.SemaphoreType.DMA,
        ],
        compiler_params=pltpu.CompilerParams(
            collective_id=0, has_side_effects=True, vmem_limit_bytes=50 << 20
        ),
        name="fetch",
    )(
        item_owner.reshape(1, TOK),
        neg_owner.reshape(1, NEG),
        item_slot.reshape(1, TOK),
        neg_slot.reshape(1, NEG),
        table,
        update,
    )


def scatter_kernel(
    arrived_ref,
    ids_ref,
    update_ref,
    total_ref,
    out_ref,
    grad_in_ref,
    grad_out_ref,
    wide,
    rows,
    slots,
):
    step = pl.program_id(0)
    grad_out_ref[...] = total_ref[:, :D].astype(F32)
    grad_in_ref[...] = total_ref[:, D:].astype(F32)

    @pl.when(step == 0)
    def _():
        for s in range(8):
            block = arrived_ref[s * 16 : (s + 1) * 16].astype(F32)
            wide[s * 16 * MSG : (s + 1) * 16 * MSG, :] = block.reshape(16 * MSG, 128)
        for c in range(CAP):
            for b in range(4):
                piece = wide[pl.ds(4 * c + b, DEV, stride=MSG), :]
                rows[c * 128 : (c + 1) * 128, b * 128 : (b + 1) * 128] = piece.astype(BF16)
        slots[...] = jnp.transpose(ids_ref[...])[:16, :]

    fade = jnp.exp((NOW - update_ref[...]).astype(F32) * LOG_RHO)
    fade = jnp.transpose(jnp.concatenate([fade, jnp.zeros((120, 128), F32)], 0))
    for s in range(8):
        first = step * 1024 + s * 128
        chosen = [
            (iota((128, 128), 0) + first == slots[c : c + 1, :]).astype(F32).astype(BF16)
            for c in range(CAP)
        ]
        summed = nn(jnp.concatenate(chosen, 1), rows[...])
        out_ref[s * 128 : (s + 1) * 128, :] = summed * fade[:, s : s + 1]


def scatter(arrived, ids, update, total):
    return pl.pallas_call(
        scatter_kernel,
        grid=(4,),
        out_shape=(
            jax.ShapeDtypeStruct((ROWS, D), F32),
            jax.ShapeDtypeStruct((D, 4 * D), F32),
            jax.ShapeDtypeStruct((D, D), F32),
        ),
        in_specs=[
            pl.BlockSpec((DEV, MSG, 128), lambda i: (0, 0, 0)),
            pl.BlockSpec((DEV, 128), lambda i: (0, 0)),
            pl.BlockSpec((8, 128), lambda i: (i, 0)),
            pl.BlockSpec((128, WIDE), lambda i: (i, 0)),
        ],
        out_specs=(
            pl.BlockSpec((1024, D), lambda i: (i, 0)),
            pl.BlockSpec((128, 4 * D), lambda i: (i, 0)),
            pl.BlockSpec((128, D), lambda i: (i, 0)),
        ),
        scratch_shapes=[
            pltpu.VMEM((DEV * MSG, 128), F32),
            pltpu.VMEM((CAP * 128, D), BF16),
            pltpu.VMEM((16, 128), jnp.int32),
        ],
        compiler_params=pltpu.CompilerParams(vmem_limit_bytes=48 << 20),
        name="scatter",
    )(arrived, ids, update, total)


class Wave:
    AXES = (("x", "y", "z"), ("y", "z", "x"), ("z", "x", "y"))

    def __init__(self, place, number, parts, refs):
        self.place, self.number, self.parts = place, number, parts
        (self.grad, self.total, self.half, self.acc0, self.acc1, self.acc2) = refs[:6]
        (self.in1, self.in2, self.in3) = refs[6:9]
        (self.core_send, self.core_recv, self.step_send, self.step_recv) = refs[9:]
        self.mine = pl.multiple_of(place.core * 256, 256)
        self.other = pl.multiple_of((1 - place.core) * 256, 256)
        self.at = {"x": place.x, "y": place.y, "z": place.z}
        self.first, self.second, self.third, self.fourth, self.fifth = [], [], [], [], []

    def across(self, slot, src, dst):
        copy = pltpu.make_async_remote_copy(
            src_ref=src,
            dst_ref=dst,
            send_sem=self.core_send.at[self.number, slot],
            recv_sem=self.core_recv.at[self.number, slot],
            device_id=self.place.sibling(),
            device_id_type=MESH,
        )
        copy.start()
        return copy

    def send(self, p, step, shift, src, dst):
        copy = pltpu.make_async_remote_copy(
            src_ref=src,
            dst_ref=dst,
            send_sem=self.step_send.at[self.number, p, step, shift - 1],
            recv_sem=self.step_recv.at[self.number, p, step, shift - 1],
            device_id=self.place.along(self.AXES[p][(0, 1, 2, 1, 0)[step]], shift),
            device_id_type=MESH,
        )
        copy.start()
        return copy

    def coordinate(self, p, level):
        return self.at[self.AXES[p][level]]

    def swap(self):
        self.swaps = []
        for p, (start, width) in enumerate(self.parts):
            cols = pl.ds(start, width)
            self.swaps.append(
                self.across(p, self.grad.at[pl.ds(self.other, 256), cols], self.half.at[:, cols])
            )

    def scatter1(self):
        for p, (start, width) in enumerate(self.parts):
            cols = pl.ds(start, width)
            self.swaps[p].wait()
            self.acc0[:, cols] = (
                self.grad[pl.ds(self.mine, 256), cols].astype(F32)
                + self.half[:, cols].astype(F32)
            ).astype(BF16)
            for shift in (1, 2, 3):
                to = pl.multiple_of(lax.rem(self.coordinate(p, 0) + shift, 4) * 64, 64)
                src = self.acc0.at[pl.ds(to, 64), cols]
                self.first.append(self.send(p, 0, shift, src, self.in1.at[shift - 1, :, cols]))

    def scatter2(self):
        for p, (start, width) in enumerate(self.parts):
            cols = pl.ds(start, width)
            for copy in self.first[3 * p : 3 * p + 3]:
                copy.wait()
            own = pl.multiple_of(self.coordinate(p, 0) * 64, 64)
            total = self.acc0[pl.ds(own, 64), cols].astype(F32)
            for k in range(3):
                total += self.in1[k, :, cols].astype(F32)
            self.acc1[:, cols] = total.astype(BF16)
            for shift in (1, 2, 3):
                to = pl.multiple_of(lax.rem(self.coordinate(p, 1) + shift, 4) * 16, 16)
                src = self.acc1.at[pl.ds(to, 16), cols]
                self.second.append(self.send(p, 1, shift, src, self.in2.at[shift - 1, :, cols]))

    def exchange(self):
        for p, (start, width) in enumerate(self.parts):
            cols = pl.ds(start, width)
            for copy in self.second[3 * p : 3 * p + 3]:
                copy.wait()
            own = pl.multiple_of(self.coordinate(p, 1) * 16, 16)
            total = self.acc1[pl.ds(own, 16), cols].astype(F32)
            for k in range(3):
                total += self.in2[k, :, cols].astype(F32)
            self.acc2[:, cols] = total.astype(BF16)
            at = self.coordinate(p, 2)
            self.in3[at, :, cols] = self.acc2[:, cols]
            for shift in (1, 2, 3):
                self.third.append(
                    self.send(p, 2, shift, self.acc2.at[:, cols], self.in3.at[at, :, cols])
                )

    def gather4(self):
        for p, (start, width) in enumerate(self.parts):
            cols = pl.ds(start, width)
            for copy in self.third[3 * p : 3 * p + 3]:
                copy.wait()
            total = self.in3[0, :, cols].astype(F32)
            for k in range(1, 4):
                total += self.in3[k, :, cols].astype(F32)
            wide = pl.multiple_of(self.mine + self.coordinate(p, 0) * 64, 64)
            narrow = pl.multiple_of(wide + self.coordinate(p, 1) * 16, 16)
            self.total[pl.ds(narrow, 16), cols] = total.astype(BF16)
            piece = self.total.at[pl.ds(narrow, 16), cols]
            for shift in (1, 2, 3):
                self.fourth.append(self.send(p, 3, shift, piece, piece))

    def gather5(self):
        for p, (start, width) in enumerate(self.parts):
            for copy in self.fourth[3 * p : 3 * p + 3]:
                copy.wait()
            wide = pl.multiple_of(self.mine + self.coordinate(p, 0) * 64, 64)
            piece = self.total.at[pl.ds(wide, 64), pl.ds(start, width)]
            for shift in (1, 2, 3):
                self.fifth.append(self.send(p, 4, shift, piece, piece))

    def restore(self):
        self.last = []
        for p, (start, width) in enumerate(self.parts):
            for copy in self.fifth[3 * p : 3 * p + 3]:
                copy.wait()
            piece = self.total.at[pl.ds(self.mine, 256), pl.ds(start, width)]
            self.last.append(self.across(3 + p, piece, piece))

    def finish(self):
        for copy in self.last:
            copy.wait()


def layer_kernel(
    lengths,
    rows_ref,
    pos_ref,
    w_in_ref,
    w_out_ref,
    loss_ref,
    arrived_ref,
    total_ref,
    w_in,
    w_out,
    flat,
    held,
    where,
    x32,
    n32,
    nb,
    scale1,
    negatives,
    mixed,
    slope,
    weights,
    bend,
    attended,
    gated,
    d_out,
    d_next,
    d_att,
    d_score,
    d_pre,
    grads,
    box,
    grad,
    half,
    acc0,
    acc1,
    acc2,
    in1,
    in2,
    in3,
    load_sem,
    row_send,
    row_recv,
    core_send,
    core_recv,
    step_send,
    step_recv,
):
    place = Place()
    load_in = pltpu.make_async_copy(w_in_ref, w_in, load_sem.at[0])
    load_out = pltpu.make_async_copy(w_out_ref, w_out, load_sem.at[1])
    load_in.start()
    load_out.start()
    barrier = announce(place)
    refs = (grad, total_ref, half, acc0, acc1, acc2, in1, in2, in3)
    refs += (core_send, core_recv, step_send, step_recv)
    wave_a = Wave(place, 0, ((0, 384), (384, 384), (768, 256)), refs)
    wave_b = Wave(place, 1, ((1024, 512), (1536, 512), (2048, 512)), refs)
    groups = [peers(place, c) for c in range(4)]

    def post(first, last):
        for n in range(first, last):
            d, t = groups[n // 32][n % 32]
            pltpu.make_async_remote_copy(
                src_ref=box.at[d * 16 + t],
                dst_ref=arrived_ref.at[place.me],
                send_sem=row_send,
                recv_sem=row_recv,
                device_id=(d, t),
                device_id_type=MESH,
            ).start()

    for s in range(8):
        block = rows_ref[s * 16 : (s + 1) * 16].astype(F32)
        flat[s * 16 * MSG : (s + 1) * 16 * MSG, :] = block.reshape(16 * MSG, 128)
    for c in range(CAP):
        for b in range(4):
            piece = flat[pl.ds(4 * c + b, DEV, stride=MSG), :]
            held[c * 128 : (c + 1) * 128, b * 128 : (b + 1) * 128] = piece.astype(BF16)
    where[...] = jnp.transpose(jnp.broadcast_to(pos_ref[...], (128, ALL)))

    def take(i):
        at = where[i * 128 : (i + 1) * 128, :]
        chosen = [
            (iota((128, 128), 1) + c * 128 == at).astype(F32).astype(BF16) for c in range(CAP)
        ]
        return nn(jnp.concatenate(chosen, 1), held[...])

    for i in range(4):
        x = take(i)
        span = pl.ds(i * 128, 128)
        x32[span, :] = x
        center = x - jnp.mean(x, -1, keepdims=True)
        scale = lax.rsqrt(jnp.mean(center * center, -1, keepdims=True) + EPS)
        normed = center * scale
        n32[span, :] = normed
        nb[span, :] = normed.astype(BF16)
        scale1[span, :] = scale
    x = take(4)
    x32[pl.ds(512, 128), :] = x
    negatives[...] = x.astype(BF16)

    load_in.wait()

    def project(cb, carry):
        cols = pl.ds(pl.multiple_of(cb * 256, 256), 256)
        pre = nn(nb[...], w_in[:, cols])
        sig = jax.nn.sigmoid(pre)
        mixed[:, cols] = (pre * sig).astype(BF16)
        slope[:, cols] = (sig * (1.0 + pre * (1.0 - sig))).astype(BF16)
        return carry

    lax.fori_loop(0, 8, project, 0)

    end1 = lengths[0, 0]
    end2 = end1 + lengths[0, 1]
    end3 = end2 + lengths[0, 2]

    def lanes(part, h):
        return pl.ds(pl.multiple_of(part * 512 + h * 128, 128), 128)

    def visible(i):
        row = iota((256, 256 * (i + 1)), 0) + 256 * i
        col = iota((256, 256 * (i + 1)), 1)
        start = jnp.where(
            row >= end3, end3, jnp.where(row >= end2, end2, jnp.where(row >= end1, end1, 0))
        )
        return jnp.where((col <= row) & (col >= start), 1.0 / LMAX, 0.0).astype(F32)

    def attend(h, carry):
        for i in range(2):
            span, past = pl.ds(256 * i, 256), pl.ds(0, 256 * (i + 1))
            score = nt(mixed[span, lanes(2, h)], mixed[past, lanes(3, h)])
            sig = jax.nn.sigmoid(score)
            seen = visible(i)
            weight = (score * sig * seen).astype(BF16)
            weights[h, span, past] = weight
            bend[h, span, past] = (sig * (1.0 + score * (1.0 - sig)) * seen).astype(BF16)
            attended[span, lanes(0, h)] = nn(weight, mixed[past, lanes(1, h)])
        return carry

    lax.fori_loop(0, H, attend, 0)

    load_out.wait()
    d_next[pl.ds(0, 8), :] = jnp.zeros((8, D), F32)
    d_negatives = jnp.zeros((NEG, D), F32)
    for i in range(2):
        span = pl.ds(256 * i, 256)
        values = attended[span, :]
        center = values - jnp.mean(values, -1, keepdims=True)
        scale = lax.rsqrt(jnp.mean(center * center, -1, keepdims=True) + EPS)
        normed = center * scale
        gate = mixed[span, 0:512].astype(F32)
        gated_b = (normed * gate).astype(BF16)
        gated[span, :] = gated_b
        out_b = (x32[span, :] + nn(gated_b, w_out[...])).astype(BF16)
        out = out_b.astype(F32)
        following = x32[pl.ds(256 * i + 1, 256), :]
        positive = jnp.sum(out * following, -1, keepdims=True) * TAU
        negative = nt(out_b, negatives[...]) * TAU
        top = jnp.maximum(positive, jnp.max(negative, -1, keepdims=True))
        exp_p = jnp.exp(positive - top)
        exp_n = jnp.exp(negative - top)
        total = exp_p + jnp.sum(exp_n, -1, keepdims=True)
        row = iota((256, 1), 0) + (256 * i + 1)
        valid = (row != end1) & (row != end2) & (row != end3) & (row != TOK)
        valid = jnp.where(valid, 1.0, 0.0).astype(F32)
        loss = (jnp.log(total) + top - positive) * valid
        loss_ref[:, span] = jnp.transpose(jnp.broadcast_to(loss, (256, 128)))[:1, :]
        share = valid / total
        d_pos = (exp_p * share - valid) * TAU
        d_neg = (exp_n * (share * TAU)).astype(BF16)
        d_out_b = (d_pos * following + nn(d_neg, negatives[...])).astype(BF16)
        d_out[span, :] = d_out_b
        d_next[pl.ds(256 * i + 8, 256), :] = d_pos * out
        d_negatives += tn(d_neg, out_b)
        d_gated = nt(d_out_b, w_out[...])
        d_pre[span, 0:512] = (d_gated * normed * slope[span, 0:512].astype(F32)).astype(BF16)
        d_normed = d_gated * gate
        d_values = scale * (
            d_normed
            - jnp.mean(d_normed, -1, keepdims=True)
            - normed * jnp.mean(d_normed * normed, -1, keepdims=True)
        )
        d_att[span, :] = d_values.astype(BF16)
    grads[pl.ds(TOK, NEG), :] = d_negatives.astype(BF16)

    def back(h, carry):
        for i in range(2):
            span, past = pl.ds(256 * i, 256), pl.ds(0, 256 * (i + 1))
            d_weight = nt(d_att[span, lanes(0, h)], mixed[past, lanes(1, h)])
            d_s = (d_weight * bend[h, span, past].astype(F32)).astype(BF16)
            d_score[span, past] = d_s
            d_q = nn(d_s, mixed[past, lanes(3, h)])
            d_pre[span, lanes(2, h)] = (d_q * slope[span, lanes(2, h)].astype(F32)).astype(BF16)
        for i in range(2):
            span, future = pl.ds(256 * i, 256), pl.ds(256 * i, 512 - 256 * i)
            d_v = tn(weights[h, future, span], d_att[future, lanes(0, h)])
            d_pre[span, lanes(1, h)] = (d_v * slope[span, lanes(1, h)].astype(F32)).astype(BF16)
            d_k = tn(d_score[future, span], mixed[future, lanes(2, h)])
            d_pre[span, lanes(3, h)] = (d_k * slope[span, lanes(3, h)].astype(F32)).astype(BF16)
        return carry

    for cb in range(2):
        cols = pl.ds(cb * 256, 256)
        grad[:, cols] = tn(gated[...], d_out[:, cols]).astype(BF16)
    for cb in range(2):
        grad[:, pl.ds(512 + cb * 256, 256)] = tn(nb[...], d_pre[:, pl.ds(cb * 256, 256)]).astype(
            BF16
        )
    pl.semaphore_wait(barrier, DEV - 1)
    wave_a.swap()
    lax.fori_loop(0, 2, back, 0)
    wave_a.scatter1()
    lax.fori_loop(2, 4, back, 0)
    for cb in range(2, 8):
        grad[:, pl.ds(512 + cb * 256, 256)] = tn(nb[...], d_pre[:, pl.ds(cb * 256, 256)]).astype(
            BF16
        )
    wave_b.swap()
    wave_a.scatter2()

    for i in range(2):
        span = pl.ds(256 * i, 256)
        d_normed = nt(d_pre[span, :], w_in[...])
        normed = n32[span, :]
        d_x = scale1[span, :] * (
            d_normed
            - jnp.mean(d_normed, -1, keepdims=True)
            - normed * jnp.mean(d_normed * normed, -1, keepdims=True)
        )
        d_x += d_out[span, :].astype(F32) + d_next[pl.ds(256 * i + 7, 256), :]
        grads[span, :] = d_x.astype(BF16)

    wave_a.exchange()

    for j in range(CAP // 2):
        at = iota((256, ALL), 0) + j * 256
        sent = nn((at == pos_ref[...]).astype(F32).astype(BF16), grads[...])
        for c in range(2):
            for b in range(4):
                flat[pl.ds(4 * (2 * j + c) + b, DEV, stride=MSG), :] = sent[
                    c * 128 : (c + 1) * 128, b * 128 : (b + 1) * 128
                ]
    for s in range(8):
        block = flat[s * 16 * MSG : (s + 1) * 16 * MSG, :].astype(BF16)
        box[s * 16 : (s + 1) * 16] = block.reshape(16, MSG, 128)

    wave_b.scatter1()
    arrived_ref[place.me] = box[place.me]
    post(1, 32)
    wave_a.gather4()
    post(32, 48)
    wave_b.scatter2()
    post(48, 64)
    wave_a.gather5()
    post(64, 96)
    wave_b.exchange()
    post(96, 128)
    wave_b.gather4()
    wave_a.restore()
    wave_b.gather5()
    wave_b.restore()
    wave_a.finish()
    wave_b.finish()
    most = box.at[pl.ds(0, DEV - 1)]
    pltpu.make_async_copy(most, most, row_send).wait()
    pltpu.make_async_copy(most, most, row_recv).wait()


def layer(rows, pos, w_in, w_out, lengths):
    return pl.pallas_call(
        layer_kernel,
        out_shape=(
            jax.ShapeDtypeStruct((1, TOK), F32),
            jax.ShapeDtypeStruct((DEV, MSG, 128), BF16),
            jax.ShapeDtypeStruct((D, WIDE), BF16),
        ),
        in_specs=[pl.BlockSpec(memory_space=pltpu.SMEM), VMEM, VMEM, ANY, ANY],
        out_specs=(VMEM, VMEM, VMEM),
        scratch_shapes=[
            pltpu.VMEM((D, 4 * D), BF16),
            pltpu.VMEM((D, D), BF16),
            pltpu.VMEM((DEV * MSG, 128), F32),
            pltpu.VMEM((CAP * DEV, D), BF16),
            pltpu.VMEM((ALL, 128), jnp.int32),
            pltpu.VMEM((ALL, D), F32),
            pltpu.VMEM((TOK, D), F32),
            pltpu.VMEM((TOK, D), BF16),
            pltpu.VMEM((TOK, 1), F32),
            pltpu.VMEM((NEG, D), BF16),
            pltpu.VMEM((TOK, 4 * D), BF16),
            pltpu.VMEM((TOK, 4 * D), BF16),
            pltpu.VMEM((H, TOK, TOK), BF16),
            pltpu.VMEM((H, TOK, TOK), BF16),
            pltpu.VMEM((TOK, D), F32),
            pltpu.VMEM((TOK, D), BF16),
            pltpu.VMEM((TOK, D), BF16),
            pltpu.VMEM((TOK + 8, D), F32),
            pltpu.VMEM((TOK, D), BF16),
            pltpu.VMEM((TOK, TOK), BF16),
            pltpu.VMEM((TOK, 4 * D), BF16),
            pltpu.VMEM((ALL, D), BF16),
            pltpu.VMEM((DEV, MSG, 128), BF16),
            pltpu.VMEM((D, WIDE), BF16),
            pltpu.VMEM((256, WIDE), BF16),
            pltpu.VMEM((256, WIDE), BF16),
            pltpu.VMEM((64, WIDE), BF16),
            pltpu.VMEM((16, WIDE), BF16),
            pltpu.VMEM((3, 64, WIDE), BF16),
            pltpu.VMEM((3, 16, WIDE), BF16),
            pltpu.VMEM((4, 16, WIDE), BF16),
            pltpu.SemaphoreType.DMA((2,)),
            pltpu.SemaphoreType.DMA,
            pltpu.SemaphoreType.DMA,
            pltpu.SemaphoreType.DMA((2, 6)),
            pltpu.SemaphoreType.DMA((2, 6)),
            pltpu.SemaphoreType.DMA((2, 3, 5, 3)),
            pltpu.SemaphoreType.DMA((2, 3, 5, 3)),
        ],
        compiler_params=pltpu.CompilerParams(
            collective_id=1, has_side_effects=True, vmem_limit_bytes=58 << 20
        ),
        name="layer",
    )(lengths, rows, pos, w_in, w_out)


def on_device(
    table, last_update, item_owner, item_slot, neg_owner, neg_slot, seq_lengths, w_in, w_out
):
    update = last_update.reshape(ROWS // 128, 128)
    rows, ids, pos = fetch(item_owner, neg_owner, item_slot, neg_slot, table, update)
    losses, arrived, total = layer(rows, pos, w_in, w_out, seq_lengths)
    table_grad, grad_in, grad_out = scatter(arrived, ids, update, total)
    return (losses.reshape(TOK), table_grad, grad_in, grad_out)


def solution(mesh):
    placed = (
        P(("dp", "table"), None),
        P(("dp", "table")),
        P(("dp", "table"), None),
        P(("dp", "table")),
        P(("dp", "table"), None),
        P(("dp", "table")),
        P(("dp", "table"), None),
        P(),
        P(),
    )
    return jax.shard_map(
        on_device,
        mesh=mesh,
        in_specs=placed,
        out_specs=(P(("dp", "table")), P(("dp", "table"), None), P(), P()),
        check_vma=False,
    )
```

```python
import functools

import jax
import jax.numpy as jnp
from jax import lax
from jax.experimental import pallas as pl
from jax.experimental.pallas import tpu as pltpu
from jax.sharding import PartitionSpec as P

D = 512
H = 4
DH = 128
TOK = 512
NEG = 128
ALL = TOK + NEG
DEV = 128
CAP_T = 8
CAP_N = 2
CAP = CAP_T + CAP_N
MSG_T = 32
MSG_N = 16
LMAX = 256
NOW = 64
ROWS = 4096
WIDE = 5 * D
LOG_RHO = -0.030459207484708574
TAU = 0.125
EPS = 1e-05
MESH = pl.DeviceIdType.MESH
VMEM = pl.BlockSpec(memory_space=pltpu.VMEM)
HBM = pl.BlockSpec(memory_space=pltpu.HBM)
F32 = jnp.float32
BF16 = jnp.bfloat16


def nt(a, b):
    return lax.dot_general(a, b, (((1,), (1,)), ((), ())), preferred_element_type=F32)


def nn(a, b):
    return jnp.dot(a, b, preferred_element_type=F32)


def tn(a, b):
    return lax.dot_general(a, b, (((0,), (0,)), ((), ())), preferred_element_type=F32)


def iota(shape, dim):
    return lax.broadcasted_iota(jnp.int32, shape, dim)


class Place:
    def __init__(self):
        self.dp = lax.axis_index("dp")
        self.tb = lax.axis_index("table")
        self.me = self.dp * 16 + self.tb
        self.z = self.dp // 2
        self.core = lax.rem(self.dp, 2)
        self.x = self.tb // 4
        self.y = lax.rem(self.tb, 4)

    def along(self, axis, shift):
        z, x, y = self.z, self.x, self.y
        if axis == "z":
            z = lax.rem(z + shift, 4)
        if axis == "x":
            x = lax.rem(x + shift, 4)
        if axis == "y":
            y = lax.rem(y + shift, 4)
        return (z * 2 + self.core, x * 4 + y)

    def sibling(self):
        return (self.z * 2 + 1 - self.core, self.tb)


def announce(place):
    barrier = pltpu.get_barrier_semaphore()

    def greet(k, carry):
        other = lax.rem(place.me + k, DEV)
        pl.semaphore_signal(
            barrier, inc=1, device_id=(other // 16, lax.rem(other, 16)), device_id_type=MESH
        )
        return carry

    lax.fori_loop(1, DEV, greet, 0)
    return barrier


def peers(place, c):
    zs = [lax.rem(place.z + j, 4) * 2 for j in range(4)]
    xs = [lax.rem(place.x + j, 4) * 4 for j in range(4)]
    ys = [lax.rem(place.y + c + j, 4) for j in range(4)]
    cores = [place.core, 1 - place.core]
    return [
        (zs[a] + cores[k], xs[(a + b) % 4] + ys[a])
        for b in range(4)
        for a in range(4)
        for k in range(2)
    ]


class Wave:
    AXES = (("x", "y", "z"), ("y", "z", "x"), ("z", "x", "y"))

    def __init__(self, place, number, parts, refs):
        self.place, self.number, self.parts = place, number, parts
        (self.grad, self.total, self.half, self.acc0, self.acc1, self.acc2) = refs[:6]
        (self.in1, self.in2, self.in3) = refs[6:9]
        (self.core_send, self.core_recv, self.step_send, self.step_recv) = refs[9:]
        self.mine = pl.multiple_of(place.core * 256, 256)
        self.other = pl.multiple_of((1 - place.core) * 256, 256)
        self.at = {"x": place.x, "y": place.y, "z": place.z}
        self.first, self.second, self.third, self.fourth, self.fifth = [], [], [], [], []

    def across(self, slot, src, dst):
        copy = pltpu.make_async_remote_copy(
            src_ref=src,
            dst_ref=dst,
            send_sem=self.core_send.at[self.number, slot],
            recv_sem=self.core_recv.at[self.number, slot],
            device_id=self.place.sibling(),
            device_id_type=MESH,
        )
        copy.start()
        return copy

    def send(self, p, step, shift, src, dst):
        copy = pltpu.make_async_remote_copy(
            src_ref=src,
            dst_ref=dst,
            send_sem=self.step_send.at[self.number, p, step, shift - 1],
            recv_sem=self.step_recv.at[self.number, p, step, shift - 1],
            device_id=self.place.along(self.AXES[p][(0, 1, 2, 1, 0)[step]], shift),
            device_id_type=MESH,
        )
        copy.start()
        return copy

    def coordinate(self, p, level):
        return self.at[self.AXES[p][level]]

    def swap(self):
        self.swaps = []
        for p, (start, width) in enumerate(self.parts):
            cols = pl.ds(start, width)
            self.swaps.append(
                self.across(p, self.grad.at[pl.ds(self.other, 256), cols], self.half.at[:, cols])
            )

    def scatter1(self):
        for p, (start, width) in enumerate(self.parts):
            cols = pl.ds(start, width)
            self.swaps[p].wait()
            self.acc0[:, cols] = (
                self.grad[pl.ds(self.mine, 256), cols].astype(F32)
                + self.half[:, cols].astype(F32)
            ).astype(BF16)
            for shift in (1, 2, 3):
                to = pl.multiple_of(lax.rem(self.coordinate(p, 0) + shift, 4) * 64, 64)
                src = self.acc0.at[pl.ds(to, 64), cols]
                self.first.append(self.send(p, 0, shift, src, self.in1.at[shift - 1, :, cols]))

    def scatter2(self):
        for p, (start, width) in enumerate(self.parts):
            cols = pl.ds(start, width)
            for copy in self.first[3 * p : 3 * p + 3]:
                copy.wait()
            own = pl.multiple_of(self.coordinate(p, 0) * 64, 64)
            total = self.acc0[pl.ds(own, 64), cols].astype(F32)
            for k in range(3):
                total += self.in1[k, :, cols].astype(F32)
            self.acc1[:, cols] = total.astype(BF16)
            for shift in (1, 2, 3):
                to = pl.multiple_of(lax.rem(self.coordinate(p, 1) + shift, 4) * 16, 16)
                src = self.acc1.at[pl.ds(to, 16), cols]
                self.second.append(self.send(p, 1, shift, src, self.in2.at[shift - 1, :, cols]))

    def exchange(self):
        for p, (start, width) in enumerate(self.parts):
            cols = pl.ds(start, width)
            for copy in self.second[3 * p : 3 * p + 3]:
                copy.wait()
            own = pl.multiple_of(self.coordinate(p, 1) * 16, 16)
            total = self.acc1[pl.ds(own, 16), cols].astype(F32)
            for k in range(3):
                total += self.in2[k, :, cols].astype(F32)
            self.acc2[:, cols] = total.astype(BF16)
            at = self.coordinate(p, 2)
            self.in3[at, :, cols] = self.acc2[:, cols]
            for shift in (1, 2, 3):
                self.third.append(
                    self.send(p, 2, shift, self.acc2.at[:, cols], self.in3.at[at, :, cols])
                )

    def gather4(self):
        for p, (start, width) in enumerate(self.parts):
            cols = pl.ds(start, width)
            for copy in self.third[3 * p : 3 * p + 3]:
                copy.wait()
            total = self.in3[0, :, cols].astype(F32)
            for k in range(1, 4):
                total += self.in3[k, :, cols].astype(F32)
            wide = pl.multiple_of(self.mine + self.coordinate(p, 0) * 64, 64)
            narrow = pl.multiple_of(wide + self.coordinate(p, 1) * 16, 16)
            self.total[pl.ds(narrow, 16), cols] = total.astype(BF16)
            piece = self.total.at[pl.ds(narrow, 16), cols]
            for shift in (1, 2, 3):
                self.fourth.append(self.send(p, 3, shift, piece, piece))

    def gather5(self):
        for p, (start, width) in enumerate(self.parts):
            for copy in self.fourth[3 * p : 3 * p + 3]:
                copy.wait()
            wide = pl.multiple_of(self.mine + self.coordinate(p, 0) * 64, 64)
            piece = self.total.at[pl.ds(wide, 64), pl.ds(start, width)]
            for shift in (1, 2, 3):
                self.fifth.append(self.send(p, 4, shift, piece, piece))

    def restore(self):
        self.last = []
        for p, (start, width) in enumerate(self.parts):
            for copy in self.fifth[3 * p : 3 * p + 3]:
                copy.wait()
            piece = self.total.at[pl.ds(self.mine, 256), pl.ds(start, width)]
            self.last.append(self.across(3 + p, piece, piece))

    def finish(self):
        for copy in self.last:
            copy.wait()


def step_kernel(
    lengths,
    item_owner_ref,
    neg_owner_ref,
    item_slot_ref,
    neg_slot_ref,
    table_ref,
    update_ref,
    w_in_ref,
    w_out_ref,
    loss_ref,
    arrived_t,
    arrived_n,
    ids_ref,
    total_ref,
    item_owner,
    neg_owner,
    item_slot,
    neg_slot,
    update,
    table,
    w_in,
    w_out,
    asked,
    outbox_t,
    outbox_n,
    rows_t,
    rows_n,
    flat_t,
    flat_n,
    held,
    x32,
    n32,
    nb,
    scale1,
    negatives,
    mixed,
    slope,
    weights,
    bend,
    attended,
    gated,
    d_out,
    d_next,
    d_att,
    d_score,
    d_pre,
    grads,
    box_t,
    box_n,
    grad,
    half,
    acc0,
    acc1,
    acc2,
    in1,
    in2,
    in3,
    load_sem,
    id_sem,
    out_sem_t,
    out_sem_n,
    back_sem_t,
    back_sem_n,
    core_send,
    core_recv,
    step_send,
    step_recv,
):
    place = Place()
    pairs = (
        (item_owner_ref, item_owner),
        (neg_owner_ref, neg_owner),
        (item_slot_ref, item_slot),
        (neg_slot_ref, neg_slot),
        (update_ref, update),
        (table_ref, table),
        (w_in_ref, w_in),
        (w_out_ref, w_out),
    )
    loads = [pltpu.make_async_copy(src, dst, load_sem.at[n]) for n, (src, dst) in enumerate(pairs)]
    for copy in loads:
        copy.start()
    barrier = announce(place)
    for copy in loads[:5]:
        copy.wait()

    owner = jnp.concatenate([item_owner[...], neg_owner[...]], 1)
    slot = jnp.concatenate([item_slot[...], neg_slot[...]], 1)
    onehot = (iota((DEV, ALL), 0) == owner).astype(F32)
    before, after = iota((ALL, ALL), 0), iota((ALL, ALL), 1)
    upto = (before <= after) & ((before >= TOK) | (after < TOK))
    count = nn(onehot.astype(BF16), upto.astype(F32).astype(BF16))
    rank = jnp.sum(onehot * count, 0, keepdims=True).astype(jnp.int32) - 1
    rank = rank + jnp.where(iota((1, ALL), 1) >= TOK, CAP_T, 0)
    ranked = (iota((DEV, ALL), 0) == rank).astype(F32).astype(BF16)
    high = (onehot * (slot // 64).astype(F32)).astype(BF16)
    low = (onehot * (slot % 64).astype(F32)).astype(BF16)
    asked[...] = (64.0 * nt(high, ranked) + nt(low, ranked)).astype(jnp.int32)
    pos = rank * DEV + owner
    pl.semaphore_wait(barrier, DEV - 1)

    def each(c, send):
        for k, (d, t) in enumerate(peers(place, c)):
            if k == 0:
                pl.when(c > 0)(functools.partial(send, k, d, t))
            else:
                send(k, d, t)

    def drain(like, sems):
        most = like.at[pl.ds(0, DEV - 1)]
        pltpu.make_async_copy(most, most, sems.at[0]).wait()
        pltpu.make_async_copy(most, most, sems.at[1]).wait()

    def ask(c, carry):
        def send(k, d, t):
            pltpu.make_async_remote_copy(
                src_ref=asked.at[pl.ds(d * 16 + t, 1)],
                dst_ref=ids_ref.at[pl.ds(place.me, 1)],
                send_sem=id_sem.at[0],
                recv_sem=id_sem.at[1],
                device_id=(d, t),
                device_id_type=MESH,
            ).start()

        each(c, send)
        return carry

    lax.fori_loop(0, 4, ask, 0)
    ids_ref[pl.ds(place.me, 1), :] = asked[pl.ds(place.me, 1), :]
    fade = jnp.exp((NOW - update[...]).astype(F32) * LOG_RHO)
    fade = jnp.transpose(jnp.concatenate([fade, jnp.zeros((96, 128), F32)], 0))
    loads[5].wait()
    for c in range(32):
        block = table[c * 128 : (c + 1) * 128, :].astype(F32) * fade[:, c : c + 1]
        table[c * 128 : (c + 1) * 128, :] = block.astype(BF16)
    drain(asked, id_sem)

    def find(wanted, ranks):
        count = wanted.shape[0]
        chosen = [
            (iota((count, ROWS), 1) == wanted[:, r : r + 1]).astype(F32).astype(BF16)
            for r in ranks
        ]
        return nn(jnp.concatenate(chosen, 0), table[...])

    def asked_by(c):
        return [ids_ref[pl.ds(d * 16 + t, 1), :] for d, t in peers(place, c)]

    def serve(c, carry):
        found = find(jnp.concatenate(asked_by(c), 0), range(CAP_T))
        for r in range(CAP_T):
            for b in range(4):
                flat_t[pl.ds(4 * r + b, 32, stride=MSG_T), :] = found[
                    r * 32 : (r + 1) * 32, b * 128 : (b + 1) * 128
                ]
        base = c * 32
        packed = flat_t[pl.ds(0, 32 * MSG_T), :].astype(BF16)
        outbox_t[pl.ds(base, 32)] = packed.reshape(32, MSG_T, 128)

        def send(k, d, t):
            pltpu.make_async_remote_copy(
                src_ref=outbox_t.at[base + k],
                dst_ref=rows_t.at[place.me],
                send_sem=out_sem_t.at[0],
                recv_sem=out_sem_t.at[1],
                device_id=(d, t),
                device_id_type=MESH,
            ).start()

        each(c, send)
        return carry

    lax.fori_loop(0, 4, serve, 0)
    rows_t[place.me] = outbox_t[0]
    wanted = jnp.concatenate([row for c in range(4) for row in asked_by(c)], 0)
    flat_n[...] = jnp.zeros((DEV * MSG_N, 128), F32)
    for r in range(CAP_N):
        found = find(wanted, (CAP_T + r,))
        for b in range(4):
            flat_n[pl.ds(4 * r + b, DEV, stride=MSG_N), :] = found[:, b * 128 : (b + 1) * 128]
    outbox_n[...] = flat_n[...].astype(BF16).reshape(DEV, MSG_N, 128)

    def serve_n(c, carry):
        base = c * 32

        def send(k, d, t):
            pltpu.make_async_remote_copy(
                src_ref=outbox_n.at[base + k],
                dst_ref=rows_n.at[place.me],
                send_sem=out_sem_n.at[0],
                recv_sem=out_sem_n.at[1],
                device_id=(d, t),
                device_id_type=MESH,
            ).start()

        each(c, send)
        return carry

    lax.fori_loop(0, 4, serve_n, 0)
    rows_n[place.me] = outbox_n[0]

    where = jnp.transpose(jnp.broadcast_to(pos, (128, ALL)))
    drain(outbox_t, out_sem_t)

    def unpack(rows, flat, msg):
        for s in range(8):
            block = rows[s * 16 : (s + 1) * 16].astype(F32)
            flat[s * 16 * msg : (s + 1) * 16 * msg, :] = block.reshape(16 * msg, 128)

    def hold(flat, first, count, msg):
        for c in range(count):
            for b in range(4):
                piece = flat[pl.ds(4 * c + b, DEV, stride=msg), :]
                at = (first + c) * 128
                held[at : at + 128, b * 128 : (b + 1) * 128] = piece.astype(BF16)

    def take(i, first, count):
        at = where[i * 128 : (i + 1) * 128, :]
        chosen = [
            (iota((128, 128), 1) + c * 128 == at).astype(F32).astype(BF16)
            for c in range(first, first + count)
        ]
        return nn(jnp.concatenate(chosen, 1), held[first * 128 : (first + count) * 128, :])

    unpack(rows_t, flat_t, MSG_T)
    hold(flat_t, 0, CAP_T, MSG_T)
    for i in range(4):
        x = take(i, 0, CAP_T)
        span = pl.ds(i * 128, 128)
        x32[span, :] = x
        center = x - jnp.mean(x, -1, keepdims=True)
        scale = lax.rsqrt(jnp.mean(center * center, -1, keepdims=True) + EPS)
        normed = center * scale
        n32[span, :] = normed
        nb[span, :] = normed.astype(BF16)
        scale1[span, :] = scale

    loads[6].wait()

    def project(cb, carry):
        cols = pl.ds(pl.multiple_of(cb * 256, 256), 256)
        pre = nn(nb[...], w_in[:, cols])
        sig = jax.nn.sigmoid(pre)
        mixed[:, cols] = (pre * sig).astype(BF16)
        slope[:, cols] = (sig * (1.0 + pre * (1.0 - sig))).astype(BF16)
        return carry

    lax.fori_loop(0, 8, project, 0)

    end1 = lengths[0, 0]
    end2 = end1 + lengths[0, 1]
    end3 = end2 + lengths[0, 2]

    def lanes(part, h):
        return pl.ds(pl.multiple_of(part * 512 + h * 128, 128), 128)

    def visible(i):
        row = iota((256, 256 * (i + 1)), 0) + 256 * i
        col = iota((256, 256 * (i + 1)), 1)
        start = jnp.where(
            row >= end3, end3, jnp.where(row >= end2, end2, jnp.where(row >= end1, end1, 0))
        )
        return jnp.where((col <= row) & (col >= start), 1.0 / LMAX, 0.0).astype(F32)

    def attend(h, carry):
        for i in range(2):
            span, past = pl.ds(256 * i, 256), pl.ds(0, 256 * (i + 1))
            score = nt(mixed[span, lanes(2, h)], mixed[past, lanes(3, h)])
            sig = jax.nn.sigmoid(score)
            seen = visible(i)
            weight = (score * sig * seen).astype(BF16)
            weights[h, span, past] = weight
            bend[h, span, past] = (sig * (1.0 + score * (1.0 - sig)) * seen).astype(BF16)
            attended[span, lanes(0, h)] = nn(weight, mixed[past, lanes(1, h)])
        return carry

    lax.fori_loop(0, H, attend, 0)

    loads[7].wait()
    drain(outbox_n, out_sem_n)
    unpack(rows_n, flat_n, MSG_N)
    hold(flat_n, CAP_T, CAP_N, MSG_N)
    x = take(4, CAP_T, CAP_N)
    x32[pl.ds(512, 128), :] = x
    negatives[...] = x.astype(BF16)
    d_next[pl.ds(0, 8), :] = jnp.zeros((8, D), F32)
    d_negatives = jnp.zeros((NEG, D), F32)
    for i in range(2):
        span = pl.ds(256 * i, 256)
        values = attended[span, :]
        center = values - jnp.mean(values, -1, keepdims=True)
        scale = lax.rsqrt(jnp.mean(center * center, -1, keepdims=True) + EPS)
        normed = center * scale
        gate = mixed[span, 0:512].astype(F32)
        gated_b = (normed * gate).astype(BF16)
        gated[span, :] = gated_b
        out_b = (x32[span, :] + nn(gated_b, w_out[...])).astype(BF16)
        out = out_b.astype(F32)
        following = x32[pl.ds(256 * i + 1, 256), :]
        positive = jnp.sum(out * following, -1, keepdims=True) * TAU
        negative = nt(out_b, negatives[...]) * TAU
        top = jnp.maximum(positive, jnp.max(negative, -1, keepdims=True))
        exp_p = jnp.exp(positive - top)
        exp_n = jnp.exp(negative - top)
        total = exp_p + jnp.sum(exp_n, -1, keepdims=True)
        row = iota((256, 1), 0) + (256 * i + 1)
        valid = (row != end1) & (row != end2) & (row != end3) & (row != TOK)
        valid = jnp.where(valid, 1.0, 0.0).astype(F32)
        loss = (jnp.log(total) + top - positive) * valid
        loss_ref[:, span] = jnp.transpose(jnp.broadcast_to(loss, (256, 128)))[:1, :]
        share = valid / total
        d_pos = (exp_p * share - valid) * TAU
        d_neg = (exp_n * (share * TAU)).astype(BF16)
        d_out_b = (d_pos * following + nn(d_neg, negatives[...])).astype(BF16)
        d_out[span, :] = d_out_b
        d_next[pl.ds(256 * i + 8, 256), :] = d_pos * out
        d_negatives += tn(d_neg, out_b)
        d_gated = nt(d_out_b, w_out[...])
        d_pre[span, 0:512] = (d_gated * normed * slope[span, 0:512].astype(F32)).astype(BF16)
        d_normed = d_gated * gate
        d_values = scale * (
            d_normed
            - jnp.mean(d_normed, -1, keepdims=True)
            - normed * jnp.mean(d_normed * normed, -1, keepdims=True)
        )
        d_att[span, :] = d_values.astype(BF16)
    mine = pos[:, TOK:]
    d_negatives = d_negatives.astype(BF16)
    for c in range(CAP_N):
        at = iota((DEV, NEG), 0) + (CAP_T + c) * DEV
        sent = nn((at == mine).astype(F32).astype(BF16), d_negatives)
        for b in range(4):
            flat_n[pl.ds(4 * c + b, DEV, stride=MSG_N), :] = sent[:, b * 128 : (b + 1) * 128]
    box_n[...] = flat_n[...].astype(BF16).reshape(DEV, MSG_N, 128)
    arrived_n[place.me] = box_n[place.me]

    def post_n(c, carry):
        def send(k, d, t):
            pltpu.make_async_remote_copy(
                src_ref=box_n.at[d * 16 + t],
                dst_ref=arrived_n.at[place.me],
                send_sem=back_sem_n.at[0],
                recv_sem=back_sem_n.at[1],
                device_id=(d, t),
                device_id_type=MESH,
            ).start()

        each(c, send)
        return carry

    lax.fori_loop(0, 4, post_n, 0)

    def back(h, carry):
        for i in range(2):
            span, past = pl.ds(256 * i, 256), pl.ds(0, 256 * (i + 1))
            d_weight = nt(d_att[span, lanes(0, h)], mixed[past, lanes(1, h)])
            d_s = (d_weight * bend[h, span, past].astype(F32)).astype(BF16)
            d_score[span, past] = d_s
            d_q = nn(d_s, mixed[past, lanes(3, h)])
            d_pre[span, lanes(2, h)] = (d_q * slope[span, lanes(2, h)].astype(F32)).astype(BF16)
        for i in range(2):
            span, future = pl.ds(256 * i, 256), pl.ds(256 * i, 512 - 256 * i)
            d_v = tn(weights[h, future, span], d_att[future, lanes(0, h)])
            d_pre[span, lanes(1, h)] = (d_v * slope[span, lanes(1, h)].astype(F32)).astype(BF16)
            d_k = tn(d_score[future, span], mixed[future, lanes(2, h)])
            d_pre[span, lanes(3, h)] = (d_k * slope[span, lanes(3, h)].astype(F32)).astype(BF16)
        return carry

    refs = (grad, total_ref, half, acc0, acc1, acc2, in1, in2, in3)
    refs += (core_send, core_recv, step_send, step_recv)
    wave_a = Wave(place, 0, ((0, 384), (384, 384), (768, 256)), refs)
    wave_b = Wave(place, 1, ((1024, 512), (1536, 512), (2048, 512)), refs)
    groups = [peers(place, c) for c in range(4)]

    def post(first, last):
        for n in range(first, last):
            d, t = groups[n // 32][n % 32]
            pltpu.make_async_remote_copy(
                src_ref=box_t.at[d * 16 + t],
                dst_ref=arrived_t.at[place.me],
                send_sem=back_sem_t.at[0],
                recv_sem=back_sem_t.at[1],
                device_id=(d, t),
                device_id_type=MESH,
            ).start()

    for cb in range(2):
        cols = pl.ds(cb * 256, 256)
        grad[:, cols] = tn(gated[...], d_out[:, cols]).astype(BF16)
    for cb in range(2):
        grad[:, pl.ds(512 + cb * 256, 256)] = tn(nb[...], d_pre[:, pl.ds(cb * 256, 256)]).astype(
            BF16
        )
    wave_a.swap()
    lax.fori_loop(0, 2, back, 0)
    wave_a.scatter1()
    lax.fori_loop(2, 4, back, 0)
    for cb in range(2, 8):
        grad[:, pl.ds(512 + cb * 256, 256)] = tn(nb[...], d_pre[:, pl.ds(cb * 256, 256)]).astype(
            BF16
        )
    wave_b.swap()
    wave_a.scatter2()

    for i in range(2):
        span = pl.ds(256 * i, 256)
        d_normed = nt(d_pre[span, :], w_in[...])
        normed = n32[span, :]
        d_x = scale1[span, :] * (
            d_normed
            - jnp.mean(d_normed, -1, keepdims=True)
            - normed * jnp.mean(d_normed * normed, -1, keepdims=True)
        )
        d_x += d_out[span, :].astype(F32) + d_next[pl.ds(256 * i + 7, 256), :]
        grads[span, :] = d_x.astype(BF16)

    wave_a.exchange()

    for j in range(CAP_T // 2):
        at = iota((256, TOK), 0) + j * 256
        sent = nn((at == pos[:, :TOK]).astype(F32).astype(BF16), grads[...])
        for c in range(2):
            for b in range(4):
                flat_t[pl.ds(4 * (2 * j + c) + b, DEV, stride=MSG_T), :] = sent[
                    c * 128 : (c + 1) * 128, b * 128 : (b + 1) * 128
                ]
    for s in range(8):
        block = flat_t[s * 16 * MSG_T : (s + 1) * 16 * MSG_T, :].astype(BF16)
        box_t[s * 16 : (s + 1) * 16] = block.reshape(16, MSG_T, 128)

    wave_b.scatter1()
    arrived_t[place.me] = box_t[place.me]
    post(1, 32)
    wave_a.gather4()
    post(32, 48)
    wave_b.scatter2()
    post(48, 64)
    wave_a.gather5()
    post(64, 96)
    wave_b.exchange()
    post(96, 128)
    wave_b.gather4()
    wave_a.restore()
    wave_b.gather5()
    wave_b.restore()
    wave_a.finish()
    wave_b.finish()
    drain(box_n, back_sem_n)
    drain(box_t, back_sem_t)


def step(lengths, item_owner, neg_owner, item_slot, neg_slot, table, update, w_in, w_out):
    return pl.pallas_call(
        step_kernel,
        out_shape=(
            jax.ShapeDtypeStruct((1, TOK), F32),
            jax.ShapeDtypeStruct((DEV, MSG_T, 128), BF16),
            jax.ShapeDtypeStruct((DEV, MSG_N, 128), BF16),
            jax.ShapeDtypeStruct((DEV, 128), jnp.int32),
            jax.ShapeDtypeStruct((D, WIDE), BF16),
        ),
        in_specs=[pl.BlockSpec(memory_space=pltpu.SMEM)] + [HBM] * 8,
        out_specs=(VMEM,) * 5,
        scratch_shapes=[
            pltpu.VMEM((1, TOK), jnp.int32),
            pltpu.VMEM((1, NEG), jnp.int32),
            pltpu.VMEM((1, TOK), jnp.int32),
            pltpu.VMEM((1, NEG), jnp.int32),
            pltpu.VMEM((ROWS // 128, 128), jnp.int32),
            pltpu.VMEM((ROWS, D), BF16),
            pltpu.VMEM((D, 4 * D), BF16),
            pltpu.VMEM((D, D), BF16),
            pltpu.VMEM((DEV, 128), jnp.int32),
            pltpu.VMEM((DEV, MSG_T, 128), BF16),
            pltpu.VMEM((DEV, MSG_N, 128), BF16),
            pltpu.VMEM((DEV, MSG_T, 128), BF16),
            pltpu.VMEM((DEV, MSG_N, 128), BF16),
            pltpu.VMEM((DEV * MSG_T, 128), F32),
            pltpu.VMEM((DEV * MSG_N, 128), F32),
            pltpu.VMEM((CAP * DEV, D), BF16),
            pltpu.VMEM((ALL, D), F32),
            pltpu.VMEM((TOK, D), F32),
            pltpu.VMEM((TOK, D), BF16),
            pltpu.VMEM((TOK, 1), F32),
            pltpu.VMEM((NEG, D), BF16),
            pltpu.VMEM((TOK, 4 * D), BF16),
            pltpu.VMEM((TOK, 4 * D), BF16),
            pltpu.VMEM((H, TOK, TOK), BF16),
            pltpu.VMEM((H, TOK, TOK), BF16),
            pltpu.VMEM((TOK, D), F32),
            pltpu.VMEM((TOK, D), BF16),
            pltpu.VMEM((TOK, D), BF16),
            pltpu.VMEM((TOK + 8, D), F32),
            pltpu.VMEM((TOK, D), BF16),
            pltpu.VMEM((TOK, TOK), BF16),
            pltpu.VMEM((TOK, 4 * D), BF16),
            pltpu.VMEM((TOK, D), BF16),
            pltpu.VMEM((DEV, MSG_T, 128), BF16),
            pltpu.VMEM((DEV, MSG_N, 128), BF16),
            pltpu.VMEM((D, WIDE), BF16),
            pltpu.VMEM((256, WIDE), BF16),
            pltpu.VMEM((256, WIDE), BF16),
            pltpu.VMEM((64, WIDE), BF16),
            pltpu.VMEM((16, WIDE), BF16),
            pltpu.VMEM((3, 64, WIDE), BF16),
            pltpu.VMEM((3, 16, WIDE), BF16),
            pltpu.VMEM((4, 16, WIDE), BF16),
            pltpu.SemaphoreType.DMA((8,)),
            pltpu.SemaphoreType.DMA((2,)),
            pltpu.SemaphoreType.DMA((2,)),
            pltpu.SemaphoreType.DMA((2,)),
            pltpu.SemaphoreType.DMA((2,)),
            pltpu.SemaphoreType.DMA((2,)),
            pltpu.SemaphoreType.DMA((2, 6)),
            pltpu.SemaphoreType.DMA((2, 6)),
            pltpu.SemaphoreType.DMA((2, 3, 5, 3)),
            pltpu.SemaphoreType.DMA((2, 3, 5, 3)),
        ],
        compiler_params=pltpu.CompilerParams(
            collective_id=0, has_side_effects=True, vmem_limit_bytes=60 << 20
        ),
        name="step",
    )(lengths, item_owner, neg_owner, item_slot, neg_slot, table, update, w_in, w_out)


def scatter_kernel(
    arrived_t,
    arrived_n,
    ids_ref,
    update_ref,
    total_ref,
    out_ref,
    grad_in_ref,
    grad_out_ref,
    wide_t,
    wide_n,
    rows,
    slots,
):
    step = pl.program_id(0)
    grad_out_ref[...] = total_ref[:, :D].astype(F32)
    grad_in_ref[...] = total_ref[:, D:].astype(F32)

    @pl.when(step == 0)
    def _():
        for arrived, wide, first, count, msg in (
            (arrived_t, wide_t, 0, CAP_T, MSG_T),
            (arrived_n, wide_n, CAP_T, CAP_N, MSG_N),
        ):
            for s in range(8):
                block = arrived[s * 16 : (s + 1) * 16].astype(F32)
                wide[s * 16 * msg : (s + 1) * 16 * msg, :] = block.reshape(16 * msg, 128)
            for c in range(count):
                for b in range(4):
                    piece = wide[pl.ds(4 * c + b, DEV, stride=msg), :]
                    at = (first + c) * 128
                    rows[at : at + 128, b * 128 : (b + 1) * 128] = piece.astype(BF16)
        slots[...] = jnp.transpose(ids_ref[...])[:16, :]

    fade = jnp.exp((NOW - update_ref[...]).astype(F32) * LOG_RHO)
    fade = jnp.transpose(jnp.concatenate([fade, jnp.zeros((120, 128), F32)], 0))
    for s in range(8):
        first = step * 1024 + s * 128
        chosen = [
            (iota((128, 128), 0) + first == slots[c : c + 1, :]).astype(F32).astype(BF16)
            for c in range(CAP)
        ]
        summed = nn(jnp.concatenate(chosen, 1), rows[...])
        out_ref[s * 128 : (s + 1) * 128, :] = summed * fade[:, s : s + 1]


def scatter(arrived_t, arrived_n, ids, update, total):
    return pl.pallas_call(
        scatter_kernel,
        grid=(4,),
        out_shape=(
            jax.ShapeDtypeStruct((ROWS, D), F32),
            jax.ShapeDtypeStruct((D, 4 * D), F32),
            jax.ShapeDtypeStruct((D, D), F32),
        ),
        in_specs=[
            pl.BlockSpec((DEV, MSG_T, 128), lambda i: (0, 0, 0)),
            pl.BlockSpec((DEV, MSG_N, 128), lambda i: (0, 0, 0)),
            pl.BlockSpec((DEV, 128), lambda i: (0, 0)),
            pl.BlockSpec((8, 128), lambda i: (i, 0)),
            pl.BlockSpec((128, WIDE), lambda i: (i, 0)),
        ],
        out_specs=(
            pl.BlockSpec((1024, D), lambda i: (i, 0)),
            pl.BlockSpec((128, 4 * D), lambda i: (i, 0)),
            pl.BlockSpec((128, D), lambda i: (i, 0)),
        ),
        scratch_shapes=[
            pltpu.VMEM((DEV * MSG_T, 128), F32),
            pltpu.VMEM((DEV * MSG_N, 128), F32),
            pltpu.VMEM((CAP * 128, D), BF16),
            pltpu.VMEM((16, 128), jnp.int32),
        ],
        compiler_params=pltpu.CompilerParams(vmem_limit_bytes=48 << 20),
        name="scatter",
    )(arrived_t, arrived_n, ids, update, total)


def on_device(
    table, last_update, item_owner, item_slot, neg_owner, neg_slot, seq_lengths, w_in, w_out
):
    update = last_update.reshape(ROWS // 128, 128)
    losses, arrived_t, arrived_n, ids, total = step(
        seq_lengths,
        item_owner.reshape(1, TOK),
        neg_owner.reshape(1, NEG),
        item_slot.reshape(1, TOK),
        neg_slot.reshape(1, NEG),
        table,
        update,
        w_in,
        w_out,
    )
    table_grad, grad_in, grad_out = scatter(arrived_t, arrived_n, ids, update, total)
    return (losses.reshape(TOK), table_grad, grad_in, grad_out)


def solution(mesh):
    placed = (
        P(("dp", "table"), None),
        P(("dp", "table")),
        P(("dp", "table"), None),
        P(("dp", "table")),
        P(("dp", "table"), None),
        P(("dp", "table")),
        P(("dp", "table"), None),
        P(),
        P(),
    )
    return jax.shard_map(
        on_device,
        mesh=mesh,
        in_specs=placed,
        out_specs=(P(("dp", "table")), P(("dp", "table"), None), P(), P()),
        check_vma=False,
    )
```

```python
import functools

import jax
import jax.numpy as jnp
from jax import lax
from jax.experimental import pallas as pl
from jax.experimental.pallas import tpu as pltpu
from jax.sharding import PartitionSpec as P

D = 512
H = 4
DH = 128
TOK = 512
NEG = 128
ALL = TOK + NEG
DEV = 128
CAP_T = 8
CAP_N = 2
CAP = CAP_T + CAP_N
MSG_T = 32
MSG_N = 16
LMAX = 256
NOW = 64
ROWS = 4096
WIDE = 5 * D
LOG_RHO = -0.030459207484708574
TAU = 0.125
EPS = 1e-05
MESH = pl.DeviceIdType.MESH
VMEM = pl.BlockSpec(memory_space=pltpu.VMEM)
HBM = pl.BlockSpec(memory_space=pltpu.HBM)
F32 = jnp.float32
BF16 = jnp.bfloat16


def nt(a, b):
    return lax.dot_general(a, b, (((1,), (1,)), ((), ())), preferred_element_type=F32)


def nn(a, b):
    return jnp.dot(a, b, preferred_element_type=F32)


def tn(a, b):
    return lax.dot_general(a, b, (((0,), (0,)), ((), ())), preferred_element_type=F32)


def sigmoid(values):
    return 0.5 + 0.5 * jnp.tanh(0.5 * values)


def iota(shape, dim):
    return lax.broadcasted_iota(jnp.int32, shape, dim)


class Place:
    def __init__(self):
        self.dp = lax.axis_index("dp")
        self.tb = lax.axis_index("table")
        self.me = self.dp * 16 + self.tb
        self.z = self.dp // 2
        self.core = lax.rem(self.dp, 2)
        self.x = self.tb // 4
        self.y = lax.rem(self.tb, 4)

    def along(self, *shifts):
        at = {"z": self.z, "x": self.x, "y": self.y}
        for axis, shift in shifts:
            at[axis] = lax.rem(at[axis] + shift, 4)
        return (at["z"] * 2 + self.core, at["x"] * 4 + at["y"])

    def sibling(self):
        return (self.z * 2 + 1 - self.core, self.tb)


def announce(place):
    barrier = pltpu.get_barrier_semaphore()

    def greet(k, carry):
        other = lax.rem(place.me + k, DEV)
        pl.semaphore_signal(
            barrier, inc=1, device_id=(other // 16, lax.rem(other, 16)), device_id_type=MESH
        )
        return carry

    lax.fori_loop(1, DEV, greet, 0)
    return barrier


def peers(place, c):
    zs = [lax.rem(place.z + j, 4) * 2 for j in range(4)]
    xs = [lax.rem(place.x + j, 4) * 4 for j in range(4)]
    ys = [lax.rem(place.y + c + j, 4) for j in range(4)]
    cores = [place.core, 1 - place.core]
    return [
        (zs[a] + cores[k], xs[(a + b) % 4] + ys[a])
        for b in range(4)
        for a in range(4)
        for k in range(2)
    ]


class Wave:
    AXES = (("x", "y", "z"), ("y", "z", "x"), ("z", "x", "y"))
    PLANE = tuple((j, k) for j in range(4) for k in range(4))[1:]

    def __init__(self, place, number, parts, refs):
        self.place, self.number, self.parts = place, number, parts
        (self.grad, self.total, self.half, self.acc0, self.acc1, self.in1, self.in2) = refs[:7]
        (self.core_send, self.core_recv, self.line_send, self.line_recv, self.plane_sem) = refs[7:]
        self.mine = pl.multiple_of(place.core * 256, 256)
        self.other = pl.multiple_of((1 - place.core) * 256, 256)
        self.at = {"x": place.x, "y": place.y, "z": place.z}
        self.first, self.fifth = [], []

    def across(self, slot, src, dst):
        copy = pltpu.make_async_remote_copy(
            src_ref=src,
            dst_ref=dst,
            send_sem=self.core_send.at[self.number, slot],
            recv_sem=self.core_recv.at[self.number, slot],
            device_id=self.place.sibling(),
            device_id_type=MESH,
        )
        copy.start()
        return copy

    def send(self, p, step, shift, src, dst):
        copy = pltpu.make_async_remote_copy(
            src_ref=src,
            dst_ref=dst,
            send_sem=self.line_send.at[self.number, p, step, shift - 1],
            recv_sem=self.line_recv.at[self.number, p, step, shift - 1],
            device_id=self.place.along((self.AXES[p][0], shift)),
            device_id_type=MESH,
        )
        copy.start()
        return copy

    def spread(self, p, step, j, k, src, dst):
        pltpu.make_async_remote_copy(
            src_ref=src,
            dst_ref=dst,
            send_sem=self.plane_sem.at[self.number, p, step, 0],
            recv_sem=self.plane_sem.at[self.number, p, step, 1],
            device_id=self.place.along((self.AXES[p][1], j), (self.AXES[p][2], k)),
            device_id_type=MESH,
        ).start()

    def settle(self, p, step):
        like = self.in2.at[self.number, p]
        for side in range(2):
            pltpu.make_async_copy(like, like, self.plane_sem.at[self.number, p, step, side]).wait()

    def coordinate(self, p, level):
        return self.at[self.AXES[p][level]]

    def swap(self):
        self.swaps = []
        for p, (start, width) in enumerate(self.parts):
            cols = pl.ds(start, width)
            self.swaps.append(
                self.across(p, self.grad.at[pl.ds(self.other, 256), cols], self.half.at[:, cols])
            )

    def scatter1(self):
        for p, (start, width) in enumerate(self.parts):
            cols = pl.ds(start, width)
            self.swaps[p].wait()
            self.acc0[:, cols] = (
                self.grad[pl.ds(self.mine, 256), cols].astype(F32)
                + self.half[:, cols].astype(F32)
            ).astype(BF16)
            for shift in (1, 3, 2):
                to = pl.multiple_of(lax.rem(self.coordinate(p, 0) + shift, 4) * 64, 64)
                src = self.acc0.at[pl.ds(to, 64), cols]
                self.first.append(self.send(p, 0, shift, src, self.in1.at[shift - 1, :, cols]))

    def scatter2(self):
        for p, (start, width) in enumerate(self.parts):
            cols = pl.ds(start, width)
            for copy in self.first[3 * p : 3 * p + 3]:
                copy.wait()
            own = pl.multiple_of(self.coordinate(p, 0) * 64, 64)
            total = self.acc0[pl.ds(own, 64), cols].astype(F32)
            for k in range(3):
                total += self.in1[k, :, cols].astype(F32)
            self.acc1[:, cols] = total.astype(BF16)
            for n, (j, k) in enumerate(self.PLANE):
                row = pl.multiple_of(lax.rem(self.coordinate(p, 1) + j, 4) * 16, 16)
                col = pl.multiple_of(start + lax.rem(self.coordinate(p, 2) + k, 4) * 128, 128)
                src = self.acc1.at[pl.ds(row, 16), pl.ds(col, 128)]
                self.spread(p, 0, j, k, src, self.in2.at[self.number, p, n])

    def gather4(self):
        for p, (start, width) in enumerate(self.parts):
            self.settle(p, 0)
            row = pl.multiple_of(self.coordinate(p, 1) * 16, 16)
            cols = pl.ds(pl.multiple_of(start + self.coordinate(p, 2) * 128, 128), 128)
            total = self.acc1[pl.ds(row, 16), cols].astype(F32)
            for n in range(15):
                total += self.in2[self.number, p, n].astype(F32)
            narrow = pl.multiple_of(self.mine + self.coordinate(p, 0) * 64 + row, 16)
            self.total[pl.ds(narrow, 16), cols] = total.astype(BF16)
            piece = self.total.at[pl.ds(narrow, 16), cols]
            for j, k in self.PLANE:
                self.spread(p, 1, j, k, piece, piece)

    def gather5(self):
        for p, (start, width) in enumerate(self.parts):
            self.settle(p, 1)
            wide = pl.multiple_of(self.mine + self.coordinate(p, 0) * 64, 64)
            piece = self.total.at[pl.ds(wide, 64), pl.ds(start, width)]
            for shift in (1, 3, 2):
                self.fifth.append(self.send(p, 1, shift, piece, piece))

    def restore(self):
        self.last = []
        for p, (start, width) in enumerate(self.parts):
            for copy in self.fifth[3 * p : 3 * p + 3]:
                copy.wait()
            piece = self.total.at[pl.ds(self.mine, 256), pl.ds(start, width)]
            self.last.append(self.across(3 + p, piece, piece))

    def finish(self):
        for copy in self.last:
            copy.wait()


def step_kernel(
    lengths,
    item_owner_ref,
    neg_owner_ref,
    item_slot_ref,
    neg_slot_ref,
    table_ref,
    update_ref,
    w_in_ref,
    w_out_ref,
    loss_ref,
    arrived_t,
    arrived_n,
    slots_ref,
    total_ref,
    ids_ref,
    item_owner,
    neg_owner,
    item_slot,
    neg_slot,
    update,
    table,
    w_in,
    w_out,
    asked,
    outbox_t,
    outbox_n,
    rows_t,
    rows_n,
    flat_t,
    flat_n,
    held,
    x32,
    n32,
    nb,
    turned,
    scale1,
    negatives,
    placing,
    packing,
    seen0,
    seen1,
    mixed,
    slope,
    weights,
    bend,
    attended,
    gated,
    d_out,
    d_next,
    d_att,
    d_score,
    d_pre,
    grads,
    d_negatives,
    box_t,
    box_n,
    grad,
    half,
    acc0,
    acc1,
    in1,
    in2,
    load_sem,
    id_sem,
    out_sem_t,
    out_sem_n,
    back_sem_t,
    back_sem_n,
    core_send,
    core_recv,
    line_send,
    line_recv,
    plane_sem,
    own_sem,
):
    place = Place()
    pairs = (
        (item_owner_ref, item_owner),
        (neg_owner_ref, neg_owner),
        (item_slot_ref, item_slot),
        (neg_slot_ref, neg_slot),
        (update_ref, update),
        (table_ref, table),
        (w_in_ref, w_in),
        (w_out_ref, w_out),
    )
    loads = [pltpu.make_async_copy(src, dst, load_sem.at[n]) for n, (src, dst) in enumerate(pairs)]
    for copy in loads:
        copy.start()
    barrier = announce(place)
    for copy in loads[:5]:
        copy.wait()

    owner = jnp.concatenate([item_owner[...], neg_owner[...]], 1)
    slot = jnp.concatenate([item_slot[...], neg_slot[...]], 1)
    onehot = (iota((DEV, ALL), 0) == owner).astype(F32)
    before, after = iota((ALL, ALL), 0), iota((ALL, ALL), 1)
    upto = (before <= after) & ((before >= TOK) | (after < TOK))
    count = nn(onehot.astype(BF16), upto.astype(F32).astype(BF16))
    rank = jnp.sum(onehot * count, 0, keepdims=True).astype(jnp.int32) - 1
    rank = rank + jnp.where(iota((1, ALL), 1) >= TOK, CAP_T, 0)
    ranked = (iota((DEV, ALL), 0) == rank).astype(F32).astype(BF16)
    high = (onehot * (slot // 64).astype(F32)).astype(BF16)
    low = (onehot * (slot % 64).astype(F32)).astype(BF16)
    asked[...] = (64.0 * nt(high, ranked) + nt(low, ranked)).astype(jnp.int32)
    pos_t = (owner * CAP_T + rank)[:, :TOK]
    pos_n = ((rank - CAP_T) * DEV + owner)[:, TOK:]
    pl.semaphore_wait(barrier, DEV - 1)

    def each(c, send):
        for k, (d, t) in enumerate(peers(place, c)):
            if k == 0:
                pl.when(c > 0)(functools.partial(send, k, d, t))
            else:
                send(k, d, t)

    def drain(like, sems):
        most = like.at[pl.ds(0, DEV - 1)]
        pltpu.make_async_copy(most, most, sems.at[0]).wait()
        pltpu.make_async_copy(most, most, sems.at[1]).wait()

    def ask(c, carry):
        def send(k, d, t):
            pltpu.make_async_remote_copy(
                src_ref=asked.at[pl.ds(d * 16 + t, 1)],
                dst_ref=ids_ref.at[pl.ds(place.me, 1)],
                send_sem=id_sem.at[0],
                recv_sem=id_sem.at[1],
                device_id=(d, t),
                device_id_type=MESH,
            ).start()

        each(c, send)
        return carry

    lax.fori_loop(0, 4, ask, 0)
    ids_ref[pl.ds(place.me, 1), :] = asked[pl.ds(place.me, 1), :]
    fade = jnp.exp((NOW - update[...]).astype(F32) * LOG_RHO)
    fade = jnp.transpose(jnp.concatenate([fade, jnp.zeros((96, 128), F32)], 0))
    loads[5].wait()
    for c in range(32):
        block = table[c * 128 : (c + 1) * 128, :].astype(F32) * fade[:, c : c + 1]
        table[c * 128 : (c + 1) * 128, :] = block.astype(BF16)
    drain(asked, id_sem)

    def asked_by(c):
        return [ids_ref[pl.ds(d * 16 + t, 1), :] for d, t in peers(place, c)]

    def serve(c, carry):
        wanted = asked_by(c) + [jnp.zeros((96, 128), jnp.int32)]
        wanted = jnp.transpose(jnp.concatenate(wanted, 0))[:CAP_T, :]
        chosen = [
            (iota((CAP_T, ROWS), 1) == wanted[:, k : k + 1]).astype(F32) for k in range(32)
        ]
        found = nn(jnp.concatenate(chosen, 0).astype(BF16), table[...])
        found = found.reshape(32, CAP_T, D)
        for b in range(4):
            flat_t[pl.ds(0, 32), b * 8 : b * 8 + 8, :] = found[:, :, b * 128 : (b + 1) * 128]
        base = c * 32
        outbox_t[pl.ds(base, 32)] = flat_t[pl.ds(0, 32)].astype(BF16)

        def send(k, d, t):
            pltpu.make_async_remote_copy(
                src_ref=outbox_t.at[base + k],
                dst_ref=rows_t.at[place.me],
                send_sem=out_sem_t.at[0],
                recv_sem=out_sem_t.at[1],
                device_id=(d, t),
                device_id_type=MESH,
            ).start()

        each(c, send)
        return carry

    lax.fori_loop(0, 4, serve, 0)
    rows_t[place.me] = outbox_t[0]
    wanted = jnp.concatenate([row for c in range(4) for row in asked_by(c)], 0)
    flat_n[...] = jnp.zeros((DEV * MSG_N, 128), F32)
    for r in range(CAP_N):
        at = wanted[:, CAP_T + r : CAP_T + r + 1]
        found = nn((iota((DEV, ROWS), 1) == at).astype(F32).astype(BF16), table[...])
        for b in range(4):
            flat_n[pl.ds(4 * r + b, DEV, stride=MSG_N), :] = found[:, b * 128 : (b + 1) * 128]
    outbox_n[...] = flat_n[...].astype(BF16).reshape(DEV, MSG_N, 128)

    def serve_n(c, carry):
        base = c * 32

        def send(k, d, t):
            pltpu.make_async_remote_copy(
                src_ref=outbox_n.at[base + k],
                dst_ref=rows_n.at[place.me],
                send_sem=out_sem_n.at[0],
                recv_sem=out_sem_n.at[1],
                device_id=(d, t),
                device_id_type=MESH,
            ).start()

        each(c, send)
        return carry

    lax.fori_loop(0, 4, serve_n, 0)
    rows_n[place.me] = outbox_n[0]

    high = (ids_ref[...] // 64).astype(F32).astype(BF16)
    low = (ids_ref[...] % 64).astype(F32).astype(BF16)
    spread = (iota((DEV, CAP_T * DEV), 1) % CAP_T == iota((DEV, CAP_T * DEV), 0)).astype(F32)
    spread = spread.astype(BF16)
    own = iota((DEV, CAP_T * DEV), 1) // CAP_T == iota((DEV, CAP_T * DEV), 0)
    row = jnp.where(own, 64.0 * nn(high, spread) + nn(low, spread), 0.0)
    slots_ref[:, : CAP_T * DEV] = jnp.sum(row, 0, keepdims=True).astype(jnp.int32)
    column = jnp.transpose(ids_ref[...])
    for r in range(CAP_N):
        at = (CAP_T + r) * DEV
        slots_ref[:, at : at + DEV] = column[CAP_T + r : CAP_T + r + 1, :]
    where = jnp.transpose(jnp.broadcast_to(pos_t, (128, TOK)))
    for c in range(CAP_T):
        match = iota((TOK, 128), 1) + c * 128 == where
        placing[:, c * 128 : (c + 1) * 128] = match.astype(F32).astype(BF16)
    packing[...] = (iota((CAP_T * DEV, TOK), 0) == pos_t).astype(F32).astype(BF16)
    end1 = lengths[0, 0]
    end2 = end1 + lengths[0, 1]
    end3 = end2 + lengths[0, 2]

    def visible(i):
        row = iota((256, 256 * (i + 1)), 0) + 256 * i
        col = iota((256, 256 * (i + 1)), 1)
        start = jnp.where(
            row >= end3, end3, jnp.where(row >= end2, end2, jnp.where(row >= end1, end1, 0))
        )
        return jnp.where((col <= row) & (col >= start), 1.0 / LMAX, 0.0).astype(F32)

    seen0[...] = visible(0)
    seen1[...] = visible(1)
    drain(outbox_t, out_sem_t)

    flat_t[...] = rows_t[...].astype(F32)
    for b in range(4):
        piece = flat_t[:, b * 8 : b * 8 + 8, :].reshape(CAP_T * DEV, 128)
        held[: CAP_T * DEV, b * 128 : (b + 1) * 128] = piece.astype(BF16)
    x32[pl.ds(0, TOK), :] = nn(placing[...], held[: CAP_T * DEV, :])
    for i in range(4):
        span = pl.ds(i * 128, 128)
        x = x32[span, :]
        center = x - jnp.mean(x, -1, keepdims=True)
        scale = lax.rsqrt(jnp.mean(center * center, -1, keepdims=True) + EPS)
        normed = center * scale
        n32[span, :] = normed
        nb[span, :] = normed.astype(BF16)
        scale1[span, :] = scale
    turned[...] = jnp.transpose(n32[...]).astype(BF16)

    loads[6].wait()

    def project(cb, carry):
        cols = pl.ds(pl.multiple_of(cb * 256, 256), 256)
        pre = nn(nb[...], w_in[:, cols])
        sig = sigmoid(pre)
        mixed[:, cols] = (pre * sig).astype(BF16)
        slope[:, cols] = (sig * (1.0 + pre * (1.0 - sig))).astype(BF16)
        return carry

    lax.fori_loop(0, 8, project, 0, unroll=4)

    def lanes(part, h):
        at = part * 512 + h * 128
        return pl.ds(at if isinstance(at, int) else pl.multiple_of(at, 128), 128)

    def attend(h, carry):
        for i in range(2):
            span, past = pl.ds(256 * i, 256), pl.ds(0, 256 * (i + 1))
            score = nt(mixed[span, lanes(2, h)], mixed[past, lanes(3, h)])
            sig = sigmoid(score)
            seen = (seen0, seen1)[i][...]
            weight = (score * sig * seen).astype(BF16)
            weights[h, span, past] = weight
            bend[h, span, past] = (sig * (1.0 + score * (1.0 - sig)) * seen).astype(BF16)
            attended[span, lanes(0, h)] = nn(weight, mixed[past, lanes(1, h)])
        return carry

    lax.fori_loop(0, H, attend, 0, unroll=True)

    loads[7].wait()
    drain(outbox_n, out_sem_n)
    flat_n[...] = rows_n[...].astype(F32).reshape(DEV * MSG_N, 128)
    for c in range(CAP_N):
        for b in range(4):
            piece = flat_n[pl.ds(4 * c + b, DEV, stride=MSG_N), :]
            at = (CAP_T + c) * 128
            held[at : at + 128, b * 128 : (b + 1) * 128] = piece.astype(BF16)
    x = tn((iota((CAP_N * DEV, NEG), 0) == pos_n).astype(F32).astype(BF16), held[CAP_T * DEV :, :])
    x32[pl.ds(512, 128), :] = x
    negatives[...] = x.astype(BF16)
    d_next[pl.ds(0, 8), :] = jnp.zeros((8, D), F32)
    d_negs = jnp.zeros((NEG, D), F32)
    for i in range(2):
        span = pl.ds(256 * i, 256)
        values = attended[span, :]
        center = values - jnp.mean(values, -1, keepdims=True)
        scale = lax.rsqrt(jnp.mean(center * center, -1, keepdims=True) + EPS)
        normed = center * scale
        gate = mixed[span, 0:512].astype(F32)
        gated_b = (normed * gate).astype(BF16)
        gated[span, :] = gated_b
        out_b = (x32[span, :] + nn(gated_b, w_out[...])).astype(BF16)
        out = out_b.astype(F32)
        following = x32[pl.ds(256 * i + 1, 256), :]
        positive = jnp.sum(out * following, -1, keepdims=True) * TAU
        negative = nt(out_b, negatives[...]) * TAU
        top = jnp.maximum(positive, jnp.max(negative, -1, keepdims=True))
        exp_p = jnp.exp(positive - top)
        exp_n = jnp.exp(negative - top)
        total = exp_p + jnp.sum(exp_n, -1, keepdims=True)
        row = iota((256, 1), 0) + (256 * i + 1)
        valid = (row != end1) & (row != end2) & (row != end3) & (row != TOK)
        valid = jnp.where(valid, 1.0, 0.0).astype(F32)
        loss = (jnp.log(total) + top - positive) * valid
        loss_ref[:, span] = jnp.transpose(jnp.broadcast_to(loss, (256, 128)))[:1, :]
        share = valid / total
        d_pos = (exp_p * share - valid) * TAU
        d_neg = (exp_n * (share * TAU)).astype(BF16)
        d_out_b = (d_pos * following + nn(d_neg, negatives[...])).astype(BF16)
        d_out[span, :] = d_out_b
        d_next[pl.ds(256 * i + 8, 256), :] = d_pos * out
        d_negs += tn(d_neg, out_b)
        d_gated = nt(d_out_b, w_out[...])
        d_pre[span, 0:512] = (d_gated * normed * slope[span, 0:512].astype(F32)).astype(BF16)
        d_normed = d_gated * gate
        d_values = scale * (
            d_normed
            - jnp.mean(d_normed, -1, keepdims=True)
            - normed * jnp.mean(d_normed * normed, -1, keepdims=True)
        )
        d_att[span, :] = d_values.astype(BF16)
    d_negatives[...] = d_negs.astype(BF16)
    for c in range(CAP_N):
        at = iota((DEV, NEG), 0) + c * DEV
        sent = nn((at == pos_n).astype(F32).astype(BF16), d_negatives[...])
        for b in range(4):
            flat_n[pl.ds(4 * c + b, DEV, stride=MSG_N), :] = sent[:, b * 128 : (b + 1) * 128]
    box_n[...] = flat_n[...].astype(BF16).reshape(DEV, MSG_N, 128)
    own_n = pltpu.make_async_copy(box_n.at[place.me], arrived_n.at[place.me], own_sem.at[0])
    own_n.start()

    def post_n(c, carry):
        def send(k, d, t):
            pltpu.make_async_remote_copy(
                src_ref=box_n.at[d * 16 + t],
                dst_ref=arrived_n.at[place.me],
                send_sem=back_sem_n.at[0],
                recv_sem=back_sem_n.at[1],
                device_id=(d, t),
                device_id_type=MESH,
            ).start()

        each(c, send)
        return carry

    lax.fori_loop(0, 4, post_n, 0)

    def back(h, carry):
        for i in range(2):
            span, past = pl.ds(256 * i, 256), pl.ds(0, 256 * (i + 1))
            d_weight = nt(d_att[span, lanes(0, h)], mixed[past, lanes(1, h)])
            d_s = (d_weight * bend[h, span, past].astype(F32)).astype(BF16)
            d_score[span, past] = d_s
            d_q = nn(d_s, mixed[past, lanes(3, h)])
            d_pre[span, lanes(2, h)] = (d_q * slope[span, lanes(2, h)].astype(F32)).astype(BF16)
        for i in range(2):
            span, future = pl.ds(256 * i, 256), pl.ds(256 * i, 512 - 256 * i)
            d_v = tn(weights[h, future, span], d_att[future, lanes(0, h)])
            d_pre[span, lanes(1, h)] = (d_v * slope[span, lanes(1, h)].astype(F32)).astype(BF16)
            d_k = tn(d_score[future, span], mixed[future, lanes(2, h)])
            d_pre[span, lanes(3, h)] = (d_k * slope[span, lanes(3, h)].astype(F32)).astype(BF16)
        return carry

    refs = (grad, total_ref, half, acc0, acc1, in1, in2)
    refs += (core_send, core_recv, line_send, line_recv, plane_sem)
    wave_a = Wave(place, 0, ((0, 512), (512, 512)), refs)
    wave_b = Wave(place, 1, ((1024, 512), (1536, 512), (2048, 512)), refs)
    groups = [peers(place, c) for c in range(4)]

    def post(first, last):
        for n in range(first, last):
            d, t = groups[n // 32][n % 32]
            pltpu.make_async_remote_copy(
                src_ref=box_t.at[d * 16 + t],
                dst_ref=arrived_t.at[place.me],
                send_sem=back_sem_t.at[0],
                recv_sem=back_sem_t.at[1],
                device_id=(d, t),
                device_id_type=MESH,
            ).start()

    grad[:, pl.ds(0, 512)] = tn(gated[...], d_out[...]).astype(BF16)
    grad[:, pl.ds(512, 512)] = nn(turned[...], d_pre[:, pl.ds(0, 512)]).astype(BF16)
    wave_a.swap()
    back(0, 0)
    back(1, 0)
    wave_a.scatter1()
    back(2, 0)
    back(3, 0)
    for cb in range(1, 4):
        cols = pl.ds(cb * 512, 512)
        grad[:, pl.ds(512 + cb * 512, 512)] = nn(turned[...], d_pre[:, cols]).astype(BF16)
    wave_b.swap()
    wave_a.scatter2()

    for i in range(2):
        span = pl.ds(256 * i, 256)
        d_normed = nt(d_pre[span, :], w_in[...])
        normed = n32[span, :]
        d_x = scale1[span, :] * (
            d_normed
            - jnp.mean(d_normed, -1, keepdims=True)
            - normed * jnp.mean(d_normed * normed, -1, keepdims=True)
        )
        d_x += d_out[span, :].astype(F32) + d_next[pl.ds(256 * i + 7, 256), :]
        grads[span, :] = d_x.astype(BF16)

    wave_b.scatter1()

    for j in range(4):
        half_of = pl.ds(j * 256, 256)
        sent = nn(packing[half_of, :], grads[...]).reshape(32, CAP_T, D)
        for b in range(4):
            flat_t[pl.ds(j * 32, 32), b * 8 : b * 8 + 8, :] = sent[:, :, b * 128 : (b + 1) * 128]
    box_t[...] = flat_t[...].astype(BF16)

    own_t = pltpu.make_async_copy(box_t.at[place.me], arrived_t.at[place.me], own_sem.at[1])
    own_t.start()
    wave_a.gather4()
    wave_b.scatter2()
    post(1, 50)
    wave_b.gather4()
    post(50, 90)
    wave_a.gather5()
    wave_b.gather5()
    post(90, 128)
    wave_a.restore()
    wave_b.restore()
    wave_a.finish()
    wave_b.finish()
    own_n.wait()
    own_t.wait()
    drain(box_n, back_sem_n)
    drain(box_t, back_sem_t)


def step(lengths, item_owner, neg_owner, item_slot, neg_slot, table, update, w_in, w_out):
    return pl.pallas_call(
        step_kernel,
        out_shape=(
            jax.ShapeDtypeStruct((1, TOK), F32),
            jax.ShapeDtypeStruct((DEV, MSG_T, 128), BF16),
            jax.ShapeDtypeStruct((DEV, MSG_N, 128), BF16),
            jax.ShapeDtypeStruct((1, CAP * DEV), jnp.int32),
            jax.ShapeDtypeStruct((D, WIDE), BF16),
        ),
        in_specs=[pl.BlockSpec(memory_space=pltpu.SMEM)] + [HBM] * 8,
        out_specs=(VMEM, HBM, HBM, VMEM, VMEM),
        scratch_shapes=[
            pltpu.VMEM((DEV, 128), jnp.int32),
            pltpu.VMEM((1, TOK), jnp.int32),
            pltpu.VMEM((1, NEG), jnp.int32),
            pltpu.VMEM((1, TOK), jnp.int32),
            pltpu.VMEM((1, NEG), jnp.int32),
            pltpu.VMEM((ROWS // 128, 128), jnp.int32),
            pltpu.VMEM((ROWS, D), BF16),
            pltpu.VMEM((D, 4 * D), BF16),
            pltpu.VMEM((D, D), BF16),
            pltpu.VMEM((DEV, 128), jnp.int32),
            pltpu.VMEM((DEV, MSG_T, 128), BF16),
            pltpu.VMEM((DEV, MSG_N, 128), BF16),
            pltpu.VMEM((DEV, MSG_T, 128), BF16),
            pltpu.VMEM((DEV, MSG_N, 128), BF16),
            pltpu.VMEM((DEV, MSG_T, 128), F32),
            pltpu.VMEM((DEV * MSG_N, 128), F32),
            pltpu.VMEM((CAP * DEV, D), BF16),
            pltpu.VMEM((ALL, D), F32),
            pltpu.VMEM((TOK, D), F32),
            pltpu.VMEM((TOK, D), BF16),
            pltpu.VMEM((D, TOK), BF16),
            pltpu.VMEM((TOK, 1), F32),
            pltpu.VMEM((NEG, D), BF16),
            pltpu.VMEM((TOK, CAP_T * DEV), BF16),
            pltpu.VMEM((CAP_T * DEV, TOK), BF16),
            pltpu.VMEM((256, 256), F32),
            pltpu.VMEM((256, 512), F32),
            pltpu.VMEM((TOK, 4 * D), BF16),
            pltpu.VMEM((TOK, 4 * D), BF16),
            pltpu.VMEM((H, TOK, TOK), BF16),
            pltpu.VMEM((H, TOK, TOK), BF16),
            pltpu.VMEM((TOK, D), F32),
            pltpu.VMEM((TOK, D), BF16),
            pltpu.VMEM((TOK, D), BF16),
            pltpu.VMEM((TOK + 8, D), F32),
            pltpu.VMEM((TOK, D), BF16),
            pltpu.VMEM((TOK, TOK), BF16),
            pltpu.VMEM((TOK, 4 * D), BF16),
            pltpu.VMEM((TOK, D), BF16),
            pltpu.VMEM((NEG, D), BF16),
            pltpu.VMEM((DEV, MSG_T, 128), BF16),
            pltpu.VMEM((DEV, MSG_N, 128), BF16),
            pltpu.VMEM((D, WIDE), BF16),
            pltpu.VMEM((256, WIDE), BF16),
            pltpu.VMEM((256, WIDE), BF16),
            pltpu.VMEM((64, WIDE), BF16),
            pltpu.VMEM((3, 64, WIDE), BF16),
            pltpu.VMEM((2, 3, 15, 16, 128), BF16),
            pltpu.SemaphoreType.DMA((8,)),
            pltpu.SemaphoreType.DMA((2,)),
            pltpu.SemaphoreType.DMA((2,)),
            pltpu.SemaphoreType.DMA((2,)),
            pltpu.SemaphoreType.DMA((2,)),
            pltpu.SemaphoreType.DMA((2,)),
            pltpu.SemaphoreType.DMA((2, 6)),
            pltpu.SemaphoreType.DMA((2, 6)),
            pltpu.SemaphoreType.DMA((2, 3, 2, 3)),
            pltpu.SemaphoreType.DMA((2, 3, 2, 3)),
            pltpu.SemaphoreType.DMA((2, 3, 2, 2)),
            pltpu.SemaphoreType.DMA((2,)),
        ],
        compiler_params=pltpu.CompilerParams(
            collective_id=0, has_side_effects=True, vmem_limit_bytes=60 << 20
        ),
        name="step",
    )(lengths, item_owner, neg_owner, item_slot, neg_slot, table, update, w_in, w_out)


def scatter_kernel(
    arrived_t_ref,
    arrived_n_ref,
    slots_ref,
    update_ref,
    total_ref,
    out_ref,
    grad_in_ref,
    grad_out_ref,
    arrived_t,
    arrived_n,
    slots,
    update,
    total,
    wide_t,
    wide_n,
    rows,
    chosen0,
    chosen1,
    load_sem,
):
    step = pl.program_id(0)

    def choose(block, chosen):
        for half in range(2):
            local = slots[...] - (block * 512 + half * 256)
            local = jnp.where((local >= 0) & (local < 256), local, -1).astype(F32).astype(BF16)
            row = iota((256, 1), 0).astype(F32).astype(BF16)
            far = jnp.abs(row - local)
            chosen[half * 256 : (half + 1) * 256, :] = jnp.maximum(1.0 - far, 0.0).astype(BF16)

    def fold(first, chosen):
        summed = nn(chosen[...], rows[...])
        for k in range(4):
            at = first + k
            out_ref[at * 128 : (at + 1) * 128, :] = (
                summed[k * 128 : (k + 1) * 128] * fade[:, at : at + 1]
            )

    pairs = (
        (arrived_t_ref, arrived_t),
        (arrived_n_ref, arrived_n),
        (slots_ref, slots),
        (update_ref, update),
        (total_ref, total),
    )
    loads = [pltpu.make_async_copy(src, dst, load_sem.at[n]) for n, (src, dst) in enumerate(pairs)]

    @pl.when(step == 0)
    def _():
        for copy in loads:
            copy.start()
        loads[2].wait()
        choose(0, chosen0)
        for copy in loads[:2] + loads[3:]:
            copy.wait()
        wide_t[...] = arrived_t[...].astype(F32)
        for b in range(4):
            piece = wide_t[:, b * 8 : b * 8 + 8, :].reshape(CAP_T * DEV, 128)
            rows[: CAP_T * DEV, b * 128 : (b + 1) * 128] = piece.astype(BF16)
        wide_n[...] = arrived_n[...].astype(F32).reshape(DEV * MSG_N, 128)
        for c in range(CAP_N):
            for b in range(4):
                piece = wide_n[pl.ds(4 * c + b, DEV, stride=MSG_N), :]
                at = (CAP_T + c) * 128
                rows[at : at + 128, b * 128 : (b + 1) * 128] = piece.astype(BF16)

    part = total[pl.ds(pl.multiple_of(step * 128, 128), 128), :]
    grad_out_ref[...] = part[:, :D].astype(F32)
    grad_in_ref[...] = part[:, D:].astype(F32)
    fade = jnp.exp((NOW - update[pl.ds(pl.multiple_of(step * 8, 8), 8), :]).astype(F32) * LOG_RHO)
    fade = jnp.transpose(jnp.concatenate([fade, jnp.zeros((120, 128), F32)], 0))
    choose(2 * step + 1, chosen1)
    fold(0, chosen0)
    choose(2 * step + 2, chosen0)
    fold(4, chosen1)


def scatter(arrived_t, arrived_n, slots, update, total):
    return pl.pallas_call(
        scatter_kernel,
        grid=(4,),
        out_shape=(
            jax.ShapeDtypeStruct((ROWS, D), F32),
            jax.ShapeDtypeStruct((D, 4 * D), F32),
            jax.ShapeDtypeStruct((D, D), F32),
        ),
        in_specs=[HBM] * 5,
        out_specs=(
            pl.BlockSpec((1024, D), lambda i: (i, 0)),
            pl.BlockSpec((128, 4 * D), lambda i: (i, 0)),
            pl.BlockSpec((128, D), lambda i: (i, 0)),
        ),
        scratch_shapes=[
            pltpu.VMEM((DEV, MSG_T, 128), BF16),
            pltpu.VMEM((DEV, MSG_N, 128), BF16),
            pltpu.VMEM((1, CAP * DEV), jnp.int32),
            pltpu.VMEM((ROWS // 128, 128), jnp.int32),
            pltpu.VMEM((D, WIDE), BF16),
            pltpu.VMEM((DEV, MSG_T, 128), F32),
            pltpu.VMEM((DEV * MSG_N, 128), F32),
            pltpu.VMEM((CAP * DEV, D), BF16),
            pltpu.VMEM((512, CAP * DEV), BF16),
            pltpu.VMEM((512, CAP * DEV), BF16),
            pltpu.SemaphoreType.DMA((5,)),
        ],
        compiler_params=pltpu.CompilerParams(vmem_limit_bytes=60 << 20),
        name="scatter",
    )(arrived_t, arrived_n, slots, update, total)


def on_device(
    table, last_update, item_owner, item_slot, neg_owner, neg_slot, seq_lengths, w_in, w_out
):
    update = last_update.reshape(ROWS // 128, 128)
    losses, arrived_t, arrived_n, slots, total = step(
        seq_lengths,
        item_owner.reshape(1, TOK),
        neg_owner.reshape(1, NEG),
        item_slot.reshape(1, TOK),
        neg_slot.reshape(1, NEG),
        table,
        update,
        w_in,
        w_out,
    )
    table_grad, grad_in, grad_out = scatter(arrived_t, arrived_n, slots, update, total)
    return (losses.reshape(TOK), table_grad, grad_in, grad_out)


def solution(mesh):
    placed = (
        P(("dp", "table"), None),
        P(("dp", "table")),
        P(("dp", "table"), None),
        P(("dp", "table")),
        P(("dp", "table"), None),
        P(("dp", "table")),
        P(("dp", "table"), None),
        P(),
        P(),
    )
    return jax.shard_map(
        on_device,
        mesh=mesh,
        in_specs=placed,
        out_specs=(P(("dp", "table")), P(("dp", "table"), None), P(), P()),
        check_vma=False,
    )
```

```python
import functools

import jax
import jax.numpy as jnp
from jax import lax
from jax.experimental import pallas as pl
from jax.experimental.pallas import tpu as pltpu
from jax.sharding import PartitionSpec as P

D = 512
H = 4
DH = 128
TOK = 512
NEG = 128
ALL = TOK + NEG
DEV = 128
CAP_T = 8
CAP_N = 2
CAP = CAP_T + CAP_N
MSG_T = 32
MSG_N = 16
LMAX = 256
NOW = 64
ROWS = 4096
WIDE = 5 * D
LOG_RHO = -0.030459207484708574
TAU = 0.125
EPS = 1e-05
MESH = pl.DeviceIdType.MESH
VMEM = pl.BlockSpec(memory_space=pltpu.VMEM)
HBM = pl.BlockSpec(memory_space=pltpu.HBM)
F32 = jnp.float32
BF16 = jnp.bfloat16


def nt(a, b):
    return lax.dot_general(a, b, (((1,), (1,)), ((), ())), preferred_element_type=F32)


def nn(a, b):
    return jnp.dot(a, b, preferred_element_type=F32)


def tn(a, b):
    return lax.dot_general(a, b, (((0,), (0,)), ((), ())), preferred_element_type=F32)


def sigmoid(values):
    return 0.5 + 0.5 * jnp.tanh(0.5 * values)


def iota(shape, dim):
    return lax.broadcasted_iota(jnp.int32, shape, dim)


class Place:
    def __init__(self):
        self.dp = lax.axis_index("dp")
        self.tb = lax.axis_index("table")
        self.me = self.dp * 16 + self.tb
        self.z = self.dp // 2
        self.core = lax.rem(self.dp, 2)
        self.x = self.tb // 4
        self.y = lax.rem(self.tb, 4)

    def along(self, *shifts):
        at = {"z": self.z, "x": self.x, "y": self.y}
        for axis, shift in shifts:
            at[axis] = lax.rem(at[axis] + shift, 4)
        return (at["z"] * 2 + self.core, at["x"] * 4 + at["y"])

    def sibling(self):
        return (self.z * 2 + 1 - self.core, self.tb)


def announce(place):
    barrier = pltpu.get_barrier_semaphore()

    def greet(k, carry):
        other = lax.rem(place.me + k, DEV)
        pl.semaphore_signal(
            barrier, inc=1, device_id=(other // 16, lax.rem(other, 16)), device_id_type=MESH
        )
        return carry

    lax.fori_loop(1, DEV, greet, 0)
    return barrier


def peers(place, c):
    zs = [lax.rem(place.z + j, 4) * 2 for j in range(4)]
    xs = [lax.rem(place.x + j, 4) * 4 for j in range(4)]
    ys = [lax.rem(place.y + c + j, 4) for j in range(4)]
    cores = [place.core, 1 - place.core]
    return [
        (zs[a] + cores[k], xs[(a + b) % 4] + ys[a])
        for b in range(4)
        for a in range(4)
        for k in range(2)
    ]


class Wave:
    AXES = (("x", "y", "z"), ("y", "z", "x"), ("z", "x", "y"))
    PLANE = tuple((j, k) for j in range(4) for k in range(4))[1:]

    def __init__(self, place, number, parts, refs):
        self.place, self.number, self.parts = place, number, parts
        (self.grad, self.total, self.half, self.acc0, self.acc1, self.in1, self.in2) = refs[:7]
        (self.core_send, self.core_recv, self.line_send, self.line_recv, self.plane_sem) = refs[7:]
        self.mine = pl.multiple_of(place.core * 256, 256)
        self.other = pl.multiple_of((1 - place.core) * 256, 256)
        self.at = {"x": place.x, "y": place.y, "z": place.z}
        self.first, self.fifth = [], []

    def across(self, slot, src, dst):
        copy = pltpu.make_async_remote_copy(
            src_ref=src,
            dst_ref=dst,
            send_sem=self.core_send.at[self.number, slot],
            recv_sem=self.core_recv.at[self.number, slot],
            device_id=self.place.sibling(),
            device_id_type=MESH,
        )
        copy.start()
        return copy

    def send(self, p, step, shift, src, dst):
        copy = pltpu.make_async_remote_copy(
            src_ref=src,
            dst_ref=dst,
            send_sem=self.line_send.at[self.number, p, step, shift - 1],
            recv_sem=self.line_recv.at[self.number, p, step, shift - 1],
            device_id=self.place.along((self.AXES[p][0], shift)),
            device_id_type=MESH,
        )
        copy.start()
        return copy

    def spread(self, p, step, j, k, src, dst):
        pltpu.make_async_remote_copy(
            src_ref=src,
            dst_ref=dst,
            send_sem=self.plane_sem.at[self.number, p, step, 0],
            recv_sem=self.plane_sem.at[self.number, p, step, 1],
            device_id=self.place.along((self.AXES[p][1], j), (self.AXES[p][2], k)),
            device_id_type=MESH,
        ).start()

    def settle(self, p, step):
        like = self.in2.at[self.number, p]
        for side in range(2):
            pltpu.make_async_copy(like, like, self.plane_sem.at[self.number, p, step, side]).wait()

    def coordinate(self, p, level):
        return self.at[self.AXES[p][level]]

    def swap(self):
        self.swaps = []
        for p, (start, width) in enumerate(self.parts):
            cols = pl.ds(start, width)
            self.swaps.append(
                self.across(p, self.grad.at[pl.ds(self.other, 256), cols], self.half.at[:, cols])
            )

    def scatter1(self):
        for p, (start, width) in enumerate(self.parts):
            cols = pl.ds(start, width)
            self.swaps[p].wait()
            self.acc0[:, cols] = (
                self.grad[pl.ds(self.mine, 256), cols].astype(F32)
                + self.half[:, cols].astype(F32)
            ).astype(BF16)
            for shift in (1, 3, 2):
                to = pl.multiple_of(lax.rem(self.coordinate(p, 0) + shift, 4) * 64, 64)
                src = self.acc0.at[pl.ds(to, 64), cols]
                self.first.append(self.send(p, 0, shift, src, self.in1.at[shift - 1, :, cols]))

    def scatter2(self):
        for p, (start, width) in enumerate(self.parts):
            cols = pl.ds(start, width)
            for copy in self.first[3 * p : 3 * p + 3]:
                copy.wait()
            own = pl.multiple_of(self.coordinate(p, 0) * 64, 64)
            total = self.acc0[pl.ds(own, 64), cols].astype(F32)
            for k in range(3):
                total += self.in1[k, :, cols].astype(F32)
            self.acc1[:, cols] = total.astype(BF16)
            for n, (j, k) in enumerate(self.PLANE):
                row = pl.multiple_of(lax.rem(self.coordinate(p, 1) + j, 4) * 16, 16)
                col = pl.multiple_of(start + lax.rem(self.coordinate(p, 2) + k, 4) * 128, 128)
                src = self.acc1.at[pl.ds(row, 16), pl.ds(col, 128)]
                self.spread(p, 0, j, k, src, self.in2.at[self.number, p, n])

    def gather4(self):
        for p, (start, width) in enumerate(self.parts):
            self.settle(p, 0)
            row = pl.multiple_of(self.coordinate(p, 1) * 16, 16)
            cols = pl.ds(pl.multiple_of(start + self.coordinate(p, 2) * 128, 128), 128)
            total = self.acc1[pl.ds(row, 16), cols].astype(F32)
            for n in range(15):
                total += self.in2[self.number, p, n].astype(F32)
            narrow = pl.multiple_of(self.mine + self.coordinate(p, 0) * 64 + row, 16)
            self.total[pl.ds(narrow, 16), cols] = total.astype(BF16)
            piece = self.total.at[pl.ds(narrow, 16), cols]
            for j, k in self.PLANE:
                self.spread(p, 1, j, k, piece, piece)

    def gather5(self):
        for p, (start, width) in enumerate(self.parts):
            self.settle(p, 1)
            wide = pl.multiple_of(self.mine + self.coordinate(p, 0) * 64, 64)
            piece = self.total.at[pl.ds(wide, 64), pl.ds(start, width)]
            for shift in (1, 3, 2):
                self.fifth.append(self.send(p, 1, shift, piece, piece))

    def restore(self):
        self.last = []
        for p, (start, width) in enumerate(self.parts):
            for copy in self.fifth[3 * p : 3 * p + 3]:
                copy.wait()
            piece = self.total.at[pl.ds(self.mine, 256), pl.ds(start, width)]
            self.last.append(self.across(3 + p, piece, piece))

    def finish(self):
        for copy in self.last:
            copy.wait()


def step_kernel(
    lengths,
    item_owner_ref,
    neg_owner_ref,
    item_slot_ref,
    neg_slot_ref,
    table_ref,
    update_ref,
    w_in_ref,
    w_out_ref,
    loss_ref,
    arrived_t,
    arrived_n,
    slots_ref,
    total_out,
    total_ref,
    ids_ref,
    item_owner,
    neg_owner,
    item_slot,
    neg_slot,
    update,
    table,
    w_in,
    w_out,
    asked,
    outbox_t,
    outbox_n,
    rows_t,
    rows_n,
    flat_t,
    flat_n,
    held,
    x32,
    n32,
    nb,
    turned,
    scale1,
    negatives,
    placing,
    packing,
    seen0,
    seen1,
    mixed,
    slope,
    weights,
    bend,
    attended,
    gated,
    d_out,
    d_next,
    d_att,
    d_score,
    d_pre,
    grads,
    d_negatives,
    box_t,
    box_n,
    grad,
    half,
    acc0,
    acc1,
    in1,
    in2,
    load_sem,
    id_sem,
    out_sem_t,
    out_sem_n,
    back_sem_t,
    back_sem_n,
    core_send,
    core_recv,
    line_send,
    line_recv,
    plane_sem,
    own_sem,
    total_sem,
):
    place = Place()
    pairs = (
        (item_owner_ref, item_owner),
        (neg_owner_ref, neg_owner),
        (item_slot_ref, item_slot),
        (neg_slot_ref, neg_slot),
        (update_ref, update),
        (table_ref, table),
        (w_in_ref, w_in),
        (w_out_ref, w_out),
    )
    loads = [pltpu.make_async_copy(src, dst, load_sem.at[n]) for n, (src, dst) in enumerate(pairs)]
    for copy in loads:
        copy.start()
    barrier = announce(place)
    for copy in loads[:5]:
        copy.wait()

    owner = jnp.concatenate([item_owner[...], neg_owner[...]], 1)
    slot = jnp.concatenate([item_slot[...], neg_slot[...]], 1)
    onehot = (iota((DEV, ALL), 0) == owner).astype(F32)
    before, after = iota((ALL, ALL), 0), iota((ALL, ALL), 1)
    upto = (before <= after) & ((before >= TOK) | (after < TOK))
    count = nn(onehot.astype(BF16), upto.astype(F32).astype(BF16))
    rank = jnp.sum(onehot * count, 0, keepdims=True).astype(jnp.int32) - 1
    rank = rank + jnp.where(iota((1, ALL), 1) >= TOK, CAP_T, 0)
    ranked = (iota((DEV, ALL), 0) == rank).astype(F32).astype(BF16)
    high = (onehot * (slot // 64).astype(F32)).astype(BF16)
    low = (onehot * (slot % 64).astype(F32)).astype(BF16)
    asked[...] = (64.0 * nt(high, ranked) + nt(low, ranked)).astype(jnp.int32)
    pos_t = (owner * CAP_T + rank)[:, :TOK]
    pos_n = ((rank - CAP_T) * DEV + owner)[:, TOK:]
    pl.semaphore_wait(barrier, DEV - 1)

    def each(c, send):
        for k, (d, t) in enumerate(peers(place, c)):
            if k == 0:
                pl.when(c > 0)(functools.partial(send, k, d, t))
            else:
                send(k, d, t)

    def drain(like, sems):
        most = like.at[pl.ds(0, DEV - 1)]
        pltpu.make_async_copy(most, most, sems.at[0]).wait()
        pltpu.make_async_copy(most, most, sems.at[1]).wait()

    def ask(c, carry):
        def send(k, d, t):
            pltpu.make_async_remote_copy(
                src_ref=asked.at[pl.ds(d * 16 + t, 1)],
                dst_ref=ids_ref.at[pl.ds(place.me, 1)],
                send_sem=id_sem.at[0],
                recv_sem=id_sem.at[1],
                device_id=(d, t),
                device_id_type=MESH,
            ).start()

        each(c, send)
        return carry

    lax.fori_loop(0, 4, ask, 0)
    ids_ref[pl.ds(place.me, 1), :] = asked[pl.ds(place.me, 1), :]
    fade = jnp.exp((NOW - update[...]).astype(F32) * LOG_RHO)
    fade = jnp.transpose(jnp.concatenate([fade, jnp.zeros((96, 128), F32)], 0))
    loads[5].wait()
    for c in range(32):
        block = table[c * 128 : (c + 1) * 128, :].astype(F32) * fade[:, c : c + 1]
        table[c * 128 : (c + 1) * 128, :] = block.astype(BF16)
    drain(asked, id_sem)

    def asked_by(c):
        return [ids_ref[pl.ds(d * 16 + t, 1), :] for d, t in peers(place, c)]

    def serve(c, carry):
        wanted = asked_by(c) + [jnp.zeros((96, 128), jnp.int32)]
        wanted = jnp.transpose(jnp.concatenate(wanted, 0))[:CAP_T, :]
        chosen = [
            (iota((CAP_T, ROWS), 1) == wanted[:, k : k + 1]).astype(F32) for k in range(32)
        ]
        found = nn(jnp.concatenate(chosen, 0).astype(BF16), table[...])
        found = found.reshape(32, CAP_T, D)
        for b in range(4):
            flat_t[pl.ds(0, 32), b * 8 : b * 8 + 8, :] = found[:, :, b * 128 : (b + 1) * 128]
        base = c * 32
        outbox_t[pl.ds(base, 32)] = flat_t[pl.ds(0, 32)].astype(BF16)

        def send(k, d, t):
            pltpu.make_async_remote_copy(
                src_ref=outbox_t.at[base + k],
                dst_ref=rows_t.at[place.me],
                send_sem=out_sem_t.at[0],
                recv_sem=out_sem_t.at[1],
                device_id=(d, t),
                device_id_type=MESH,
            ).start()

        each(c, send)
        return carry

    lax.fori_loop(0, 4, serve, 0)
    rows_t[place.me] = outbox_t[0]
    wanted = jnp.concatenate([row for c in range(4) for row in asked_by(c)], 0)
    flat_n[...] = jnp.zeros((DEV * MSG_N, 128), F32)
    for r in range(CAP_N):
        at = wanted[:, CAP_T + r : CAP_T + r + 1]
        found = nn((iota((DEV, ROWS), 1) == at).astype(F32).astype(BF16), table[...])
        for b in range(4):
            flat_n[pl.ds(4 * r + b, DEV, stride=MSG_N), :] = found[:, b * 128 : (b + 1) * 128]
    outbox_n[...] = flat_n[...].astype(BF16).reshape(DEV, MSG_N, 128)

    def serve_n(c, carry):
        base = c * 32

        def send(k, d, t):
            pltpu.make_async_remote_copy(
                src_ref=outbox_n.at[base + k],
                dst_ref=rows_n.at[place.me],
                send_sem=out_sem_n.at[0],
                recv_sem=out_sem_n.at[1],
                device_id=(d, t),
                device_id_type=MESH,
            ).start()

        each(c, send)
        return carry

    lax.fori_loop(0, 4, serve_n, 0)
    rows_n[place.me] = outbox_n[0]

    high = (ids_ref[...] // 64).astype(F32).astype(BF16)
    low = (ids_ref[...] % 64).astype(F32).astype(BF16)
    spread = (iota((DEV, CAP_T * DEV), 1) % CAP_T == iota((DEV, CAP_T * DEV), 0)).astype(F32)
    spread = spread.astype(BF16)
    own = iota((DEV, CAP_T * DEV), 1) // CAP_T == iota((DEV, CAP_T * DEV), 0)
    row = jnp.where(own, 64.0 * nn(high, spread) + nn(low, spread), 0.0)
    slots_ref[:, : CAP_T * DEV] = jnp.sum(row, 0, keepdims=True).astype(jnp.int32)
    column = jnp.transpose(ids_ref[...])
    for r in range(CAP_N):
        at = (CAP_T + r) * DEV
        slots_ref[:, at : at + DEV] = column[CAP_T + r : CAP_T + r + 1, :]
    where = jnp.transpose(jnp.broadcast_to(pos_t, (128, TOK)))
    for c in range(CAP_T):
        match = iota((TOK, 128), 1) + c * 128 == where
        placing[:, c * 128 : (c + 1) * 128] = match.astype(F32).astype(BF16)
    packing[...] = (iota((CAP_T * DEV, TOK), 0) == pos_t).astype(F32).astype(BF16)
    end1 = lengths[0, 0]
    end2 = end1 + lengths[0, 1]
    end3 = end2 + lengths[0, 2]

    def visible(i):
        row = iota((256, 256 * (i + 1)), 0) + 256 * i
        col = iota((256, 256 * (i + 1)), 1)
        start = jnp.where(
            row >= end3, end3, jnp.where(row >= end2, end2, jnp.where(row >= end1, end1, 0))
        )
        return jnp.where((col <= row) & (col >= start), 1.0 / LMAX, 0.0).astype(F32)

    seen0[...] = visible(0)
    seen1[...] = visible(1)
    drain(outbox_t, out_sem_t)

    flat_t[...] = rows_t[...].astype(F32)
    for b in range(4):
        piece = flat_t[:, b * 8 : b * 8 + 8, :].reshape(CAP_T * DEV, 128)
        held[: CAP_T * DEV, b * 128 : (b + 1) * 128] = piece.astype(BF16)
    x32[pl.ds(0, TOK), :] = nn(placing[...], held[: CAP_T * DEV, :])
    for i in range(4):
        span = pl.ds(i * 128, 128)
        x = x32[span, :]
        center = x - jnp.mean(x, -1, keepdims=True)
        scale = lax.rsqrt(jnp.mean(center * center, -1, keepdims=True) + EPS)
        normed = center * scale
        n32[span, :] = normed
        nb[span, :] = normed.astype(BF16)
        scale1[span, :] = scale
    turned[...] = jnp.transpose(n32[...]).astype(BF16)

    loads[6].wait()

    def project(cb, carry):
        cols = pl.ds(pl.multiple_of(cb * 256, 256), 256)
        pre = nn(nb[...], w_in[:, cols])
        sig = sigmoid(pre)
        mixed[:, cols] = (pre * sig).astype(BF16)
        slope[:, cols] = (sig * (1.0 + pre * (1.0 - sig))).astype(BF16)
        return carry

    lax.fori_loop(0, 8, project, 0, unroll=4)

    def lanes(part, h):
        at = part * 512 + h * 128
        return pl.ds(at if isinstance(at, int) else pl.multiple_of(at, 128), 128)

    def attend(h, carry):
        for i in range(2):
            span, past = pl.ds(256 * i, 256), pl.ds(0, 256 * (i + 1))
            score = nt(mixed[span, lanes(2, h)], mixed[past, lanes(3, h)])
            sig = sigmoid(score)
            seen = (seen0, seen1)[i][...]
            weight = (score * sig * seen).astype(BF16)
            weights[h, span, past] = weight
            bend[h, span, past] = (sig * (1.0 + score * (1.0 - sig)) * seen).astype(BF16)
            attended[span, lanes(0, h)] = nn(weight, mixed[past, lanes(1, h)])
        return carry

    lax.fori_loop(0, H, attend, 0, unroll=True)

    loads[7].wait()
    drain(outbox_n, out_sem_n)
    flat_n[...] = rows_n[...].astype(F32).reshape(DEV * MSG_N, 128)
    for c in range(CAP_N):
        for b in range(4):
            piece = flat_n[pl.ds(4 * c + b, DEV, stride=MSG_N), :]
            at = (CAP_T + c) * 128
            held[at : at + 128, b * 128 : (b + 1) * 128] = piece.astype(BF16)
    x = tn((iota((CAP_N * DEV, NEG), 0) == pos_n).astype(F32).astype(BF16), held[CAP_T * DEV :, :])
    x32[pl.ds(512, 128), :] = x
    negatives[...] = x.astype(BF16)
    d_next[pl.ds(0, 8), :] = jnp.zeros((8, D), F32)
    d_negs = jnp.zeros((NEG, D), F32)
    for i in range(2):
        span = pl.ds(256 * i, 256)
        values = attended[span, :]
        center = values - jnp.mean(values, -1, keepdims=True)
        scale = lax.rsqrt(jnp.mean(center * center, -1, keepdims=True) + EPS)
        normed = center * scale
        gate = mixed[span, 0:512].astype(F32)
        gated_b = (normed * gate).astype(BF16)
        gated[span, :] = gated_b
        out_b = (x32[span, :] + nn(gated_b, w_out[...])).astype(BF16)
        out = out_b.astype(F32)
        following = x32[pl.ds(256 * i + 1, 256), :]
        positive = jnp.sum(out * following, -1, keepdims=True) * TAU
        negative = nt(out_b, negatives[...]) * TAU
        top = jnp.maximum(positive, jnp.max(negative, -1, keepdims=True))
        exp_p = jnp.exp(positive - top)
        exp_n = jnp.exp(negative - top)
        total = exp_p + jnp.sum(exp_n, -1, keepdims=True)
        row = iota((256, 1), 0) + (256 * i + 1)
        valid = (row != end1) & (row != end2) & (row != end3) & (row != TOK)
        valid = jnp.where(valid, 1.0, 0.0).astype(F32)
        loss = (jnp.log(total) + top - positive) * valid
        loss_ref[:, span] = jnp.transpose(jnp.broadcast_to(loss, (256, 128)))[:1, :]
        share = valid / total
        d_pos = (exp_p * share - valid) * TAU
        d_neg = (exp_n * (share * TAU)).astype(BF16)
        d_out_b = (d_pos * following + nn(d_neg, negatives[...])).astype(BF16)
        d_out[span, :] = d_out_b
        d_next[pl.ds(256 * i + 8, 256), :] = d_pos * out
        d_negs += tn(d_neg, out_b)
        d_gated = nt(d_out_b, w_out[...])
        d_pre[span, 0:512] = (d_gated * normed * slope[span, 0:512].astype(F32)).astype(BF16)
        d_normed = d_gated * gate
        d_values = scale * (
            d_normed
            - jnp.mean(d_normed, -1, keepdims=True)
            - normed * jnp.mean(d_normed * normed, -1, keepdims=True)
        )
        d_att[span, :] = d_values.astype(BF16)
    d_negatives[...] = d_negs.astype(BF16)
    for c in range(CAP_N):
        at = iota((DEV, NEG), 0) + c * DEV
        sent = nn((at == pos_n).astype(F32).astype(BF16), d_negatives[...])
        for b in range(4):
            flat_n[pl.ds(4 * c + b, DEV, stride=MSG_N), :] = sent[:, b * 128 : (b + 1) * 128]
    box_n[...] = flat_n[...].astype(BF16).reshape(DEV, MSG_N, 128)
    own_n = pltpu.make_async_copy(box_n.at[place.me], arrived_n.at[place.me], own_sem.at[0])
    own_n.start()

    def post_n(first, last):
        for n in range(first, last):
            d, t = groups[n // 32][n % 32]
            pltpu.make_async_remote_copy(
                src_ref=box_n.at[d * 16 + t],
                dst_ref=arrived_n.at[place.me],
                send_sem=back_sem_n.at[0],
                recv_sem=back_sem_n.at[1],
                device_id=(d, t),
                device_id_type=MESH,
            ).start()

    def back(h, carry):
        for i in range(2):
            span, past = pl.ds(256 * i, 256), pl.ds(0, 256 * (i + 1))
            d_weight = nt(d_att[span, lanes(0, h)], mixed[past, lanes(1, h)])
            d_s = (d_weight * bend[h, span, past].astype(F32)).astype(BF16)
            d_score[span, past] = d_s
            d_q = nn(d_s, mixed[past, lanes(3, h)])
            d_pre[span, lanes(2, h)] = (d_q * slope[span, lanes(2, h)].astype(F32)).astype(BF16)
        for i in range(2):
            span, future = pl.ds(256 * i, 256), pl.ds(256 * i, 512 - 256 * i)
            d_v = tn(weights[h, future, span], d_att[future, lanes(0, h)])
            d_pre[span, lanes(1, h)] = (d_v * slope[span, lanes(1, h)].astype(F32)).astype(BF16)
            d_k = tn(d_score[future, span], mixed[future, lanes(2, h)])
            d_pre[span, lanes(3, h)] = (d_k * slope[span, lanes(3, h)].astype(F32)).astype(BF16)
        return carry

    refs = (grad, total_ref, half, acc0, acc1, in1, in2)
    refs += (core_send, core_recv, line_send, line_recv, plane_sem)
    wave_a = Wave(place, 0, ((0, 512), (512, 512)), refs)
    wave_b = Wave(place, 1, ((1024, 512), (1536, 512), (2048, 512)), refs)
    groups = [peers(place, c) for c in range(4)]

    def post(first, last):
        for n in range(first, last):
            d, t = groups[n // 32][n % 32]
            pltpu.make_async_remote_copy(
                src_ref=box_t.at[d * 16 + t],
                dst_ref=arrived_t.at[place.me],
                send_sem=back_sem_t.at[0],
                recv_sem=back_sem_t.at[1],
                device_id=(d, t),
                device_id_type=MESH,
            ).start()

    grad[:, pl.ds(0, 512)] = tn(gated[...], d_out[...]).astype(BF16)
    grad[:, pl.ds(512, 512)] = nn(turned[...], d_pre[:, pl.ds(0, 512)]).astype(BF16)
    wave_a.swap()
    post_n(1, 32)
    back(0, 0)
    post_n(32, 64)
    back(1, 0)
    wave_a.scatter1()
    post_n(64, 96)
    back(2, 0)
    post_n(96, 128)
    back(3, 0)
    for cb in range(1, 4):
        cols = pl.ds(cb * 512, 512)
        grad[:, pl.ds(512 + cb * 512, 512)] = nn(turned[...], d_pre[:, cols]).astype(BF16)
    wave_b.swap()
    wave_a.scatter2()

    for i in range(2):
        span = pl.ds(256 * i, 256)
        d_normed = nt(d_pre[span, :], w_in[...])
        normed = n32[span, :]
        d_x = scale1[span, :] * (
            d_normed
            - jnp.mean(d_normed, -1, keepdims=True)
            - normed * jnp.mean(d_normed * normed, -1, keepdims=True)
        )
        d_x += d_out[span, :].astype(F32) + d_next[pl.ds(256 * i + 7, 256), :]
        grads[span, :] = d_x.astype(BF16)

    wave_b.scatter1()

    for j in range(4):
        half_of = pl.ds(j * 256, 256)
        sent = nn(packing[half_of, :], grads[...]).reshape(32, CAP_T, D)
        for b in range(4):
            flat_t[pl.ds(j * 32, 32), b * 8 : b * 8 + 8, :] = sent[:, :, b * 128 : (b + 1) * 128]
    box_t[...] = flat_t[...].astype(BF16)

    own_t = pltpu.make_async_copy(box_t.at[place.me], arrived_t.at[place.me], own_sem.at[1])
    own_t.start()
    wave_a.gather4()
    wave_b.scatter2()
    post(1, 50)
    wave_b.gather4()
    post(50, 90)
    wave_a.gather5()
    wave_b.gather5()
    post(90, 128)
    wave_a.restore()
    wave_b.restore()
    rest = pl.ds(1024, 3 * D)

    def leave(n, rows, cols):
        copy = pltpu.make_async_copy(
            total_ref.at[rows, cols], total_out.at[rows, cols], total_sem.at[n]
        )
        copy.start()
        return copy

    leaving = [leave(0, pl.ds(wave_b.mine, 256), rest)]
    wave_a.finish()
    leaving.append(leave(1, pl.ds(0, D), pl.ds(0, 1024)))
    wave_b.finish()
    leaving.append(leave(2, pl.ds(wave_b.other, 256), rest))
    own_n.wait()
    own_t.wait()
    drain(box_n, back_sem_n)
    drain(box_t, back_sem_t)
    for copy in leaving:
        copy.wait()


def step(lengths, item_owner, neg_owner, item_slot, neg_slot, table, update, w_in, w_out):
    return pl.pallas_call(
        step_kernel,
        out_shape=(
            jax.ShapeDtypeStruct((1, TOK), F32),
            jax.ShapeDtypeStruct((DEV, MSG_T, 128), BF16),
            jax.ShapeDtypeStruct((DEV, MSG_N, 128), BF16),
            jax.ShapeDtypeStruct((1, CAP * DEV), jnp.int32),
            jax.ShapeDtypeStruct((D, WIDE), BF16),
        ),
        in_specs=[pl.BlockSpec(memory_space=pltpu.SMEM)] + [HBM] * 8,
        out_specs=(VMEM, HBM, HBM, VMEM, HBM),
        scratch_shapes=[
            pltpu.VMEM((D, WIDE), BF16),
            pltpu.VMEM((DEV, 128), jnp.int32),
            pltpu.VMEM((1, TOK), jnp.int32),
            pltpu.VMEM((1, NEG), jnp.int32),
            pltpu.VMEM((1, TOK), jnp.int32),
            pltpu.VMEM((1, NEG), jnp.int32),
            pltpu.VMEM((ROWS // 128, 128), jnp.int32),
            pltpu.VMEM((ROWS, D), BF16),
            pltpu.VMEM((D, 4 * D), BF16),
            pltpu.VMEM((D, D), BF16),
            pltpu.VMEM((DEV, 128), jnp.int32),
            pltpu.VMEM((DEV, MSG_T, 128), BF16),
            pltpu.VMEM((DEV, MSG_N, 128), BF16),
            pltpu.VMEM((DEV, MSG_T, 128), BF16),
            pltpu.VMEM((DEV, MSG_N, 128), BF16),
            pltpu.VMEM((DEV, MSG_T, 128), F32),
            pltpu.VMEM((DEV * MSG_N, 128), F32),
            pltpu.VMEM((CAP * DEV, D), BF16),
            pltpu.VMEM((ALL, D), F32),
            pltpu.VMEM((TOK, D), F32),
            pltpu.VMEM((TOK, D), BF16),
            pltpu.VMEM((D, TOK), BF16),
            pltpu.VMEM((TOK, 1), F32),
            pltpu.VMEM((NEG, D), BF16),
            pltpu.VMEM((TOK, CAP_T * DEV), BF16),
            pltpu.VMEM((CAP_T * DEV, TOK), BF16),
            pltpu.VMEM((256, 256), F32),
            pltpu.VMEM((256, 512), F32),
            pltpu.VMEM((TOK, 4 * D), BF16),
            pltpu.VMEM((TOK, 4 * D), BF16),
            pltpu.VMEM((H, TOK, TOK), BF16),
            pltpu.VMEM((H, TOK, TOK), BF16),
            pltpu.VMEM((TOK, D), F32),
            pltpu.VMEM((TOK, D), BF16),
            pltpu.VMEM((TOK, D), BF16),
            pltpu.VMEM((TOK + 8, D), F32),
            pltpu.VMEM((TOK, D), BF16),
            pltpu.VMEM((TOK, TOK), BF16),
            pltpu.VMEM((TOK, 4 * D), BF16),
            pltpu.VMEM((TOK, D), BF16),
            pltpu.VMEM((NEG, D), BF16),
            pltpu.VMEM((DEV, MSG_T, 128), BF16),
            pltpu.VMEM((DEV, MSG_N, 128), BF16),
            pltpu.VMEM((D, WIDE), BF16),
            pltpu.VMEM((256, WIDE), BF16),
            pltpu.VMEM((256, WIDE), BF16),
            pltpu.VMEM((64, WIDE), BF16),
            pltpu.VMEM((3, 64, WIDE), BF16),
            pltpu.VMEM((2, 3, 15, 16, 128), BF16),
            pltpu.SemaphoreType.DMA((8,)),
            pltpu.SemaphoreType.DMA((2,)),
            pltpu.SemaphoreType.DMA((2,)),
            pltpu.SemaphoreType.DMA((2,)),
            pltpu.SemaphoreType.DMA((2,)),
            pltpu.SemaphoreType.DMA((2,)),
            pltpu.SemaphoreType.DMA((2, 6)),
            pltpu.SemaphoreType.DMA((2, 6)),
            pltpu.SemaphoreType.DMA((2, 3, 2, 3)),
            pltpu.SemaphoreType.DMA((2, 3, 2, 3)),
            pltpu.SemaphoreType.DMA((2, 3, 2, 2)),
            pltpu.SemaphoreType.DMA((2,)),
            pltpu.SemaphoreType.DMA((3,)),
        ],
        compiler_params=pltpu.CompilerParams(
            collective_id=0, has_side_effects=True, vmem_limit_bytes=60 << 20
        ),
        name="step",
    )(lengths, item_owner, neg_owner, item_slot, neg_slot, table, update, w_in, w_out)


def scatter_kernel(
    arrived_t_ref,
    arrived_n_ref,
    slots_ref,
    update_ref,
    total_ref,
    loss_ref,
    out_ref,
    grad_in_ref,
    grad_out_ref,
    loss_out_ref,
    arrived_t,
    arrived_n,
    slots,
    update,
    total,
    loss,
    wide_t,
    wide_n,
    rows,
    chosen0,
    chosen1,
    load_sem,
):
    step = pl.program_id(0)

    def choose(block, chosen):
        for half in range(2):
            local = slots[...] - (block * 512 + half * 256)
            local = jnp.where((local >= 0) & (local < 256), local, -1).astype(F32).astype(BF16)
            row = iota((256, 1), 0).astype(F32).astype(BF16)
            far = jnp.abs(row - local)
            chosen[half * 256 : (half + 1) * 256, :] = jnp.maximum(1.0 - far, 0.0).astype(BF16)

    def fold(first, chosen):
        summed = nn(chosen[...], rows[...])
        for k in range(4):
            at = first + k
            out_ref[at * 128 : (at + 1) * 128, :] = (
                summed[k * 128 : (k + 1) * 128] * fade[:, at : at + 1]
            )

    pairs = (
        (arrived_t_ref, arrived_t),
        (arrived_n_ref, arrived_n),
        (slots_ref, slots),
        (update_ref, update),
        (total_ref, total),
        (loss_ref, loss),
    )
    loads = [pltpu.make_async_copy(src, dst, load_sem.at[n]) for n, (src, dst) in enumerate(pairs)]

    @pl.when(step == 0)
    def _():
        for copy in loads:
            copy.start()
        loads[2].wait()
        choose(0, chosen0)
        for copy in loads[:2] + loads[3:]:
            copy.wait()
        wide_t[...] = arrived_t[...].astype(F32)
        for b in range(4):
            piece = wide_t[:, b * 8 : b * 8 + 8, :].reshape(CAP_T * DEV, 128)
            rows[: CAP_T * DEV, b * 128 : (b + 1) * 128] = piece.astype(BF16)
        wide_n[...] = arrived_n[...].astype(F32).reshape(DEV * MSG_N, 128)
        for c in range(CAP_N):
            for b in range(4):
                piece = wide_n[pl.ds(4 * c + b, DEV, stride=MSG_N), :]
                at = (CAP_T + c) * 128
                rows[at : at + 128, b * 128 : (b + 1) * 128] = piece.astype(BF16)

    loss_out_ref[...] = loss[...]
    part = total[pl.ds(pl.multiple_of(step * 128, 128), 128), :]
    grad_out_ref[...] = part[:, :D].astype(F32)
    grad_in_ref[...] = part[:, D:].astype(F32)
    fade = jnp.exp((NOW - update[pl.ds(pl.multiple_of(step * 8, 8), 8), :]).astype(F32) * LOG_RHO)
    fade = jnp.transpose(jnp.concatenate([fade, jnp.zeros((120, 128), F32)], 0))
    choose(2 * step + 1, chosen1)
    fold(0, chosen0)
    choose(2 * step + 2, chosen0)
    fold(4, chosen1)


def scatter(arrived_t, arrived_n, slots, update, total, losses):
    return pl.pallas_call(
        scatter_kernel,
        grid=(4,),
        out_shape=(
            jax.ShapeDtypeStruct((ROWS, D), F32),
            jax.ShapeDtypeStruct((D, 4 * D), F32),
            jax.ShapeDtypeStruct((D, D), F32),
            jax.ShapeDtypeStruct((1, TOK), F32),
        ),
        in_specs=[HBM] * 6,
        out_specs=(
            pl.BlockSpec((1024, D), lambda i: (i, 0)),
            pl.BlockSpec((128, 4 * D), lambda i: (i, 0)),
            pl.BlockSpec((128, D), lambda i: (i, 0)),
            pl.BlockSpec((1, TOK), lambda i: (0, 0)),
        ),
        scratch_shapes=[
            pltpu.VMEM((DEV, MSG_T, 128), BF16),
            pltpu.VMEM((DEV, MSG_N, 128), BF16),
            pltpu.VMEM((1, CAP * DEV), jnp.int32),
            pltpu.VMEM((ROWS // 128, 128), jnp.int32),
            pltpu.VMEM((D, WIDE), BF16),
            pltpu.VMEM((1, TOK), F32),
            pltpu.VMEM((DEV, MSG_T, 128), F32),
            pltpu.VMEM((DEV * MSG_N, 128), F32),
            pltpu.VMEM((CAP * DEV, D), BF16),
            pltpu.VMEM((512, CAP * DEV), BF16),
            pltpu.VMEM((512, CAP * DEV), BF16),
            pltpu.SemaphoreType.DMA((6,)),
        ],
        compiler_params=pltpu.CompilerParams(vmem_limit_bytes=60 << 20),
        name="scatter",
    )(arrived_t, arrived_n, slots, update, total, losses)


def on_device(
    table, last_update, item_owner, item_slot, neg_owner, neg_slot, seq_lengths, w_in, w_out
):
    update = last_update.reshape(ROWS // 128, 128)
    losses, arrived_t, arrived_n, slots, total = step(
        seq_lengths,
        item_owner.reshape(1, TOK),
        neg_owner.reshape(1, NEG),
        item_slot.reshape(1, TOK),
        neg_slot.reshape(1, NEG),
        table,
        update,
        w_in,
        w_out,
    )
    table_grad, grad_in, grad_out, losses = scatter(
        arrived_t, arrived_n, slots, update, total, losses
    )
    return (losses.reshape(TOK), table_grad, grad_in, grad_out)


def solution(mesh):
    placed = (
        P(("dp", "table"), None),
        P(("dp", "table")),
        P(("dp", "table"), None),
        P(("dp", "table")),
        P(("dp", "table"), None),
        P(("dp", "table")),
        P(("dp", "table"), None),
        P(),
        P(),
    )
    return jax.shard_map(
        on_device,
        mesh=mesh,
        in_specs=placed,
        out_specs=(P(("dp", "table")), P(("dp", "table"), None), P(), P()),
        check_vma=False,
    )
```
